32 devices in a mesh: groups: 1, blk: 16 (over z, y, x), heads: 2 (over core).
Axes of the slice: x: 2, y: 2, z: 4, core: 2. Of those that a mesh axis runs over, the one named last changes fastest.
Arguments:
- queries: bfloat16 [4096, 2048], P(('groups', 'blk', 'heads')), may hold values from -186 to 186
- keys: bfloat16 [4096, 1024], P(('groups', 'blk', 'heads')), may hold values from -6 to 6
- values: bfloat16 [4096, 1024], P(('groups', 'blk', 'heads')), may hold values from -6 to 6
- upstream: bfloat16 [4096, 2048], P(('groups', 'blk', 'heads')), may hold values from -6 to 6
- doc_ids: int32 [32], P('groups'), may hold values from 0 to 3, never falling along the last dimension, each value on 1 to 16 neighbouring positions
- band: int32 [32], P('groups'), may hold values from 0 to 8, as said below
Outputs:
- query_grad: bfloat16 [4096, 2048], P(('groups', 'blk', 'heads'))
- key_gradient: bfloat16 [4096, 1024], P(('groups', 'blk', 'heads'))
- value_gradient: bfloat16 [4096, 1024], P(('groups', 'blk', 'heads'))
The draws below stay inside these ranges and needn't reach their ends.
Inputs may be any that keep to these rules, and one draw needn't show every extreme that they name: `band`: earlier blocks a query block may see; some block sees 8 and some sees 0.
All inputs are finite; a program needn't handle non-finite values.
Results may differ from the reference program's by a relative error of at most 0.0083.
Values may be sent and summed in bfloat16 or wider, within the bound.
No kernel may reach another device: no remote copies, remote signals or barrier semaphores. Data moves between devices by JAX's collectives and lax.ppermute only.
A program may use at most 64 MiB of HBM per device.

```python
import math
import jax
import jax.numpy as jnp
import numpy as np
from jax import lax

QUERY_HEADS = 16
KEY_VALUE_HEADS = 8
HEAD_SIZE = 128
SCALAR = 168
WINDOW_TOKENS = 1024
MASK_BLOCK = 128
SEQUENCE_TOKENS = 4096
NB = 32
WB = 8
DOCS = 4
DOC_MOST = 16


def common_draw(key):
    base_offset = jnp.clip(jax.random.normal(jax.random.fold_in(key, 11), (SEQUENCE_TOKENS, KEY_VALUE_HEADS, HEAD_SIZE), jnp.float32), -6.0, 6.0)
    levels = jax.random.randint(jax.random.fold_in(key, 13), (SEQUENCE_TOKENS,), 0, 3)
    position = jnp.arange(SEQUENCE_TOKENS)
    chosen = position < 0
    strength = jnp.where(chosen, 10.0 + 10.0 * levels.astype(jnp.float32), 0.0)
    return (base_offset, strength)


def draw_keys(key, part):
    base_offset, strength = common_draw(key)
    after = jnp.roll(strength, -1)
    following = jnp.roll(base_offset, -1, axis=0)
    shrink = 1.0 - 0.2 / jnp.maximum(after, 1.0)
    mixed_rows = jnp.where((after > 0.0)[:, None, None], shrink[:, None, None] * following, base_offset)
    return mixed_rows.reshape(SEQUENCE_TOKENS, KEY_VALUE_HEADS * HEAD_SIZE).astype(jnp.bfloat16)


def draw_queries(key, part):
    base_offset, strength = common_draw(key)
    noise = jnp.clip(jax.random.normal(jax.random.fold_in(key, 14), (SEQUENCE_TOKENS, QUERY_HEADS, HEAD_SIZE), jnp.float32), -6.0, 6.0)
    block_aligned = jnp.repeat(base_offset, QUERY_HEADS // KEY_VALUE_HEADS, axis=1)
    mixed_rows = noise + strength[:, None, None] * block_aligned
    return mixed_rows.reshape(SEQUENCE_TOKENS, QUERY_HEADS * HEAD_SIZE).astype(jnp.bfloat16)


def draw_band(key, part):
    widths = jax.random.randint(jax.random.fold_in(key, 21), (NB,), 0, WB + 1)
    widest = jax.random.randint(jax.random.fold_in(key, 22), (), 0, NB)
    narrow = jax.random.randint(jax.random.fold_in(key, 23), (), 0, NB)
    position = jnp.arange(NB)
    widths = jnp.where(position == narrow, 0, widths)
    widths = jnp.where(position == widest, WB, widths)
    return widths.astype(jnp.int32)


def block_levels(rng, shape, cuts, least, largest):
    loudness = 1.0
    for dim, parts in cuts:
        steps = jax.random.uniform(jax.random.fold_in(jax.random.fold_in(rng, 6), dim), (parts,), jnp.float32, least / len(cuts), largest / len(cuts))
        loudness = loudness * jnp.repeat(jnp.exp(steps), shape[dim] // parts).reshape((-1,) + (1,) * (len(shape) - 1 - dim))
    return loudness


def split_up(amount, total, bound, slope):
    portions = [(1 << 20) // math.isqrt(standing ** slope) + 1 for standing in range(2, amount + 1)]
    spare, given = total - bound - (amount - 1), [1] * (amount - 1)
    while spare > 0:
        movable = [i for i in range(amount - 1) if given[i] < bound]
        pool, left = sum([portions[i] for i in movable]), spare
        for i in movable:
            more = min(bound - given[i], max(1, left * portions[i] // pool), spare)
            given[i] = given[i] + more
            spare = spare - more
    return np.array([bound] + given)


def uneven(key, number_of, total, bound, slope):
    if number_of == 2:
        one = jax.random.randint(key, (), max(1, total - bound), min(bound, total - 1) + 1)
        return jnp.stack([one, total - one])
    sizes = jnp.asarray(split_up(number_of, total, bound, slope), jnp.int32)
    pairs = (number_of - 1) // 2
    donor, sink = sizes[1:1 + 2 * pairs:2], sizes[2:2 + 2 * pairs:2]
    slack = jnp.minimum(donor - 1, bound - sink)
    moved = jax.random.randint(jax.random.fold_in(key, 1), (pairs,), 0, 1 << 20) % (slack + 1)
    sizes = sizes.at[1:1 + 2 * pairs:2].set(donor - moved).at[2:2 + 2 * pairs:2].set(sink + moved)
    return sizes[jax.random.permutation(jax.random.fold_in(key, 2), number_of)]


def scatter_about(own_key, dims, width, most, cuts=(), kind=jnp.bfloat16):
    values = jax.random.normal(own_key, dims, jnp.float32) * width
    if len(cuts) > 0:
        values = block_levels(own_key, dims, cuts, -0.22, 0.18) * values
    return jnp.clip(values, min=-most, max=most).astype(kind)


def setup_inputs(seed: int = 0, part: int = 0) -> dict:
    streams_of = jax.random.split(jax.random.key(seed), 7)
    own_keys = jax.random.split(jax.random.fold_in(streams_of[6], part), 7)
    queries = draw_queries(jax.random.fold_in(jax.random.fold_in(streams_of[6], part), 71), part)
    keys = draw_keys(jax.random.fold_in(jax.random.fold_in(streams_of[6], part), 71), part)
    values = scatter_about(own_keys[2], (SEQUENCE_TOKENS, KEY_VALUE_HEADS * HEAD_SIZE), 1.0, 6.0, ((0, 32),))
    upstream = scatter_about(own_keys[3], (SEQUENCE_TOKENS, QUERY_HEADS * HEAD_SIZE), 1.0, 6.0, ((0, 32),))
    doc_ids = jnp.searchsorted(jnp.cumsum(uneven(own_keys[4], DOCS, NB, DOC_MOST, 1)), jnp.arange(NB), side="right").astype(jnp.int32)
    band = draw_band(jax.random.fold_in(jax.random.fold_in(streams_of[6], part), 71), part)
    return {"queries": queries, "keys": keys, "values": values, "upstream": upstream, "doc_ids": doc_ids, "band": band}


def reference(queries, keys, values, upstream, doc_ids, band):
    blocks = SEQUENCE_TOKENS // MASK_BLOCK
    window_blocks = WINDOW_TOKENS // MASK_BLOCK
    group_ratio = QUERY_HEADS // KEY_VALUE_HEADS
    scale = SCALAR ** -0.5
    span_extent = WINDOW_TOKENS + MASK_BLOCK
    leading_rows = jnp.zeros((WINDOW_TOKENS, KEY_VALUE_HEADS * HEAD_SIZE), jnp.bfloat16)
    key_padding = jnp.concatenate([leading_rows, keys], 0)
    value_padding = jnp.concatenate([leading_rows, values], 0)
    doc_pad = jnp.concatenate([jnp.full((window_blocks,), -1, jnp.int32), doc_ids.astype(jnp.int32)])
    offsets = jnp.arange(window_blocks + 1, dtype=jnp.int32)
    causal = jnp.arange(span_extent, dtype=jnp.int32)[None, :] <= jnp.arange(MASK_BLOCK, dtype=jnp.int32)[:, None] + WINDOW_TOKENS

    def one_block(carry, index):
        key_accumulator, value_accumulator = carry
        start_index = (index * MASK_BLOCK).astype(jnp.int32)
        query_row_slice = lax.dynamic_slice_in_dim(queries, start_index, MASK_BLOCK, 0).reshape(MASK_BLOCK, KEY_VALUE_HEADS, group_ratio, HEAD_SIZE).astype(jnp.float32)
        gradient_rows = lax.dynamic_slice_in_dim(upstream, start_index, MASK_BLOCK, 0).reshape(MASK_BLOCK, KEY_VALUE_HEADS, group_ratio, HEAD_SIZE).astype(jnp.float32)
        key_row_slice = lax.dynamic_slice_in_dim(key_padding, start_index, span_extent, 0).reshape(span_extent, KEY_VALUE_HEADS, HEAD_SIZE).astype(jnp.float32)
        value_row_slice = lax.dynamic_slice_in_dim(value_padding, start_index, span_extent, 0).reshape(span_extent, KEY_VALUE_HEADS, HEAD_SIZE).astype(jnp.float32)
        key_docs = lax.dynamic_slice_in_dim(doc_pad, index.astype(jnp.int32), window_blocks + 1, 0)
        own_doc = lax.dynamic_slice_in_dim(doc_ids.astype(jnp.int32), index.astype(jnp.int32), 1, 0)
        own_band = lax.dynamic_slice_in_dim(band.astype(jnp.int32), index.astype(jnp.int32), 1, 0)
        block_ok = (key_docs == own_doc) & (window_blocks - offsets <= own_band)
        allowed = jnp.repeat(block_ok, MASK_BLOCK, total_repeat_length=span_extent)[None, :] & causal
        scores = jnp.einsum('qhrd,khd->hrqk', query_row_slice, key_row_slice) * scale
        scores = jnp.where(allowed, scores, -jnp.inf)
        top = jnp.max(scores, axis=-1, keepdims=True)
        expo = jnp.exp(scores - top)
        probs = expo / jnp.sum(expo, axis=-1, keepdims=True)
        probs_f = lax.optimization_barrier(probs.astype(jnp.bfloat16)).astype(jnp.float32)
        output = jnp.einsum('hrqk,khd->hrqd', probs_f, value_row_slice)
        delta = jnp.sum(jnp.transpose(gradient_rows, (1, 2, 0, 3)) * output, axis=-1)
        dprob = jnp.einsum('qhrd,khd->hrqk', gradient_rows, value_row_slice)
        dscore = lax.optimization_barrier((probs * (dprob - delta[..., None])).astype(jnp.bfloat16)).astype(jnp.float32)
        query_grad = jnp.einsum('hrqk,khd->qhrd', dscore, key_row_slice) * scale
        key_gradient = jnp.einsum('hrqk,qhrd->khd', dscore, query_row_slice) * scale
        value_gradient = jnp.einsum('hrqk,qhrd->khd', probs_f, gradient_rows)
        key_accumulator = lax.dynamic_update_slice_in_dim(key_accumulator, lax.dynamic_slice_in_dim(key_accumulator, start_index, span_extent, 0) + key_gradient, start_index, 0)
        value_accumulator = lax.dynamic_update_slice_in_dim(value_accumulator, lax.dynamic_slice_in_dim(value_accumulator, start_index, span_extent, 0) + value_gradient, start_index, 0)
        return (key_accumulator, value_accumulator), query_grad.reshape(MASK_BLOCK, QUERY_HEADS * HEAD_SIZE).astype(jnp.bfloat16)

    empty_rows = jnp.zeros((WINDOW_TOKENS + SEQUENCE_TOKENS, KEY_VALUE_HEADS, HEAD_SIZE), jnp.float32)
    (key_accumulator, value_accumulator), query_parts = lax.scan(one_block, (empty_rows, empty_rows), jnp.arange(blocks, dtype=jnp.int32))
    query_grad = query_parts.reshape(SEQUENCE_TOKENS, QUERY_HEADS * HEAD_SIZE)
    key_gradient = key_accumulator[WINDOW_TOKENS:].reshape(SEQUENCE_TOKENS, KEY_VALUE_HEADS * HEAD_SIZE).astype(jnp.bfloat16)
    value_gradient = value_accumulator[WINDOW_TOKENS:].reshape(SEQUENCE_TOKENS, KEY_VALUE_HEADS * HEAD_SIZE).astype(jnp.bfloat16)
    return (query_grad, key_gradient, value_gradient)
```

```python
import math

import jax
import jax.numpy as jnp
from jax import lax
from jax.experimental import pallas as pl
from jax.experimental.pallas import tpu as pltpu
from jax.sharding import PartitionSpec as P

HEAD = 128
SCALAR = 168
WINDOW = 1024
BLOCK = 128
WB = WINDOW // BLOCK
SCALE = SCALAR ** (-0.5)
LOG2E = math.log2(math.e)

NT = (((1,), (1,)), ((), ()))
NN = (((1,), (0,)), ((), ()))
TN = (((0,), (0,)), ((), ()))


def dot(a, b, dims):
    return lax.dot_general(a, b, dims, preferred_element_type=jnp.float32)


def pack_kernel(a_ref, b_ref, out_ref):
    heads = out_ref.shape[0]
    width = out_ref.shape[2] // 2
    for h in range(heads):
        out_ref[h, :, :width] = a_ref[:, h * width : (h + 1) * width]
        out_ref[h, :, width:] = b_ref[:, h * width : (h + 1) * width]


def pack(a, b, heads):
    tokens, cols = a.shape
    return pl.pallas_call(
        pack_kernel,
        out_shape=jax.ShapeDtypeStruct((heads, tokens, 2 * cols // heads), a.dtype),
    )(a, b)


def attend_kernel(
    chunk_ref, doc_ref, band_ref, qd_ref, own_ref, halo_ref,
    dq_ref, dkv_own_ref, dkv_halo_ref,
    keys, values, dk, dv,
):
    chunk = own_ref.shape[0] * BLOCK
    blocks = chunk // BLOCK
    q_heads = qd_ref.shape[2] // (2 * HEAD)
    for j in range(blocks):
        rows = slice(j * BLOCK, (j + 1) * BLOCK)
        late = slice(WINDOW + j * BLOCK, WINDOW + (j + 1) * BLOCK)
        keys[rows, :] = halo_ref[j, :, :HEAD]
        values[rows, :] = halo_ref[j, :, HEAD:]
        keys[late, :] = own_ref[j, :, :HEAD]
        values[late, :] = own_ref[j, :, HEAD:]
    dk[...] = jnp.zeros_like(dk)
    dv[...] = jnp.zeros_like(dv)
    first = chunk_ref[0] * blocks

    def one_block(i, carry):
        index = first + i
        own_band = band_ref[index]
        own_doc = doc_ref[index]
        reach = jnp.int32(0)
        for back in range(1, WB + 1):
            seen = (
                (back <= own_band)
                & (index >= back)
                & (doc_ref[jnp.maximum(index - back, 0)] == own_doc)
            )
            reach = reach + seen.astype(jnp.int32)

        def work(span_blocks):
            span = span_blocks * BLOCK
            start = pl.multiple_of((i + WB + 1 - span_blocks) * BLOCK, BLOCK)
            window = pl.ds(start, span)
            query = jnp.concatenate(
                [qd_ref[i, :, h * HEAD : (h + 1) * HEAD] for h in range(q_heads)], axis=0
            )
            grad = jnp.concatenate(
                [
                    qd_ref[i, :, (q_heads + h) * HEAD : (q_heads + h + 1) * HEAD]
                    for h in range(q_heads)
                ],
                axis=0,
            )
            rows = q_heads * BLOCK
            key = keys[window, :]
            value = values[window, :]
            scores = dot(key, query, NT)
            key_pos = lax.broadcasted_iota(jnp.int32, (span, rows), 0)
            query_pos = lax.broadcasted_iota(jnp.int32, (span, rows), 1) % BLOCK
            low = (span_blocks - 1 - reach) * BLOCK
            allowed = (key_pos >= low) & (key_pos <= query_pos + (span - BLOCK))
            scores = jnp.where(allowed, scores, -jnp.inf)
            top = jnp.max(scores, axis=0, keepdims=True)
            expo = jnp.exp2((scores - top) * (SCALE * LOG2E))
            probs = expo * (1.0 / jnp.sum(expo, axis=0, keepdims=True))
            probs_b = probs.astype(jnp.bfloat16)
            dprob = dot(value, grad, NT)
            delta = jnp.sum(probs_b.astype(jnp.float32) * dprob, axis=0, keepdims=True)
            dscore = (probs * (dprob - delta)).astype(jnp.bfloat16)
            dv[window, :] += dot(probs_b, grad, NN)
            dk[window, :] += dot(dscore, query, NN)
            query_grad = (dot(dscore, key, TN) * SCALE).astype(jnp.bfloat16)
            for h in range(q_heads):
                dq_ref[i, :, h * HEAD : (h + 1) * HEAD] = query_grad[
                    h * BLOCK : (h + 1) * BLOCK, :
                ]

        sizes = (3, 6, WB + 1)
        least = 0
        for size in sizes:
            pl.when((reach + 1 > least) & (reach + 1 <= size))(lambda size=size: work(size))
            least = size
        return carry

    lax.fori_loop(0, blocks, one_block, 0)
    for j in range(blocks):
        rows = slice(j * BLOCK, (j + 1) * BLOCK)
        late = slice(WINDOW + j * BLOCK, WINDOW + (j + 1) * BLOCK)
        dkv_halo_ref[j, :, :HEAD] = (dk[rows, :] * SCALE).astype(dkv_halo_ref.dtype)
        dkv_halo_ref[j, :, HEAD:] = dv[rows, :].astype(dkv_halo_ref.dtype)
        dkv_own_ref[j, :, :HEAD] = dk[late, :] * SCALE
        dkv_own_ref[j, :, HEAD:] = dv[late, :]


def attend(chunk_index, doc_ids, band, queries_grads, own, halo):
    blocks = own.shape[0]
    total = WINDOW + blocks * BLOCK
    smem = pl.BlockSpec(memory_space=pltpu.SMEM)
    vmem = pl.BlockSpec(memory_space=pltpu.VMEM)
    return pl.pallas_call(
        attend_kernel,
        in_specs=[smem] * 3 + [vmem] * 3,
        out_specs=[vmem] * 3,
        out_shape=[
            jax.ShapeDtypeStruct(
                (blocks, BLOCK, queries_grads.shape[2] // 2), jnp.bfloat16
            ),
            jax.ShapeDtypeStruct(own.shape, jnp.float32),
            jax.ShapeDtypeStruct(own.shape, jnp.bfloat16),
        ],
        scratch_shapes=[
            pltpu.VMEM((total, HEAD), jnp.bfloat16),
            pltpu.VMEM((total, HEAD), jnp.bfloat16),
            pltpu.VMEM((total, HEAD), jnp.float32),
            pltpu.VMEM((total, HEAD), jnp.float32),
        ],
        compiler_params=pltpu.CompilerParams(vmem_limit_bytes=40 * 1024 * 1024),
    )(chunk_index, doc_ids, band, queries_grads, own, halo)


def per_device(queries, keys, values, upstream, doc_ids, band):
    tokens = queries.shape[0]
    parts = WINDOW // tokens
    cores = lax.axis_size("heads")
    spans = lax.axis_size("blk")
    step = parts // cores
    axes = ("blk", "heads")
    groups = [
        [first * parts + member for member in range(parts)] for first in range(spans // step)
    ]

    def exchange(value):
        return lax.all_to_all(
            value, axes, split_axis=0, concat_axis=0, axis_index_groups=groups, tiled=True
        )

    kv = exchange(pack(keys, values, parts))
    halo = lax.ppermute(kv, "blk", [(s, s + step) for s in range(spans - step)])
    qd = exchange(pack(queries, upstream, parts))
    chunk_index = (lax.axis_index("blk") // step).astype(jnp.int32).reshape(1)
    dq, dkv_own, dkv_halo = attend(chunk_index, doc_ids, band, qd, kv, halo)
    spill = lax.ppermute(dkv_halo, "blk", [(s + step, s) for s in range(spans - step)])
    query_out = exchange(dq)
    dkv = exchange((dkv_own + spill.astype(jnp.float32)).astype(jnp.bfloat16))

    def merge(value):
        return value.transpose(1, 0, 2).reshape(tokens, -1)

    return merge(query_out), merge(dkv[:, :, :HEAD]), merge(dkv[:, :, HEAD:])


def solution(mesh):
    sharded = P(("groups", "blk", "heads"), None)
    return jax.shard_map(
        per_device,
        mesh=mesh,
        in_specs=(sharded,) * 4 + (P("groups"),) * 2,
        out_specs=(sharded,) * 3,
        check_vma=False,
    )
```

```python
import functools
import math

import jax
import jax.numpy as jnp
from jax import lax
from jax.experimental import pallas as pl
from jax.experimental.pallas import tpu as pltpu
from jax.sharding import PartitionSpec as P

HEAD = 128
SCALAR = 168
WINDOW = 1024
BLOCK = 128
WB = WINDOW // BLOCK
SCALE = SCALAR ** (-0.5)
LOG2E = math.log2(math.e)

NT = (((1,), (1,)), ((), ()))
NN = (((1,), (0,)), ((), ()))
TN = (((0,), (0,)), ((), ()))


def dot(a, b, dims):
    return lax.dot_general(a, b, dims, preferred_element_type=jnp.float32)


def pack_kernel(a_ref, b_ref, out_ref):
    heads = out_ref.shape[0]
    width = out_ref.shape[2] // 2
    for h in range(heads):
        out_ref[h, :, :width] = a_ref[:, h * width : (h + 1) * width]
        out_ref[h, :, width:] = b_ref[:, h * width : (h + 1) * width]


def pack(a, b, heads):
    tokens, cols = a.shape
    vmem = pl.BlockSpec(memory_space=pltpu.VMEM)
    return pl.pallas_call(
        pack_kernel,
        in_specs=[vmem] * 2,
        out_specs=vmem,
        out_shape=jax.ShapeDtypeStruct((heads, tokens, 2 * cols // heads), a.dtype),
    )(a, b)


def unpack_kernel(in_ref, *out_refs):
    heads = in_ref.shape[0]
    width = in_ref.shape[2] // len(out_refs)
    for n, out_ref in enumerate(out_refs):
        for h in range(heads):
            out_ref[:, h * width : (h + 1) * width] = in_ref[h, :, n * width : (n + 1) * width]


def unpack(value, outputs):
    heads, tokens, width = value.shape
    shape = jax.ShapeDtypeStruct((tokens, heads * width // outputs), value.dtype)
    vmem = pl.BlockSpec(memory_space=pltpu.VMEM)
    return pl.pallas_call(
        unpack_kernel, in_specs=[vmem], out_specs=[vmem] * outputs, out_shape=[shape] * outputs
    )(value)


def attend_kernel(
    chunk_ref, doc_ref, band_ref, qd_ref, own_ref, halo_ref,
    dq_ref, dkv_own_ref, dkv_halo_ref,
    keys, values, dk, dv,
):
    chunk = own_ref.shape[0] * BLOCK
    blocks = chunk // BLOCK
    q_heads = qd_ref.shape[2] // (2 * HEAD)
    for j in range(blocks):
        rows = slice(j * BLOCK, (j + 1) * BLOCK)
        late = slice(WINDOW + j * BLOCK, WINDOW + (j + 1) * BLOCK)
        keys[rows, :] = halo_ref[j, :, :HEAD]
        values[rows, :] = halo_ref[j, :, HEAD:]
        keys[late, :] = own_ref[j, :, :HEAD]
        values[late, :] = own_ref[j, :, HEAD:]
    dk[...] = jnp.zeros_like(dk)
    dv[...] = jnp.zeros_like(dv)
    first = chunk_ref[0] * blocks

    def one_block(i, carry):
        index = first + i
        own_band = band_ref[index]
        own_doc = doc_ref[index]
        reach = jnp.int32(0)
        for back in range(1, WB + 1):
            seen = (
                (back <= own_band)
                & (index >= back)
                & (doc_ref[jnp.maximum(index - back, 0)] == own_doc)
            )
            reach = reach + seen.astype(jnp.int32)

        def work(span_blocks):
            span = span_blocks * BLOCK
            start = pl.multiple_of((i + WB + 1 - span_blocks) * BLOCK, BLOCK)
            window = pl.ds(start, span)
            query = jnp.concatenate(
                [qd_ref[i, :, h * HEAD : (h + 1) * HEAD] for h in range(q_heads)], axis=0
            )
            grad = jnp.concatenate(
                [
                    qd_ref[i, :, (q_heads + h) * HEAD : (q_heads + h + 1) * HEAD]
                    for h in range(q_heads)
                ],
                axis=0,
            )
            rows = q_heads * BLOCK
            key = keys[window, :]
            value = values[window, :]

            def split(x):
                return [x[b * BLOCK : (b + 1) * BLOCK] for b in range(span_blocks)]

            def fold(x):
                return x.reshape(BLOCK // 8, 8, rows)

            scores = split(dot(key, query, NT))
            key_pos = lax.broadcasted_iota(jnp.int32, (BLOCK, rows), 0)
            query_pos = lax.broadcasted_iota(jnp.int32, (BLOCK, rows), 1) % BLOCK
            scores[-1] = jnp.where(key_pos <= query_pos, scores[-1], -jnp.inf)
            top = functools.reduce(jnp.maximum, [jnp.max(fold(x), axis=0) for x in scores])
            top = jnp.max(top, axis=0, keepdims=True)
            dprob = split(dot(value, grad, NT))
            expo = [jnp.exp2((x - top) * (SCALE * LOG2E)) for x in scores]
            total = functools.reduce(jnp.add, [jnp.sum(fold(x), axis=0) for x in expo])
            inverse = 1.0 / jnp.sum(total, axis=0, keepdims=True)
            probs = [x * inverse for x in expo]
            probs_b = [x.astype(jnp.bfloat16) for x in probs]
            delta = functools.reduce(
                jnp.add,
                [
                    jnp.sum(fold(x.astype(jnp.float32) * y), axis=0)
                    for x, y in zip(probs_b, dprob)
                ],
            )
            delta = jnp.sum(delta, axis=0, keepdims=True)
            dscore = jnp.concatenate(
                [(x * (y - delta)).astype(jnp.bfloat16) for x, y in zip(probs, dprob)], axis=0
            )
            probs_b = jnp.concatenate(probs_b, axis=0)
            dv[window, :] += dot(probs_b, grad, NN)
            dk[window, :] += dot(dscore, query, NN)
            query_grad = (dot(dscore, key, TN) * SCALE).astype(jnp.bfloat16)
            for h in range(q_heads):
                dq_ref[i, :, h * HEAD : (h + 1) * HEAD] = query_grad[
                    h * BLOCK : (h + 1) * BLOCK, :
                ]

        for size in range(1, WB + 2):
            pl.when(reach + 1 == size)(functools.partial(work, size))
        return carry

    lax.fori_loop(0, blocks, one_block, 0)
    for j in range(blocks):
        rows = slice(j * BLOCK, (j + 1) * BLOCK)
        late = slice(WINDOW + j * BLOCK, WINDOW + (j + 1) * BLOCK)
        dkv_halo_ref[j, :, :HEAD] = (dk[rows, :] * SCALE).astype(dkv_halo_ref.dtype)
        dkv_halo_ref[j, :, HEAD:] = dv[rows, :].astype(dkv_halo_ref.dtype)
        dkv_own_ref[j, :, :HEAD] = dk[late, :] * SCALE
        dkv_own_ref[j, :, HEAD:] = dv[late, :]


def attend(chunk_index, doc_ids, band, queries_grads, own, halo):
    blocks = own.shape[0]
    total = WINDOW + blocks * BLOCK
    smem = pl.BlockSpec(memory_space=pltpu.SMEM)
    vmem = pl.BlockSpec(memory_space=pltpu.VMEM)
    return pl.pallas_call(
        attend_kernel,
        in_specs=[smem] * 3 + [vmem] * 3,
        out_specs=[vmem] * 3,
        out_shape=[
            jax.ShapeDtypeStruct(
                (blocks, BLOCK, queries_grads.shape[2] // 2), jnp.bfloat16
            ),
            jax.ShapeDtypeStruct(own.shape, jnp.float32),
            jax.ShapeDtypeStruct(own.shape, jnp.bfloat16),
        ],
        scratch_shapes=[
            pltpu.VMEM((total, HEAD), jnp.bfloat16),
            pltpu.VMEM((total, HEAD), jnp.bfloat16),
            pltpu.VMEM((total, HEAD), jnp.float32),
            pltpu.VMEM((total, HEAD), jnp.float32),
        ],
        compiler_params=pltpu.CompilerParams(vmem_limit_bytes=40 * 1024 * 1024),
    )(chunk_index, doc_ids, band, queries_grads, own, halo)


def per_device(queries, keys, values, upstream, doc_ids, band):
    tokens = queries.shape[0]
    parts = WINDOW // tokens
    cores = lax.axis_size("heads")
    spans = lax.axis_size("blk")
    step = parts // cores
    axes = ("blk", "heads")
    groups = [
        [first * parts + member for member in range(parts)] for first in range(spans // step)
    ]

    def exchange(value):
        return lax.all_to_all(
            value, axes, split_axis=0, concat_axis=0, axis_index_groups=groups, tiled=True
        )

    kv = exchange(pack(keys, values, parts))
    halo = lax.ppermute(kv, "blk", [(s, s + step) for s in range(spans - step)])
    qd = exchange(pack(queries, upstream, parts))
    chunk_index = (lax.axis_index("blk") // step).astype(jnp.int32).reshape(1)
    dq, dkv_own, dkv_halo = attend(chunk_index, doc_ids, band, qd, kv, halo)
    spill = lax.ppermute(dkv_halo, "blk", [(s + step, s) for s in range(spans - step)])
    query_out = exchange(dq)
    dkv = exchange((dkv_own + spill.astype(jnp.float32)).astype(jnp.bfloat16))

    return (*unpack(query_out, 1), *unpack(dkv, 2))


def solution(mesh):
    sharded = P(("groups", "blk", "heads"), None)
    return jax.shard_map(
        per_device,
        mesh=mesh,
        in_specs=(sharded,) * 4 + (P("groups"),) * 2,
        out_specs=(sharded,) * 3,
        check_vma=False,
    )
```

```python
import functools
import math

import jax
import jax.numpy as jnp
from jax import lax
from jax.experimental import pallas as pl
from jax.experimental.pallas import tpu as pltpu
from jax.sharding import PartitionSpec as P

HEAD = 128
SCALAR = 168
WINDOW = 1024
BLOCK = 128
WB = WINDOW // BLOCK
SCALE = SCALAR ** (-0.5)
LOG2E = math.log2(math.e)
SMALL = 8 * 1024 * 1024
TOGETHER = 2

NT = (((1,), (1,)), ((), ()))
NN = (((1,), (0,)), ((), ()))
TN = (((0,), (0,)), ((), ()))


def dot(a, b, dims):
    return lax.dot_general(a, b, dims, preferred_element_type=jnp.float32)


def run_copies(pairs, sems):
    copies = [pltpu.make_async_copy(x, y, sems.at[n]) for n, (x, y) in enumerate(pairs)]
    for copy in copies:
        copy.start()
    for copy in copies:
        copy.wait()


def pack_kernel(a_ref, b_ref, out_ref, sems):
    width = out_ref.shape[2] // 2
    run_copies(
        [
            (ref.at[:, pl.ds(h * width, width)], out_ref.at[h, :, pl.ds(n * width, width)])
            for h in range(out_ref.shape[0])
            for n, ref in enumerate((a_ref, b_ref))
        ],
        sems,
    )


def pack(a, b, heads):
    tokens, cols = a.shape
    hbm = pl.BlockSpec(memory_space=pl.ANY)
    return pl.pallas_call(
        pack_kernel,
        in_specs=[hbm] * 2,
        out_specs=hbm,
        out_shape=jax.ShapeDtypeStruct((heads, tokens, 2 * cols // heads), a.dtype),
        scratch_shapes=[pltpu.SemaphoreType.DMA((2 * heads,))],
    )(a, b)


def unpack_kernel(in_ref, *refs):
    out_refs, sems = refs[:-1], refs[-1]
    width = in_ref.shape[2] // len(out_refs)
    run_copies(
        [
            (in_ref.at[h, :, pl.ds(n * width, width)], ref.at[:, pl.ds(h * width, width)])
            for h in range(in_ref.shape[0])
            for n, ref in enumerate(out_refs)
        ],
        sems,
    )


def unpack(value, outputs):
    heads, tokens, width = value.shape
    shape = jax.ShapeDtypeStruct((tokens, heads * width // outputs), value.dtype)
    return pl.pallas_call(
        unpack_kernel,
        in_specs=[pl.BlockSpec(memory_space=pltpu.VMEM)],
        out_specs=[pl.BlockSpec(memory_space=pl.ANY)] * outputs,
        out_shape=[shape] * outputs,
        scratch_shapes=[pltpu.SemaphoreType.DMA((outputs * heads,))],
        compiler_params=pltpu.CompilerParams(vmem_limit_bytes=SMALL),
    )(value)


def attend_kernel(
    chunk_ref, doc_ref, band_ref, qd_ref, own_ref, halo_ref,
    dq_ref, dkv_own_ref, dkv_halo_ref,
    keys, values, dk, dv,
):
    chunk = own_ref.shape[0] * BLOCK
    blocks = chunk // BLOCK
    q_heads = qd_ref.shape[2] // (2 * HEAD)
    for j in range(blocks):
        rows = slice(j * BLOCK, (j + 1) * BLOCK)
        late = slice(WINDOW + j * BLOCK, WINDOW + (j + 1) * BLOCK)
        keys[rows, :] = halo_ref[j, :, :HEAD]
        values[rows, :] = halo_ref[j, :, HEAD:]
        keys[late, :] = own_ref[j, :, :HEAD]
        values[late, :] = own_ref[j, :, HEAD:]
    dk[...] = jnp.zeros_like(dk)
    dv[...] = jnp.zeros_like(dv)
    first = chunk_ref[0] * blocks

    def reach_of(i):
        index = first + i
        own_band = band_ref[index]
        own_doc = doc_ref[index]
        reach = jnp.int32(0)
        for back in range(1, WB + 1):
            seen = (
                (back <= own_band)
                & (index >= back)
                & (doc_ref[jnp.maximum(index - back, 0)] == own_doc)
            )
            reach = reach + seen.astype(jnp.int32)
        return reach

    rows = q_heads * BLOCK

    def stacked(i, offset):
        return jnp.concatenate(
            [qd_ref[i, :, (offset + h) * HEAD : (offset + h + 1) * HEAD] for h in range(q_heads)],
            axis=0,
        )

    def fold(x, reduce):
        return reduce(x.reshape(BLOCK // 8, 8, rows), axis=0)

    def work(count, members, reaches):
        span = count * BLOCK
        windows = [
            pl.ds(pl.multiple_of((i + WB + 1 - count) * BLOCK, BLOCK), span) for i in members
        ]
        lanes = range(len(members))

        def split(x):
            return [x[b * BLOCK : (b + 1) * BLOCK] for b in range(count)]

        query = [stacked(i, 0) for i in members]
        grad = [stacked(i, q_heads) for i in members]
        scores = [split(dot(keys[windows[n], :], query[n], NT)) for n in lanes]
        key_pos = lax.broadcasted_iota(jnp.int32, (BLOCK, rows), 0)
        query_pos = lax.broadcasted_iota(jnp.int32, (BLOCK, rows), 1) % BLOCK
        causal = key_pos <= query_pos
        probs, probs_b, dprob = {}, {}, {}
        for n in lanes:
            scores[n][-1] = jnp.where(causal, scores[n][-1], -jnp.inf)
            seen = [count - 1 - b <= reaches[n] for b in range(count)]
            tops = [
                jnp.where(seen[b], fold(x, jnp.max), -jnp.inf) for b, x in enumerate(scores[n])
            ]
            top = jnp.max(functools.reduce(jnp.maximum, tops), axis=0, keepdims=True)
            shift = [jnp.where(seen[b], top, jnp.inf) for b in range(count)]
            dprob[n] = split(dot(values[windows[n], :], grad[n], NT))
            expo = [jnp.exp2((x - y) * (SCALE * LOG2E)) for x, y in zip(scores[n], shift)]
            total = functools.reduce(jnp.add, [fold(x, jnp.sum) for x in expo])
            inverse = 1.0 / jnp.sum(total, axis=0, keepdims=True)
            probs[n] = [x * inverse for x in expo]
            probs_b[n] = [x.astype(jnp.bfloat16) for x in probs[n]]
        dscore = {}
        for n in lanes:
            dv[windows[n], :] += dot(jnp.concatenate(probs_b[n], axis=0), grad[n], NN)
            delta = functools.reduce(
                jnp.add,
                [
                    fold(x.astype(jnp.float32) * y, jnp.sum)
                    for x, y in zip(probs_b[n], dprob[n])
                ],
            )
            delta = jnp.sum(delta, axis=0, keepdims=True)
            dscore[n] = jnp.concatenate(
                [
                    (x * (y - delta)).astype(jnp.bfloat16)
                    for x, y in zip(probs[n], dprob[n])
                ],
                axis=0,
            )
        for n, i in enumerate(members):
            dk[windows[n], :] += dot(dscore[n], query[n], NN)
            query_grad = dot(dscore[n], keys[windows[n], :], TN) * SCALE
            for h in range(q_heads):
                dq_ref[i, :, h * HEAD : (h + 1) * HEAD] = query_grad[
                    h * BLOCK : (h + 1) * BLOCK, :
                ].astype(dq_ref.dtype)

    def one_step(step, carry):
        members = [step * TOGETHER + n for n in range(TOGETHER)]
        reaches = [reach_of(i) for i in members]
        widest = functools.reduce(jnp.maximum, reaches) + 1
        for count in range(1, WB + 2):
            pl.when(widest == count)(functools.partial(work, count, members, reaches))
        return carry

    lax.fori_loop(0, blocks // TOGETHER, one_step, 0)
    for j in range(blocks):
        rows = slice(j * BLOCK, (j + 1) * BLOCK)
        late = slice(WINDOW + j * BLOCK, WINDOW + (j + 1) * BLOCK)
        dkv_halo_ref[j, :, :HEAD] = (dk[rows, :] * SCALE).astype(dkv_halo_ref.dtype)
        dkv_halo_ref[j, :, HEAD:] = dv[rows, :].astype(dkv_halo_ref.dtype)
        dkv_own_ref[j, :, :HEAD] = dk[late, :] * SCALE
        dkv_own_ref[j, :, HEAD:] = dv[late, :]


def attend(chunk_index, doc_ids, band, queries_grads, own, halo):
    blocks = own.shape[0]
    total = WINDOW + blocks * BLOCK
    smem = pl.BlockSpec(memory_space=pltpu.SMEM)
    vmem = pl.BlockSpec(memory_space=pltpu.VMEM)
    return pl.pallas_call(
        attend_kernel,
        in_specs=[smem] * 3 + [vmem] * 3,
        out_specs=[vmem] * 3,
        out_shape=[
            jax.ShapeDtypeStruct(
                (blocks, BLOCK, queries_grads.shape[2] // 2), jnp.bfloat16
            ),
            jax.ShapeDtypeStruct(own.shape, jnp.float32),
            jax.ShapeDtypeStruct(own.shape, jnp.bfloat16),
        ],
        scratch_shapes=[
            pltpu.VMEM((total, HEAD), jnp.bfloat16),
            pltpu.VMEM((total, HEAD), jnp.bfloat16),
            pltpu.VMEM((total, HEAD), jnp.float32),
            pltpu.VMEM((total, HEAD), jnp.float32),
        ],
        compiler_params=pltpu.CompilerParams(vmem_limit_bytes=40 * 1024 * 1024),
    )(chunk_index, doc_ids, band, queries_grads, own, halo)


def per_device(queries, keys, values, upstream, doc_ids, band):
    tokens = queries.shape[0]
    parts = WINDOW // tokens
    cores = lax.axis_size("heads")
    spans = lax.axis_size("blk")
    step = parts // cores
    axes = ("blk", "heads")
    groups = [
        [first * parts + member for member in range(parts)] for first in range(spans // step)
    ]

    def exchange(value):
        return lax.all_to_all(
            value, axes, split_axis=0, concat_axis=0, axis_index_groups=groups, tiled=True
        )

    kv = exchange(pack(keys, values, parts))
    halo = lax.ppermute(kv, "blk", [(s, s + step) for s in range(spans - step)])
    qd = exchange(pack(queries, upstream, parts))
    chunk_index = (lax.axis_index("blk") // step).astype(jnp.int32).reshape(1)
    dq, dkv_own, dkv_halo = attend(chunk_index, doc_ids, band, qd, kv, halo)
    spill = lax.ppermute(dkv_halo, "blk", [(s + step, s) for s in range(spans - step)])
    query_out = exchange(dq)
    dkv = exchange((dkv_own + spill.astype(jnp.float32)).astype(jnp.bfloat16))

    return (*unpack(query_out, 1), *unpack(dkv, 2))


def solution(mesh):
    sharded = P(("groups", "blk", "heads"), None)
    return jax.shard_map(
        per_device,
        mesh=mesh,
        in_specs=(sharded,) * 4 + (P("groups"),) * 2,
        out_specs=(sharded,) * 3,
        check_vma=False,
    )
```

```python
import functools
import math

import jax
import jax.numpy as jnp
from jax import lax
from jax.experimental import pallas as pl
from jax.experimental.pallas import tpu as pltpu
from jax.sharding import PartitionSpec as P

HEAD = 128
SCALAR = 168
WINDOW = 1024
BLOCK = 128
WB = WINDOW // BLOCK
SCALE = SCALAR ** (-0.5)
LOG2E = math.log2(math.e)
SMALL = 8 * 1024 * 1024
TOGETHER = 4

NT = (((1,), (1,)), ((), ()))
NN = (((1,), (0,)), ((), ()))
TN = (((0,), (0,)), ((), ()))


def dot(a, b, dims):
    return lax.dot_general(a, b, dims, preferred_element_type=jnp.float32)


def run_copies(pairs, sems):
    copies = [pltpu.make_async_copy(x, y, sems.at[n]) for n, (x, y) in enumerate(pairs)]
    for copy in copies:
        copy.start()
    for copy in copies:
        copy.wait()


def pack_kernel(a_ref, b_ref, out_ref, slabs, in_sems, out_sems):
    heads = out_ref.shape[0]
    width = out_ref.shape[2] // 2
    reads = [
        [
            pltpu.make_async_copy(
                ref.at[:, pl.ds(h * width, width)],
                slabs.at[h, :, pl.ds(n * width, width)],
                in_sems.at[2 * h + n],
            )
            for n, ref in enumerate((a_ref, b_ref))
        ]
        for h in range(heads)
    ]
    writes = [
        pltpu.make_async_copy(slabs.at[h], out_ref.at[h], out_sems.at[h]) for h in range(heads)
    ]
    for pair in reads:
        for copy in pair:
            copy.start()
    for pair, write in zip(reads, writes):
        for copy in pair:
            copy.wait()
        write.start()
    for write in writes:
        write.wait()


def pack(a, b, heads):
    tokens, cols = a.shape
    hbm = pl.BlockSpec(memory_space=pl.ANY)
    shape = (heads, tokens, 2 * cols // heads)
    return pl.pallas_call(
        pack_kernel,
        in_specs=[hbm] * 2,
        out_specs=hbm,
        out_shape=jax.ShapeDtypeStruct(shape, a.dtype),
        scratch_shapes=[
            pltpu.VMEM(shape, a.dtype),
            pltpu.SemaphoreType.DMA((2 * heads,)),
            pltpu.SemaphoreType.DMA((heads,)),
        ],
    )(a, b)


def unpack_kernel(in_ref, *refs):
    out_refs, sems = refs[:-1], refs[-1]
    width = in_ref.shape[2] // len(out_refs)
    run_copies(
        [
            (in_ref.at[h, :, pl.ds(n * width, width)], ref.at[:, pl.ds(h * width, width)])
            for h in range(in_ref.shape[0])
            for n, ref in enumerate(out_refs)
        ],
        sems,
    )


def unpack(value, outputs):
    heads, tokens, width = value.shape
    shape = jax.ShapeDtypeStruct((tokens, heads * width // outputs), value.dtype)
    return pl.pallas_call(
        unpack_kernel,
        in_specs=[pl.BlockSpec(memory_space=pltpu.VMEM)],
        out_specs=[pl.BlockSpec(memory_space=pl.ANY)] * outputs,
        out_shape=[shape] * outputs,
        scratch_shapes=[pltpu.SemaphoreType.DMA((outputs * heads,))],
        compiler_params=pltpu.CompilerParams(vmem_limit_bytes=SMALL),
    )(value)


def attend_kernel(
    chunk_ref, doc_ref, band_ref, qd_ref, own_ref, halo_ref,
    dq_ref, dkv_own_ref, dkv_halo_ref,
    keys, values, dk, dv,
):
    chunk = own_ref.shape[0] * BLOCK
    blocks = chunk // BLOCK
    q_heads = qd_ref.shape[2] // (2 * HEAD)
    for j in range(blocks):
        rows = slice(j * BLOCK, (j + 1) * BLOCK)
        late = slice(WINDOW + j * BLOCK, WINDOW + (j + 1) * BLOCK)
        keys[rows, :] = halo_ref[j, :, :HEAD]
        values[rows, :] = halo_ref[j, :, HEAD:]
        keys[late, :] = own_ref[j, :, :HEAD]
        values[late, :] = own_ref[j, :, HEAD:]
    dk[...] = jnp.zeros_like(dk)
    dv[...] = jnp.zeros_like(dv)
    first = chunk_ref[0] * blocks

    def reach_of(i):
        index = first + i
        own_band = band_ref[index]
        own_doc = doc_ref[index]
        reach = jnp.int32(0)
        for back in range(1, WB + 1):
            seen = (
                (back <= own_band)
                & (index >= back)
                & (doc_ref[jnp.maximum(index - back, 0)] == own_doc)
            )
            reach = reach + seen.astype(jnp.int32)
        return reach

    rows = q_heads * BLOCK

    def stacked(i, offset):
        return jnp.concatenate(
            [qd_ref[i, :, (offset + h) * HEAD : (offset + h + 1) * HEAD] for h in range(q_heads)],
            axis=0,
        )

    def fold(x, reduce):
        return reduce(x.reshape(BLOCK // 8, 8, rows), axis=0)

    def work(count, members, reaches):
        span = count * BLOCK
        windows = [
            pl.ds(pl.multiple_of((i + WB + 1 - count) * BLOCK, BLOCK), span) for i in members
        ]
        lanes = range(len(members))

        def split(x):
            return [x[b * BLOCK : (b + 1) * BLOCK] for b in range(count)]

        query = [stacked(i, 0) for i in members]
        grad = [stacked(i, q_heads) for i in members]
        scores = [split(dot(keys[windows[n], :], query[n], NT)) for n in lanes]
        key_pos = lax.broadcasted_iota(jnp.int32, (BLOCK, rows), 0)
        query_pos = lax.broadcasted_iota(jnp.int32, (BLOCK, rows), 1) % BLOCK
        causal = key_pos <= query_pos
        probs, probs_b, dprob = {}, {}, {}
        for n in lanes:
            scores[n][-1] = jnp.where(causal, scores[n][-1], -jnp.inf)
            seen = [count - 1 - b <= reaches[n] for b in range(count)]
            tops = [
                jnp.where(seen[b], fold(x, jnp.max), -jnp.inf) for b, x in enumerate(scores[n])
            ]
            top = jnp.max(functools.reduce(jnp.maximum, tops), axis=0, keepdims=True)
            shift = [jnp.where(seen[b], top, jnp.inf) for b in range(count)]
            dprob[n] = split(dot(values[windows[n], :], grad[n], NT))
            expo = [jnp.exp2((x - y) * (SCALE * LOG2E)) for x, y in zip(scores[n], shift)]
            total = functools.reduce(jnp.add, [fold(x, jnp.sum) for x in expo])
            inverse = 1.0 / jnp.sum(total, axis=0, keepdims=True)
            probs[n] = [x * inverse for x in expo]
            probs_b[n] = [x.astype(jnp.bfloat16) for x in probs[n]]
        dscore = {}
        for n in lanes:
            dv[windows[n], :] += dot(jnp.concatenate(probs_b[n], axis=0), grad[n], NN)
            delta = functools.reduce(
                jnp.add,
                [
                    fold(x.astype(jnp.float32) * y, jnp.sum)
                    for x, y in zip(probs_b[n], dprob[n])
                ],
            )
            delta = jnp.sum(delta, axis=0, keepdims=True)
            dscore[n] = jnp.concatenate(
                [
                    (x * (y - delta)).astype(jnp.bfloat16)
                    for x, y in zip(probs[n], dprob[n])
                ],
                axis=0,
            )
        for n, i in enumerate(members):
            dk[windows[n], :] += dot(dscore[n], query[n], NN)
            query_grad = dot(dscore[n], keys[windows[n], :], TN) * SCALE
            for h in range(q_heads):
                dq_ref[i, :, h * HEAD : (h + 1) * HEAD] = query_grad[
                    h * BLOCK : (h + 1) * BLOCK, :
                ].astype(dq_ref.dtype)

    def one_step(step, carry):
        members = [step * TOGETHER + n for n in range(TOGETHER)]
        reaches = [reach_of(i) for i in members]
        widest = functools.reduce(jnp.maximum, reaches) + 1
        for count in range(1, WB + 2):
            pl.when(widest == count)(functools.partial(work, count, members, reaches))
        return carry

    lax.fori_loop(0, blocks // TOGETHER, one_step, 0)
    for j in range(blocks):
        rows = slice(j * BLOCK, (j + 1) * BLOCK)
        late = slice(WINDOW + j * BLOCK, WINDOW + (j + 1) * BLOCK)
        dkv_halo_ref[j, :, :HEAD] = (dk[rows, :] * SCALE).astype(dkv_halo_ref.dtype)
        dkv_halo_ref[j, :, HEAD:] = dv[rows, :].astype(dkv_halo_ref.dtype)
        dkv_own_ref[j, :, :HEAD] = dk[late, :] * SCALE
        dkv_own_ref[j, :, HEAD:] = dv[late, :]


def attend(chunk_index, doc_ids, band, queries_grads, own, halo):
    blocks = own.shape[0]
    total = WINDOW + blocks * BLOCK
    smem = pl.BlockSpec(memory_space=pltpu.SMEM)
    vmem = pl.BlockSpec(memory_space=pltpu.VMEM)
    return pl.pallas_call(
        attend_kernel,
        in_specs=[smem] * 3 + [vmem] * 3,
        out_specs=[vmem] * 3,
        out_shape=[
            jax.ShapeDtypeStruct(
                (blocks, BLOCK, queries_grads.shape[2] // 2), jnp.bfloat16
            ),
            jax.ShapeDtypeStruct(own.shape, jnp.float32),
            jax.ShapeDtypeStruct(own.shape, jnp.bfloat16),
        ],
        scratch_shapes=[
            pltpu.VMEM((total, HEAD), jnp.bfloat16),
            pltpu.VMEM((total, HEAD), jnp.bfloat16),
            pltpu.VMEM((total, HEAD), jnp.float32),
            pltpu.VMEM((total, HEAD), jnp.float32),
        ],
        compiler_params=pltpu.CompilerParams(vmem_limit_bytes=40 * 1024 * 1024),
    )(chunk_index, doc_ids, band, queries_grads, own, halo)


def per_device(queries, keys, values, upstream, doc_ids, band):
    tokens = queries.shape[0]
    parts = WINDOW // tokens
    cores = lax.axis_size("heads")
    spans = lax.axis_size("blk")
    step = parts // cores
    axes = ("blk", "heads")
    groups = [
        [first * parts + member for member in range(parts)] for first in range(spans // step)
    ]

    def exchange(value):
        return lax.all_to_all(
            value, axes, split_axis=0, concat_axis=0, axis_index_groups=groups, tiled=True
        )

    kv = exchange(pack(keys, values, parts))
    halo = lax.ppermute(kv, "blk", [(s, s + step) for s in range(spans - step)])
    qd = exchange(pack(queries, upstream, parts))
    chunk_index = (lax.axis_index("blk") // step).astype(jnp.int32).reshape(1)
    dq, dkv_own, dkv_halo = attend(chunk_index, doc_ids, band, qd, kv, halo)
    spill = lax.ppermute(dkv_halo, "blk", [(s + step, s) for s in range(spans - step)])
    query_out = exchange(dq)
    dkv = exchange((dkv_own + spill.astype(jnp.float32)).astype(jnp.bfloat16))

    return (*unpack(query_out, 1), *unpack(dkv, 2))


def solution(mesh):
    sharded = P(("groups", "blk", "heads"), None)
    return jax.shard_map(
        per_device,
        mesh=mesh,
        in_specs=(sharded,) * 4 + (P("groups"),) * 2,
        out_specs=(sharded,) * 3,
        check_vma=False,
    )
```

```python
import functools
import math

import jax
import jax.numpy as jnp
from jax import lax
from jax.experimental import pallas as pl
from jax.experimental.pallas import tpu as pltpu
from jax.sharding import PartitionSpec as P

HEAD = 128
SCALAR = 168
WINDOW = 1024
BLOCK = 128
WB = WINDOW // BLOCK
SCALE = SCALAR ** (-0.5)
LOG2E = math.log2(math.e)
SMALL = 8 * 1024 * 1024
TOGETHER = 2

NT = (((1,), (1,)), ((), ()))
NN = (((1,), (0,)), ((), ()))


def dot(a, b, dims):
    return lax.dot_general(a, b, dims, preferred_element_type=jnp.float32)


def run_copies(pairs, sems):
    copies = [pltpu.make_async_copy(x, y, sems.at[n]) for n, (x, y) in enumerate(pairs)]
    for copy in copies:
        copy.start()
    for copy in copies:
        copy.wait()


def pack_kernel(a_ref, b_ref, out_ref, slabs, in_sems, out_sems):
    heads = out_ref.shape[0]
    width = out_ref.shape[2] // 2
    reads = [
        [
            pltpu.make_async_copy(
                ref.at[:, pl.ds(h * width, width)],
                slabs.at[h, :, pl.ds(n * width, width)],
                in_sems.at[2 * h + n],
            )
            for n, ref in enumerate((a_ref, b_ref))
        ]
        for h in range(heads)
    ]
    writes = [
        pltpu.make_async_copy(slabs.at[h], out_ref.at[h], out_sems.at[h]) for h in range(heads)
    ]
    for pair in reads:
        for copy in pair:
            copy.start()
    for pair, write in zip(reads, writes):
        for copy in pair:
            copy.wait()
        write.start()
    for write in writes:
        write.wait()


def pack(a, b, heads):
    tokens, cols = a.shape
    hbm = pl.BlockSpec(memory_space=pl.ANY)
    shape = (heads, tokens, 2 * cols // heads)
    return pl.pallas_call(
        pack_kernel,
        in_specs=[hbm] * 2,
        out_specs=hbm,
        out_shape=jax.ShapeDtypeStruct(shape, a.dtype),
        scratch_shapes=[
            pltpu.VMEM(shape, a.dtype),
            pltpu.SemaphoreType.DMA((2 * heads,)),
            pltpu.SemaphoreType.DMA((heads,)),
        ],
    )(a, b)


def unpack_kernel(in_ref, *refs):
    out_refs, sems = refs[:-1], refs[-1]
    width = in_ref.shape[2] // len(out_refs)
    run_copies(
        [
            (in_ref.at[h, :, pl.ds(n * width, width)], ref.at[:, pl.ds(h * width, width)])
            for h in range(in_ref.shape[0])
            for n, ref in enumerate(out_refs)
        ],
        sems,
    )


def unpack(value, outputs):
    heads, tokens, width = value.shape
    shape = jax.ShapeDtypeStruct((tokens, heads * width // outputs), value.dtype)
    return pl.pallas_call(
        unpack_kernel,
        in_specs=[pl.BlockSpec(memory_space=pltpu.VMEM)],
        out_specs=[pl.BlockSpec(memory_space=pl.ANY)] * outputs,
        out_shape=[shape] * outputs,
        scratch_shapes=[pltpu.SemaphoreType.DMA((outputs * heads,))],
        compiler_params=pltpu.CompilerParams(vmem_limit_bytes=SMALL),
    )(value)


def attend_kernel(
    chunk_ref, doc_ref, band_ref, qd_ref, own_ref, halo_ref,
    dq_ref, dkv_own_ref, dkv_halo_ref,
    keys, keys_t, values, dk, dv, order, counts,
):
    chunk = own_ref.shape[0] * BLOCK
    blocks = chunk // BLOCK
    q_heads = qd_ref.shape[2] // (2 * HEAD)
    for j in range(blocks):
        rows = slice(j * BLOCK, (j + 1) * BLOCK)
        late = slice(WINDOW + j * BLOCK, WINDOW + (j + 1) * BLOCK)
        keys[rows, :] = halo_ref[j, :, :HEAD]
        values[rows, :] = halo_ref[j, :, HEAD:]
        keys[late, :] = own_ref[j, :, :HEAD]
        keys_t[:, rows] = halo_ref[j, :, :HEAD].T
        keys_t[:, late] = own_ref[j, :, :HEAD].T
        values[late, :] = own_ref[j, :, HEAD:]
    dk[...] = jnp.zeros_like(dk)
    dv[...] = jnp.zeros_like(dv)
    first = chunk_ref[0] * blocks

    length = jnp.int32(0)
    for back in range(1, WB + 1):
        same = (first >= back) & (doc_ref[jnp.maximum(first - back, 0)] == doc_ref[first])
        length = length + same.astype(jnp.int32)
    seen = []
    for i in range(blocks):
        if i > 0:
            same = doc_ref[first + i] == doc_ref[first + i - 1]
            length = jnp.where(same, length + 1, 0)
        seen.append(jnp.minimum(band_ref[first + i], length) + 1)
    for i in range(blocks):
        rank = jnp.int32(0)
        for j in range(blocks):
            if j != i:
                below = seen[j] <= seen[i] if j < i else seen[j] < seen[i]
                rank = rank + below.astype(jnp.int32)
        order[rank] = i
        counts[rank] = seen[i]

    rows = q_heads * BLOCK

    def stacked(i, offset):
        return jnp.concatenate(
            [qd_ref[i, :, (offset + h) * HEAD : (offset + h + 1) * HEAD] for h in range(q_heads)],
            axis=0,
        )

    def fold(x, reduce):
        return reduce(x.reshape(BLOCK // 8, 8, rows), axis=0)

    def work(count, members, sizes):
        span = count * BLOCK
        windows = [
            pl.ds(pl.multiple_of((i + WB + 1 - count) * BLOCK, BLOCK), span) for i in members
        ]
        lanes = range(len(members))

        def split(x):
            return [x[b * BLOCK : (b + 1) * BLOCK] for b in range(count)]

        query = [stacked(i, 0) for i in members]
        grad = [stacked(i, q_heads) for i in members]
        scores = [split(dot(keys[windows[n], :], query[n], NT)) for n in lanes]
        key_pos = lax.broadcasted_iota(jnp.int32, (BLOCK, rows), 0)
        query_pos = lax.broadcasted_iota(jnp.int32, (BLOCK, rows), 1) % BLOCK
        causal = key_pos <= query_pos
        probs_b, dprob = {}, {}
        for n in lanes:
            scores[n][-1] = jnp.where(causal, scores[n][-1], -jnp.inf)
            seen = [count - b <= sizes[n] for b in range(count)]
            tops = [
                jnp.where(seen[b], fold(x, jnp.max), -jnp.inf) for b, x in enumerate(scores[n])
            ]
            top = jnp.max(functools.reduce(jnp.maximum, tops), axis=0, keepdims=True)
            shift = [jnp.where(seen[b], top, jnp.inf) for b in range(count)]
            dprob[n] = split(dot(values[windows[n], :], grad[n], NT))
            expo = [jnp.exp2((x - y) * (SCALE * LOG2E)) for x, y in zip(scores[n], shift)]
            total = functools.reduce(jnp.add, [fold(x, jnp.sum) for x in expo])
            inverse = 1.0 / jnp.sum(total, axis=0, keepdims=True)
            probs_b[n] = [(x * inverse).astype(jnp.bfloat16) for x in expo]
        dscore = {}
        for n in lanes:
            dv[windows[n], :] += dot(jnp.concatenate(probs_b[n], axis=0), grad[n], NN)
            delta = functools.reduce(
                jnp.add,
                [
                    fold(x.astype(jnp.float32) * y, jnp.sum)
                    for x, y in zip(probs_b[n], dprob[n])
                ],
            )
            delta = jnp.sum(delta, axis=0, keepdims=True)
            dscore[n] = jnp.concatenate(
                [
                    (x.astype(jnp.float32) * (y - delta)).astype(jnp.bfloat16)
                    for x, y in zip(probs_b[n], dprob[n])
                ],
                axis=0,
            )
        for n, i in enumerate(members):
            dk[windows[n], :] += dot(dscore[n], query[n], NN)
            query_grad = dot(keys_t[:, windows[n]], dscore[n], NN) * SCALE
            for h in range(q_heads):
                dq_ref[i, :, h * HEAD : (h + 1) * HEAD] = query_grad[
                    :, h * BLOCK : (h + 1) * BLOCK
                ].T.astype(dq_ref.dtype)

    def one_step(step, carry):
        members = [order[step * TOGETHER + n] for n in range(TOGETHER)]
        sizes = [counts[step * TOGETHER + n] for n in range(TOGETHER)]
        for count in range(1, WB + 2):
            pl.when(sizes[-1] == count)(functools.partial(work, count, members, sizes))
        return carry

    lax.fori_loop(0, blocks // TOGETHER, one_step, 0)
    for j in range(blocks):
        rows = slice(j * BLOCK, (j + 1) * BLOCK)
        late = slice(WINDOW + j * BLOCK, WINDOW + (j + 1) * BLOCK)
        dkv_halo_ref[j, :, :HEAD] = (dk[rows, :] * SCALE).astype(dkv_halo_ref.dtype)
        dkv_halo_ref[j, :, HEAD:] = dv[rows, :].astype(dkv_halo_ref.dtype)
        dkv_own_ref[j, :, :HEAD] = dk[late, :] * SCALE
        dkv_own_ref[j, :, HEAD:] = dv[late, :]


def attend(chunk_index, doc_ids, band, queries_grads, own, halo):
    blocks = own.shape[0]
    total = WINDOW + blocks * BLOCK
    smem = pl.BlockSpec(memory_space=pltpu.SMEM)
    vmem = pl.BlockSpec(memory_space=pltpu.VMEM)
    return pl.pallas_call(
        attend_kernel,
        in_specs=[smem] * 3 + [vmem] * 3,
        out_specs=[vmem] * 3,
        out_shape=[
            jax.ShapeDtypeStruct(
                (blocks, BLOCK, queries_grads.shape[2] // 2), jnp.bfloat16
            ),
            jax.ShapeDtypeStruct(own.shape, jnp.float32),
            jax.ShapeDtypeStruct(own.shape, jnp.bfloat16),
        ],
        scratch_shapes=[
            pltpu.VMEM((total, HEAD), jnp.bfloat16),
            pltpu.VMEM((HEAD, total), jnp.bfloat16),
            pltpu.VMEM((total, HEAD), jnp.bfloat16),
            pltpu.VMEM((total, HEAD), jnp.float32),
            pltpu.VMEM((total, HEAD), jnp.float32),
            pltpu.SMEM((blocks,), jnp.int32),
            pltpu.SMEM((blocks,), jnp.int32),
        ],
        compiler_params=pltpu.CompilerParams(vmem_limit_bytes=40 * 1024 * 1024),
    )(chunk_index, doc_ids, band, queries_grads, own, halo)


def add_kernel(own_ref, spill_ref, out_ref, slabs, sems):
    copies = []
    for j in range(out_ref.shape[0]):
        slabs[j] = (own_ref[j] + spill_ref[j].astype(jnp.float32)).astype(slabs.dtype)
        copies.append(pltpu.make_async_copy(slabs.at[j], out_ref.at[j], sems.at[j]))
        copies[j].start()
    for copy in copies:
        copy.wait()


def add_spill(own, spill):
    return pl.pallas_call(
        add_kernel,
        in_specs=[pl.BlockSpec(memory_space=pltpu.VMEM)] * 2,
        out_specs=pl.BlockSpec(memory_space=pl.ANY),
        out_shape=jax.ShapeDtypeStruct(spill.shape, spill.dtype),
        scratch_shapes=[
            pltpu.VMEM(spill.shape, spill.dtype),
            pltpu.SemaphoreType.DMA((spill.shape[0],)),
        ],
        compiler_params=pltpu.CompilerParams(vmem_limit_bytes=SMALL),
    )(own, spill)


def per_device(queries, keys, values, upstream, doc_ids, band):
    tokens = queries.shape[0]
    parts = WINDOW // tokens
    cores = lax.axis_size("heads")
    spans = lax.axis_size("blk")
    step = parts // cores
    axes = ("blk", "heads")
    groups = [
        [first * parts + member for member in range(parts)] for first in range(spans // step)
    ]

    def exchange(value):
        return lax.all_to_all(
            value, axes, split_axis=0, concat_axis=0, axis_index_groups=groups, tiled=True
        )

    kv = exchange(pack(keys, values, parts))
    halo = lax.ppermute(kv, "blk", [(s, s + step) for s in range(spans - step)])
    qd = exchange(pack(queries, upstream, parts))
    chunk_index = (lax.axis_index("blk") // step).astype(jnp.int32).reshape(1)
    dq, dkv_own, dkv_halo = attend(chunk_index, doc_ids, band, qd, kv, halo)
    spill = lax.ppermute(dkv_halo, "blk", [(s + step, s) for s in range(spans - step)])
    query_out = exchange(dq)
    dkv = exchange(add_spill(dkv_own, spill))

    return (*unpack(query_out, 1), *unpack(dkv, 2))


def solution(mesh):
    sharded = P(("groups", "blk", "heads"), None)
    return jax.shard_map(
        per_device,
        mesh=mesh,
        in_specs=(sharded,) * 4 + (P("groups"),) * 2,
        out_specs=(sharded,) * 3,
        check_vma=False,
    )
```

```python
import functools
import math

import jax
import jax.numpy as jnp
from jax import lax
from jax.experimental import pallas as pl
from jax.experimental.pallas import tpu as pltpu
from jax.sharding import PartitionSpec as P

HEAD = 128
SCALAR = 168
WINDOW = 1024
BLOCK = 128
WB = WINDOW // BLOCK
SCALE = SCALAR ** (-0.5)
LOG2E = math.log2(math.e)
SMALL = 8 * 1024 * 1024
TOGETHER = 2

NT = (((1,), (1,)), ((), ()))
NN = (((1,), (0,)), ((), ()))


def dot(a, b, dims):
    return lax.dot_general(a, b, dims, preferred_element_type=jnp.float32)


def run_copies(pairs, sems):
    copies = [pltpu.make_async_copy(x, y, sems.at[n]) for n, (x, y) in enumerate(pairs)]
    for copy in copies:
        copy.start()
    for copy in copies:
        copy.wait()


def pack_kernel(a_ref, b_ref, out_ref, sems):
    width = out_ref.shape[2] // 2
    run_copies(
        [
            (ref.at[:, pl.ds(h * width, width)], out_ref.at[h, :, pl.ds(n * width, width)])
            for h in range(out_ref.shape[0])
            for n, ref in enumerate((a_ref, b_ref))
        ],
        sems,
    )


def pack(a, b, heads):
    tokens, cols = a.shape
    return pl.pallas_call(
        pack_kernel,
        in_specs=[pl.BlockSpec(memory_space=pltpu.VMEM)] * 2,
        out_specs=pl.BlockSpec(memory_space=pl.ANY),
        out_shape=jax.ShapeDtypeStruct((heads, tokens, 2 * cols // heads), a.dtype),
        scratch_shapes=[pltpu.SemaphoreType.DMA((2 * heads,))],
        compiler_params=pltpu.CompilerParams(vmem_limit_bytes=SMALL),
    )(a, b)


def unpack_kernel(in_ref, *refs):
    out_refs, sems = refs[:-1], refs[-1]
    width = in_ref.shape[2] // len(out_refs)
    run_copies(
        [
            (in_ref.at[h, :, pl.ds(n * width, width)], ref.at[:, pl.ds(h * width, width)])
            for h in range(in_ref.shape[0])
            for n, ref in enumerate(out_refs)
        ],
        sems,
    )


def unpack(value, outputs):
    heads, tokens, width = value.shape
    shape = jax.ShapeDtypeStruct((tokens, heads * width // outputs), value.dtype)
    return pl.pallas_call(
        unpack_kernel,
        in_specs=[pl.BlockSpec(memory_space=pltpu.VMEM)],
        out_specs=[pl.BlockSpec(memory_space=pl.ANY)] * outputs,
        out_shape=[shape] * outputs,
        scratch_shapes=[pltpu.SemaphoreType.DMA((outputs * heads,))],
        compiler_params=pltpu.CompilerParams(vmem_limit_bytes=SMALL),
    )(value)


def prepare_kernel(chunk_ref, doc_ref, band_ref, own_ref, order, counts, keys_t_ref):
    blocks = own_ref.shape[0]
    for j in range(blocks):
        keys_t_ref[:, j * BLOCK : (j + 1) * BLOCK] = own_ref[j, :, :HEAD].T
    first = chunk_ref[0] * blocks
    length = jnp.int32(0)
    for back in range(1, WB + 1):
        same = (first >= back) & (doc_ref[jnp.maximum(first - back, 0)] == doc_ref[first])
        length = length + same.astype(jnp.int32)
    seen = []
    for i in range(blocks):
        if i > 0:
            same = doc_ref[first + i] == doc_ref[first + i - 1]
            length = jnp.where(same, length + 1, 0)
        seen.append(jnp.minimum(band_ref[first + i], length) + 1)
    for i in range(blocks):
        rank = jnp.int32(0)
        for j in range(blocks):
            if j != i:
                below = seen[j] <= seen[i] if j < i else seen[j] < seen[i]
                rank = rank + below.astype(jnp.int32)
        order[rank] = i
        counts[rank] = seen[i]


def prepare(chunk_index, doc_ids, band, own):
    blocks = own.shape[0]
    smem = pl.BlockSpec(memory_space=pltpu.SMEM)
    vmem = pl.BlockSpec(memory_space=pltpu.VMEM)
    return pl.pallas_call(
        prepare_kernel,
        in_specs=[smem] * 3 + [vmem],
        out_specs=[smem] * 2 + [vmem],
        out_shape=[jax.ShapeDtypeStruct((blocks,), jnp.int32)] * 2
        + [jax.ShapeDtypeStruct((HEAD, blocks * BLOCK), own.dtype)],
        compiler_params=pltpu.CompilerParams(vmem_limit_bytes=SMALL),
    )(chunk_index, doc_ids, band, own)


def attend_kernel(
    order, counts, qd_ref, own_ref, keys_t_ref, halo_ref,
    dq_ref, dkv_own_ref, dkv_halo_ref,
    keys, keys_t, values, dk, dv, dq_slabs, halo_slabs, dq_sems, halo_sems,
):
    blocks = own_ref.shape[0]
    q_heads = qd_ref.shape[2] // (2 * HEAD)
    for j in range(blocks):
        early = slice(j * BLOCK, (j + 1) * BLOCK)
        late = slice(WINDOW + j * BLOCK, WINDOW + (j + 1) * BLOCK)
        keys[early, :] = halo_ref[j, :, :HEAD]
        values[early, :] = halo_ref[j, :, HEAD:]
        keys[late, :] = own_ref[j, :, :HEAD]
        values[late, :] = own_ref[j, :, HEAD:]
        keys_t[:, early] = halo_ref[j, :, :HEAD].T
        keys_t[:, late] = keys_t_ref[:, early]
    dk[...] = jnp.zeros_like(dk)
    dv[...] = jnp.zeros_like(dv)

    def dq_copy(i):
        return pltpu.make_async_copy(dq_slabs.at[i], dq_ref.at[i], dq_sems.at[i])

    def halo_copy(j):
        return pltpu.make_async_copy(halo_slabs.at[j], dkv_halo_ref.at[j], halo_sems.at[j])

    rows = q_heads * BLOCK

    def stacked(i, offset):
        return jnp.concatenate(
            [qd_ref[i, :, (offset + h) * HEAD : (offset + h + 1) * HEAD] for h in range(q_heads)],
            axis=0,
        )

    def fold(x, reduce):
        return reduce(x.reshape(BLOCK // 8, 8, rows), axis=0)

    def work(count, members, sizes):
        span = count * BLOCK
        windows = [
            pl.ds(pl.multiple_of((i + WB + 1 - count) * BLOCK, BLOCK), span) for i in members
        ]
        lanes = range(len(members))

        def split(x):
            return [x[b * BLOCK : (b + 1) * BLOCK] for b in range(count)]

        query = [stacked(i, 0) for i in members]
        grad = [stacked(i, q_heads) for i in members]
        scores = [split(dot(keys[windows[n], :], query[n], NT)) for n in lanes]
        key_pos = lax.broadcasted_iota(jnp.int32, (BLOCK, rows), 0)
        query_pos = lax.broadcasted_iota(jnp.int32, (BLOCK, rows), 1) % BLOCK
        causal = key_pos <= query_pos
        probs, probs_b, dprob = {}, {}, {}
        for n in lanes:
            scores[n][-1] = jnp.where(causal, scores[n][-1], -jnp.inf)
            seen = [count - b <= sizes[n] for b in range(count)]
            tops = [
                jnp.where(seen[b], fold(x, jnp.max), -jnp.inf) for b, x in enumerate(scores[n])
            ]
            top = jnp.max(functools.reduce(jnp.maximum, tops), axis=0, keepdims=True)
            shift = [jnp.where(seen[b], top, jnp.inf) for b in range(count)]
            dprob[n] = split(dot(values[windows[n], :], grad[n], NT))
            expo = [jnp.exp2((x - y) * (SCALE * LOG2E)) for x, y in zip(scores[n], shift)]
            total = functools.reduce(jnp.add, [fold(x, jnp.sum) for x in expo])
            inverse = 1.0 / jnp.sum(total, axis=0, keepdims=True)
            probs[n] = [x * inverse for x in expo]
            probs_b[n] = [x.astype(jnp.bfloat16) for x in probs[n]]
        dscore = {}
        for n in lanes:
            dv[windows[n], :] += dot(jnp.concatenate(probs_b[n], axis=0), grad[n], NN)
            delta = functools.reduce(
                jnp.add,
                [
                    fold(x.astype(jnp.float32) * y, jnp.sum)
                    for x, y in zip(probs_b[n], dprob[n])
                ],
            )
            delta = jnp.sum(delta, axis=0, keepdims=True)
            dscore[n] = jnp.concatenate(
                [
                    (x * (y - delta)).astype(jnp.bfloat16)
                    for x, y in zip(probs[n], dprob[n])
                ],
                axis=0,
            )
        for n, i in enumerate(members):
            dk[windows[n], :] += dot(dscore[n], query[n], NN)
            query_grad = dot(keys_t[:, windows[n]], dscore[n], NN) * SCALE
            for h in range(q_heads):
                dq_slabs[i, :, h * HEAD : (h + 1) * HEAD] = query_grad[
                    :, h * BLOCK : (h + 1) * BLOCK
                ].T.astype(dq_ref.dtype)
            dq_copy(i).start()

    def one_step(step, carry):
        members = [order[step * TOGETHER + n] for n in range(TOGETHER)]
        sizes = [counts[step * TOGETHER + n] for n in range(TOGETHER)]
        for count in range(1, WB + 2):
            pl.when(sizes[-1] == count)(functools.partial(work, count, members, sizes))
        return carry

    lax.fori_loop(0, blocks // TOGETHER, one_step, 0)
    for j in range(blocks):
        early = slice(j * BLOCK, (j + 1) * BLOCK)
        halo_slabs[j, :, :HEAD] = (dk[early, :] * SCALE).astype(halo_slabs.dtype)
        halo_slabs[j, :, HEAD:] = dv[early, :].astype(halo_slabs.dtype)
        halo_copy(j).start()
    for j in range(blocks):
        late = slice(WINDOW + j * BLOCK, WINDOW + (j + 1) * BLOCK)
        dkv_own_ref[j, :, :HEAD] = dk[late, :] * SCALE
        dkv_own_ref[j, :, HEAD:] = dv[late, :]
    for i in range(blocks):
        dq_copy(i).wait()
    for j in range(blocks):
        halo_copy(j).wait()


def attend(chunk_index, doc_ids, band, queries_grads, own, halo):
    blocks = own.shape[0]
    total = WINDOW + blocks * BLOCK
    smem = pl.BlockSpec(memory_space=pltpu.SMEM)
    vmem = pl.BlockSpec(memory_space=pltpu.VMEM)
    hbm = pl.BlockSpec(memory_space=pl.ANY)
    order, counts, keys_t = prepare(chunk_index, doc_ids, band, own)
    dq = jax.ShapeDtypeStruct((blocks, BLOCK, queries_grads.shape[2] // 2), jnp.bfloat16)
    return pl.pallas_call(
        attend_kernel,
        in_specs=[smem] * 2 + [vmem] * 4,
        out_specs=[hbm, vmem, hbm],
        out_shape=[
            dq,
            jax.ShapeDtypeStruct(own.shape, jnp.float32),
            jax.ShapeDtypeStruct(own.shape, jnp.bfloat16),
        ],
        scratch_shapes=[
            pltpu.VMEM((total, HEAD), jnp.bfloat16),
            pltpu.VMEM((HEAD, total), jnp.bfloat16),
            pltpu.VMEM((total, HEAD), jnp.bfloat16),
            pltpu.VMEM((total, HEAD), jnp.float32),
            pltpu.VMEM((total, HEAD), jnp.float32),
            pltpu.VMEM(dq.shape, dq.dtype),
            pltpu.VMEM(own.shape, jnp.bfloat16),
            pltpu.SemaphoreType.DMA((blocks,)),
            pltpu.SemaphoreType.DMA((blocks,)),
        ],
        compiler_params=pltpu.CompilerParams(vmem_limit_bytes=40 * 1024 * 1024),
    )(order, counts, queries_grads, own, keys_t, halo)


def add_kernel(own_ref, spill_ref, out_ref, slabs, sems):
    copies = []
    for j in range(out_ref.shape[0]):
        slabs[j] = (own_ref[j] + spill_ref[j].astype(jnp.float32)).astype(slabs.dtype)
        copies.append(pltpu.make_async_copy(slabs.at[j], out_ref.at[j], sems.at[j]))
        copies[j].start()
    for copy in copies:
        copy.wait()


def add_spill(own, spill):
    return pl.pallas_call(
        add_kernel,
        in_specs=[pl.BlockSpec(memory_space=pltpu.VMEM)] * 2,
        out_specs=pl.BlockSpec(memory_space=pl.ANY),
        out_shape=jax.ShapeDtypeStruct(spill.shape, spill.dtype),
        scratch_shapes=[
            pltpu.VMEM(spill.shape, spill.dtype),
            pltpu.SemaphoreType.DMA((spill.shape[0],)),
        ],
        compiler_params=pltpu.CompilerParams(vmem_limit_bytes=SMALL),
    )(own, spill)


def per_device(queries, keys, values, upstream, doc_ids, band):
    tokens = queries.shape[0]
    parts = WINDOW // tokens
    cores = lax.axis_size("heads")
    spans = lax.axis_size("blk")
    step = parts // cores
    axes = ("blk", "heads")
    groups = [
        [first * parts + member for member in range(parts)] for first in range(spans // step)
    ]

    def exchange(value):
        return lax.all_to_all(
            value, axes, split_axis=0, concat_axis=0, axis_index_groups=groups, tiled=True
        )

    kv = exchange(pack(keys, values, parts))
    halo = lax.ppermute(kv, "blk", [(s, s + step) for s in range(spans - step)])
    qd = exchange(pack(queries, upstream, parts))
    chunk_index = (lax.axis_index("blk") // step).astype(jnp.int32).reshape(1)
    dq, dkv_own, dkv_halo = attend(chunk_index, doc_ids, band, qd, kv, halo)
    spill = lax.ppermute(dkv_halo, "blk", [(s + step, s) for s in range(spans - step)])
    query_out = exchange(dq)
    dkv = exchange(add_spill(dkv_own, spill))

    return (*unpack(query_out, 1), *unpack(dkv, 2))


def solution(mesh):
    sharded = P(("groups", "blk", "heads"), None)
    return jax.shard_map(
        per_device,
        mesh=mesh,
        in_specs=(sharded,) * 4 + (P("groups"),) * 2,
        out_specs=(sharded,) * 3,
        check_vma=False,
    )
```

```python
import functools
import math

import jax
import jax.numpy as jnp
from jax import lax
from jax.experimental import pallas as pl
from jax.experimental.pallas import tpu as pltpu
from jax.sharding import PartitionSpec as P

HEAD = 128
SCALAR = 168
WINDOW = 1024
BLOCK = 128
WB = WINDOW // BLOCK
SCALE = SCALAR ** (-0.5)
LOG2E = math.log2(math.e)
SMALL = 8 * 1024 * 1024
TOGETHER = 2

NT = (((1,), (1,)), ((), ()))
NN = (((1,), (0,)), ((), ()))


def dot(a, b, dims):
    return lax.dot_general(a, b, dims, preferred_element_type=jnp.float32)


def run_copies(pairs, sems):
    copies = [pltpu.make_async_copy(x, y, sems.at[n]) for n, (x, y) in enumerate(pairs)]
    for copy in copies:
        copy.start()
    for copy in copies:
        copy.wait()


def pack_kernel(a_ref, b_ref, out_ref, slabs, in_sems, out_sems):
    heads = out_ref.shape[0]
    width = out_ref.shape[2] // 2
    reads = [
        [
            pltpu.make_async_copy(
                ref.at[:, pl.ds(h * width, width)],
                slabs.at[h, :, pl.ds(n * width, width)],
                in_sems.at[2 * h + n],
            )
            for n, ref in enumerate((a_ref, b_ref))
        ]
        for h in range(heads)
    ]
    writes = [
        pltpu.make_async_copy(slabs.at[h], out_ref.at[h], out_sems.at[h]) for h in range(heads)
    ]
    for pair in reads:
        for copy in pair:
            copy.start()
    for pair, write in zip(reads, writes):
        for copy in pair:
            copy.wait()
        write.start()
    for write in writes:
        write.wait()


def pack(a, b, heads):
    tokens, cols = a.shape
    hbm = pl.BlockSpec(memory_space=pl.ANY)
    shape = (heads, tokens, 2 * cols // heads)
    return pl.pallas_call(
        pack_kernel,
        in_specs=[hbm] * 2,
        out_specs=hbm,
        out_shape=jax.ShapeDtypeStruct(shape, a.dtype),
        scratch_shapes=[
            pltpu.VMEM(shape, a.dtype),
            pltpu.SemaphoreType.DMA((2 * heads,)),
            pltpu.SemaphoreType.DMA((heads,)),
        ],
    )(a, b)


def unpack_kernel(in_ref, *refs):
    out_refs, sems = refs[:-1], refs[-1]
    width = in_ref.shape[2] // len(out_refs)
    run_copies(
        [
            (in_ref.at[h, :, pl.ds(n * width, width)], ref.at[:, pl.ds(h * width, width)])
            for h in range(in_ref.shape[0])
            for n, ref in enumerate(out_refs)
        ],
        sems,
    )


def unpack(value, outputs):
    heads, tokens, width = value.shape
    shape = jax.ShapeDtypeStruct((tokens, heads * width // outputs), value.dtype)
    return pl.pallas_call(
        unpack_kernel,
        in_specs=[pl.BlockSpec(memory_space=pltpu.VMEM)],
        out_specs=[pl.BlockSpec(memory_space=pl.ANY)] * outputs,
        out_shape=[shape] * outputs,
        scratch_shapes=[pltpu.SemaphoreType.DMA((outputs * heads,))],
        compiler_params=pltpu.CompilerParams(vmem_limit_bytes=SMALL),
    )(value)


def prepare_kernel(chunk_ref, doc_ref, band_ref, own_ref, order, counts, keys_t_ref):
    blocks = own_ref.shape[0]
    for j in range(blocks):
        keys_t_ref[:, j * BLOCK : (j + 1) * BLOCK] = own_ref[j, :, :HEAD].T
    first = chunk_ref[0] * blocks
    length = jnp.int32(0)
    for back in range(1, WB + 1):
        same = (first >= back) & (doc_ref[jnp.maximum(first - back, 0)] == doc_ref[first])
        length = length + same.astype(jnp.int32)
    seen = []
    for i in range(blocks):
        if i > 0:
            same = doc_ref[first + i] == doc_ref[first + i - 1]
            length = jnp.where(same, length + 1, 0)
        seen.append(jnp.minimum(band_ref[first + i], length) + 1)
    for i in range(blocks):
        rank = jnp.int32(0)
        for j in range(blocks):
            if j != i:
                below = seen[j] <= seen[i] if j < i else seen[j] < seen[i]
                rank = rank + below.astype(jnp.int32)
        order[rank] = i
        counts[rank] = seen[i]


def prepare(chunk_index, doc_ids, band, own):
    blocks = own.shape[0]
    smem = pl.BlockSpec(memory_space=pltpu.SMEM)
    vmem = pl.BlockSpec(memory_space=pltpu.VMEM)
    return pl.pallas_call(
        prepare_kernel,
        in_specs=[smem] * 3 + [vmem],
        out_specs=[smem] * 2 + [vmem],
        out_shape=[jax.ShapeDtypeStruct((blocks,), jnp.int32)] * 2
        + [jax.ShapeDtypeStruct((HEAD, blocks * BLOCK), own.dtype)],
        compiler_params=pltpu.CompilerParams(vmem_limit_bytes=SMALL),
    )(chunk_index, doc_ids, band, own)


def attend_kernel(
    order, counts, qd_ref, own_ref, keys_t_ref, halo_ref,
    dq_ref, dkv_own_ref, dkv_halo_ref,
    kv, keys_t, dk, dv, dq_slabs, halo_slabs, dq_sems, halo_sems,
):
    blocks = own_ref.shape[0]
    q_heads = qd_ref.shape[2] // (2 * HEAD)
    for j in range(blocks):
        early = slice(j * BLOCK, (j + 1) * BLOCK)
        late = slice(WINDOW + j * BLOCK, WINDOW + (j + 1) * BLOCK)
        kv[early, :] = halo_ref[j]
        kv[late, :] = own_ref[j]
        keys_t[:, early] = halo_ref[j, :, :HEAD].T
        keys_t[:, late] = keys_t_ref[:, early]
    dk[...] = jnp.zeros_like(dk)
    dv[...] = jnp.zeros_like(dv)

    def dq_copy(i):
        return pltpu.make_async_copy(dq_slabs.at[i], dq_ref.at[i], dq_sems.at[i])

    def halo_copy(j):
        return pltpu.make_async_copy(halo_slabs.at[j], dkv_halo_ref.at[j], halo_sems.at[j])

    rows = q_heads * BLOCK

    def stacked(i, offset):
        return jnp.concatenate(
            [qd_ref[i, :, (offset + h) * HEAD : (offset + h + 1) * HEAD] for h in range(q_heads)],
            axis=0,
        )

    def fold(x, reduce):
        return reduce(x.reshape(BLOCK // 8, 8, rows), axis=0)

    def work(count, members, sizes):
        span = count * BLOCK
        windows = [
            pl.ds(pl.multiple_of((i + WB + 1 - count) * BLOCK, BLOCK), span) for i in members
        ]
        lanes = range(len(members))

        def split(x):
            return [x[b * BLOCK : (b + 1) * BLOCK] for b in range(count)]

        query = [stacked(i, 0) for i in members]
        grad = [stacked(i, q_heads) for i in members]
        both = []
        for n in lanes:
            blank = jnp.zeros_like(query[n])
            weights = jnp.concatenate(
                [
                    jnp.concatenate([query[n], blank], axis=1),
                    jnp.concatenate([blank, grad[n]], axis=1),
                ],
                axis=0,
            )
            both.append(dot(kv[windows[n], :], weights, NT))
        scores = [split(x[:, :rows]) for x in both]
        dprob = [split(x[:, rows:]) for x in both]
        key_pos = lax.broadcasted_iota(jnp.int32, (BLOCK, rows), 0)
        query_pos = lax.broadcasted_iota(jnp.int32, (BLOCK, rows), 1) % BLOCK
        causal = key_pos <= query_pos
        probs, probs_b = {}, {}
        for n in lanes:
            scores[n][-1] = jnp.where(causal, scores[n][-1], -jnp.inf)
            seen = [count - b <= sizes[n] for b in range(count)]
            tops = [
                jnp.where(seen[b], fold(x, jnp.max), -jnp.inf) for b, x in enumerate(scores[n])
            ]
            top = jnp.max(functools.reduce(jnp.maximum, tops), axis=0, keepdims=True)
            shift = [jnp.where(seen[b], top, jnp.inf) for b in range(count)]
            expo = [jnp.exp2((x - y) * (SCALE * LOG2E)) for x, y in zip(scores[n], shift)]
            total = functools.reduce(jnp.add, [fold(x, jnp.sum) for x in expo])
            inverse = 1.0 / jnp.sum(total, axis=0, keepdims=True)
            probs[n] = [x * inverse for x in expo]
            probs_b[n] = [x.astype(jnp.bfloat16) for x in probs[n]]
        dscore = {}
        for n in lanes:
            dv[windows[n], :] += dot(jnp.concatenate(probs_b[n], axis=0), grad[n], NN)
            delta = functools.reduce(
                jnp.add,
                [
                    fold(x.astype(jnp.float32) * y, jnp.sum)
                    for x, y in zip(probs_b[n], dprob[n])
                ],
            )
            delta = jnp.sum(delta, axis=0, keepdims=True)
            dscore[n] = jnp.concatenate(
                [
                    (x * (y - delta)).astype(jnp.bfloat16)
                    for x, y in zip(probs[n], dprob[n])
                ],
                axis=0,
            )
        for n, i in enumerate(members):
            dk[windows[n], :] += dot(dscore[n], query[n], NN)
            query_grad = dot(keys_t[:, windows[n]], dscore[n], NN) * SCALE
            for h in range(q_heads):
                dq_slabs[i, :, h * HEAD : (h + 1) * HEAD] = query_grad[
                    :, h * BLOCK : (h + 1) * BLOCK
                ].T.astype(dq_ref.dtype)
            dq_copy(i).start()

    def one_step(step, carry):
        members = [order[step * TOGETHER + n] for n in range(TOGETHER)]
        sizes = [counts[step * TOGETHER + n] for n in range(TOGETHER)]
        for count in range(1, WB + 2):
            pl.when(sizes[-1] == count)(functools.partial(work, count, members, sizes))
        return carry

    lax.fori_loop(0, blocks // TOGETHER, one_step, 0)
    for j in range(blocks):
        early = slice(j * BLOCK, (j + 1) * BLOCK)
        halo_slabs[j, :, :HEAD] = (dk[early, :] * SCALE).astype(halo_slabs.dtype)
        halo_slabs[j, :, HEAD:] = dv[early, :].astype(halo_slabs.dtype)
        halo_copy(j).start()
    for j in range(blocks):
        late = slice(WINDOW + j * BLOCK, WINDOW + (j + 1) * BLOCK)
        dkv_own_ref[j, :, :HEAD] = dk[late, :] * SCALE
        dkv_own_ref[j, :, HEAD:] = dv[late, :]
    for i in range(blocks):
        dq_copy(i).wait()
    for j in range(blocks):
        halo_copy(j).wait()


def attend(chunk_index, doc_ids, band, queries_grads, own, halo):
    blocks = own.shape[0]
    total = WINDOW + blocks * BLOCK
    smem = pl.BlockSpec(memory_space=pltpu.SMEM)
    vmem = pl.BlockSpec(memory_space=pltpu.VMEM)
    hbm = pl.BlockSpec(memory_space=pl.ANY)
    order, counts, keys_t = prepare(chunk_index, doc_ids, band, own)
    dq = jax.ShapeDtypeStruct((blocks, BLOCK, queries_grads.shape[2] // 2), jnp.bfloat16)
    return pl.pallas_call(
        attend_kernel,
        in_specs=[smem] * 2 + [vmem] * 4,
        out_specs=[hbm, vmem, hbm],
        out_shape=[
            dq,
            jax.ShapeDtypeStruct(own.shape, jnp.float32),
            jax.ShapeDtypeStruct(own.shape, jnp.bfloat16),
        ],
        scratch_shapes=[
            pltpu.VMEM((total, 2 * HEAD), jnp.bfloat16),
            pltpu.VMEM((HEAD, total), jnp.bfloat16),
            pltpu.VMEM((total, HEAD), jnp.float32),
            pltpu.VMEM((total, HEAD), jnp.float32),
            pltpu.VMEM(dq.shape, dq.dtype),
            pltpu.VMEM(own.shape, jnp.bfloat16),
            pltpu.SemaphoreType.DMA((blocks,)),
            pltpu.SemaphoreType.DMA((blocks,)),
        ],
        compiler_params=pltpu.CompilerParams(vmem_limit_bytes=40 * 1024 * 1024),
    )(order, counts, queries_grads, own, keys_t, halo)


def add_kernel(own_ref, spill_ref, out_ref, slabs, sems):
    copies = []
    for j in range(out_ref.shape[0]):
        slabs[j] = (own_ref[j] + spill_ref[j].astype(jnp.float32)).astype(slabs.dtype)
        copies.append(pltpu.make_async_copy(slabs.at[j], out_ref.at[j], sems.at[j]))
        copies[j].start()
    for copy in copies:
        copy.wait()


def add_spill(own, spill):
    return pl.pallas_call(
        add_kernel,
        in_specs=[pl.BlockSpec(memory_space=pltpu.VMEM)] * 2,
        out_specs=pl.BlockSpec(memory_space=pl.ANY),
        out_shape=jax.ShapeDtypeStruct(spill.shape, spill.dtype),
        scratch_shapes=[
            pltpu.VMEM(spill.shape, spill.dtype),
            pltpu.SemaphoreType.DMA((spill.shape[0],)),
        ],
        compiler_params=pltpu.CompilerParams(vmem_limit_bytes=SMALL),
    )(own, spill)


def per_device(queries, keys, values, upstream, doc_ids, band):
    tokens = queries.shape[0]
    parts = WINDOW // tokens
    cores = lax.axis_size("heads")
    spans = lax.axis_size("blk")
    step = parts // cores
    axes = ("blk", "heads")
    groups = [
        [first * parts + member for member in range(parts)] for first in range(spans // step)
    ]

    def exchange(value):
        return lax.all_to_all(
            value, axes, split_axis=0, concat_axis=0, axis_index_groups=groups, tiled=True
        )

    kv = exchange(pack(keys, values, parts))
    halo = lax.ppermute(kv, "blk", [(s, s + step) for s in range(spans - step)])
    qd = exchange(pack(queries, upstream, parts))
    chunk_index = (lax.axis_index("blk") // step).astype(jnp.int32).reshape(1)
    dq, dkv_own, dkv_halo = attend(chunk_index, doc_ids, band, qd, kv, halo)
    spill = lax.ppermute(dkv_halo, "blk", [(s + step, s) for s in range(spans - step)])
    query_out = exchange(dq)
    dkv = exchange(add_spill(dkv_own, spill))

    return (*unpack(query_out, 1), *unpack(dkv, 2))


def solution(mesh):
    sharded = P(("groups", "blk", "heads"), None)
    return jax.shard_map(
        per_device,
        mesh=mesh,
        in_specs=(sharded,) * 4 + (P("groups"),) * 2,
        out_specs=(sharded,) * 3,
        check_vma=False,
    )
```

```python
import functools
import math

import jax
import jax.numpy as jnp
from jax import lax
from jax.experimental import pallas as pl
from jax.experimental.pallas import tpu as pltpu
from jax.sharding import PartitionSpec as P

HEAD = 128
SCALAR = 168
WINDOW = 1024
BLOCK = 128
WB = WINDOW // BLOCK
SCALE = SCALAR ** (-0.5)
LOG2E = math.log2(math.e)
SMALL = 8 * 1024 * 1024
TOGETHER = 2
PIECE = 32

NT = (((1,), (1,)), ((), ()))
NN = (((1,), (0,)), ((), ()))


def dot(a, b, dims):
    return lax.dot_general(a, b, dims, preferred_element_type=jnp.float32)


def run_copies(pairs, sems):
    copies = [pltpu.make_async_copy(x, y, sems.at[n]) for n, (x, y) in enumerate(pairs)]
    for copy in copies:
        copy.start()
    for copy in copies:
        copy.wait()


def pack_kernel(a_ref, b_ref, out_ref, slabs, in_sems, out_sems):
    heads = out_ref.shape[0]
    width = out_ref.shape[2] // 2
    reads = [
        [
            pltpu.make_async_copy(
                ref.at[:, pl.ds(h * width, width)],
                slabs.at[h, :, pl.ds(n * width, width)],
                in_sems.at[2 * h + n],
            )
            for n, ref in enumerate((a_ref, b_ref))
        ]
        for h in range(heads)
    ]
    writes = [
        pltpu.make_async_copy(slabs.at[h], out_ref.at[h], out_sems.at[h]) for h in range(heads)
    ]
    for pair in reads:
        for copy in pair:
            copy.start()
    for pair, write in zip(reads, writes):
        for copy in pair:
            copy.wait()
        write.start()
    for write in writes:
        write.wait()


def pack(a, b, heads):
    tokens, cols = a.shape
    hbm = pl.BlockSpec(memory_space=pl.ANY)
    shape = (heads, tokens, 2 * cols // heads)
    return pl.pallas_call(
        pack_kernel,
        in_specs=[hbm] * 2,
        out_specs=hbm,
        out_shape=jax.ShapeDtypeStruct(shape, a.dtype),
        scratch_shapes=[
            pltpu.VMEM(shape, a.dtype),
            pltpu.SemaphoreType.DMA((2 * heads,)),
            pltpu.SemaphoreType.DMA((heads,)),
        ],
    )(a, b)


def unpack_kernel(in_ref, *refs):
    out_refs, sems = refs[:-1], refs[-1]
    width = in_ref.shape[2] // len(out_refs)
    run_copies(
        [
            (in_ref.at[h, :, pl.ds(n * width, width)], ref.at[:, pl.ds(h * width, width)])
            for h in range(in_ref.shape[0])
            for n, ref in enumerate(out_refs)
        ],
        sems,
    )


def unpack(value, outputs):
    heads, tokens, width = value.shape
    shape = jax.ShapeDtypeStruct((tokens, heads * width // outputs), value.dtype)
    return pl.pallas_call(
        unpack_kernel,
        in_specs=[pl.BlockSpec(memory_space=pltpu.VMEM)],
        out_specs=[pl.BlockSpec(memory_space=pl.ANY)] * outputs,
        out_shape=[shape] * outputs,
        scratch_shapes=[pltpu.SemaphoreType.DMA((outputs * heads,))],
        compiler_params=pltpu.CompilerParams(vmem_limit_bytes=SMALL),
    )(value)


def prepare_kernel(chunk_ref, doc_ref, band_ref, own_ref, order, counts, keys_t_ref):
    blocks = own_ref.shape[0]
    for j in range(blocks):
        keys_t_ref[:, j * BLOCK : (j + 1) * BLOCK] = own_ref[j, :, :HEAD].T
    first = chunk_ref[0] * blocks
    length = jnp.int32(0)
    for back in range(1, WB + 1):
        same = (first >= back) & (doc_ref[jnp.maximum(first - back, 0)] == doc_ref[first])
        length = length + same.astype(jnp.int32)
    seen = []
    for i in range(blocks):
        if i > 0:
            same = doc_ref[first + i] == doc_ref[first + i - 1]
            length = jnp.where(same, length + 1, 0)
        seen.append(jnp.minimum(band_ref[first + i], length) + 1)
    for i in range(blocks):
        rank = jnp.int32(0)
        for j in range(blocks):
            if j != i:
                below = seen[j] <= seen[i] if j < i else seen[j] < seen[i]
                rank = rank + below.astype(jnp.int32)
        order[rank] = i
        counts[rank] = seen[i]


def prepare(chunk_index, doc_ids, band, own):
    blocks = own.shape[0]
    smem = pl.BlockSpec(memory_space=pltpu.SMEM)
    vmem = pl.BlockSpec(memory_space=pltpu.VMEM)
    return pl.pallas_call(
        prepare_kernel,
        in_specs=[smem] * 3 + [vmem],
        out_specs=[smem] * 2 + [vmem],
        out_shape=[jax.ShapeDtypeStruct((blocks,), jnp.int32)] * 2
        + [jax.ShapeDtypeStruct((HEAD, blocks * BLOCK), own.dtype)],
        compiler_params=pltpu.CompilerParams(vmem_limit_bytes=SMALL),
    )(chunk_index, doc_ids, band, own)


def attend_kernel(
    order, counts, qd_ref, own_ref, keys_t_ref, halo_ref,
    dq_ref, dkv_own_ref, dkv_halo_ref,
    kv, keys_t, dk, dv, dq_slabs, halo_slabs, dq_sems, halo_sems,
):
    blocks = own_ref.shape[0]
    q_heads = qd_ref.shape[2] // (2 * HEAD)
    for j in range(blocks):
        early = slice(j * BLOCK, (j + 1) * BLOCK)
        late = slice(WINDOW + j * BLOCK, WINDOW + (j + 1) * BLOCK)
        kv[early, :] = halo_ref[j]
        kv[late, :] = own_ref[j]
        keys_t[:, early] = halo_ref[j, :, :HEAD].T
        keys_t[:, late] = keys_t_ref[:, early]
    dk[...] = jnp.zeros_like(dk)
    dv[...] = jnp.zeros_like(dv)

    def dq_copy(i):
        return pltpu.make_async_copy(dq_slabs.at[i], dq_ref.at[i], dq_sems.at[i])

    def halo_copy(j):
        return pltpu.make_async_copy(halo_slabs.at[j], dkv_halo_ref.at[j], halo_sems.at[j])

    rows = q_heads * BLOCK

    def stacked(i, offset):
        return jnp.concatenate(
            [qd_ref[i, :, (offset + h) * HEAD : (offset + h + 1) * HEAD] for h in range(q_heads)],
            axis=0,
        )

    def work(count, members, sizes):
        span = count * BLOCK
        windows = [
            pl.ds(pl.multiple_of((i + WB + 1 - count) * BLOCK, BLOCK), span) for i in members
        ]
        lanes = range(len(members))

        pieces = [slice(r, r + PIECE) for r in range(0, span, PIECE)]
        block_of = [p.start // BLOCK for p in pieces]

        def fold(x, reduce):
            return reduce(x.reshape(PIECE // 8, 8, rows), axis=0)

        query = [stacked(i, 0) for i in members]
        grad = [stacked(i, q_heads) for i in members]
        both = []
        for n in lanes:
            blank = jnp.zeros_like(query[n])
            weights = jnp.concatenate(
                [
                    jnp.concatenate([query[n], blank], axis=1),
                    jnp.concatenate([blank, grad[n]], axis=1),
                ],
                axis=0,
            )
            both.append(dot(kv[windows[n], :], weights, NT))
        key_pos = lax.broadcasted_iota(jnp.int32, (PIECE, rows), 0)
        query_pos = lax.broadcasted_iota(jnp.int32, (PIECE, rows), 1) % BLOCK
        expo, inverse, probs_b, dscore = {}, {}, {}, {}
        for n in lanes:
            scores = [both[n][p, :rows] for p in pieces]
            for m, p in enumerate(pieces):
                if block_of[m] == count - 1:
                    causal = key_pos + (p.start - (count - 1) * BLOCK) <= query_pos
                    scores[m] = jnp.where(causal, scores[m], -jnp.inf)
            seen = [count - b <= sizes[n] for b in range(count)]
            tops = [None] * count
            for m, x in enumerate(scores):
                high = fold(x, jnp.max)
                b = block_of[m]
                tops[b] = high if tops[b] is None else jnp.maximum(tops[b], high)
            tops = [jnp.where(seen[b], x, -jnp.inf) for b, x in enumerate(tops)]
            top = jnp.max(functools.reduce(jnp.maximum, tops), axis=0, keepdims=True)
            shift = [jnp.where(seen[b], top, jnp.inf) for b in range(count)]
            expo[n] = []
            total = jnp.zeros((8, rows), jnp.float32)
            for m, x in enumerate(scores):
                x = jnp.exp2((x - shift[block_of[m]]) * (SCALE * LOG2E))
                total = total + fold(x, jnp.sum)
                expo[n].append(x)
            inverse[n] = 1.0 / jnp.sum(total, axis=0, keepdims=True)
        for n in lanes:
            probs_b[n] = []
            delta = jnp.zeros((8, rows), jnp.float32)
            for p, x in zip(pieces, expo[n]):
                x = (x * inverse[n]).astype(jnp.bfloat16)
                delta = delta + fold(x.astype(jnp.float32) * both[n][p, rows:], jnp.sum)
                probs_b[n].append(x)
            dv[windows[n], :] += dot(jnp.concatenate(probs_b[n], axis=0), grad[n], NN)
            delta = jnp.sum(delta, axis=0, keepdims=True)
            dscore[n] = jnp.concatenate(
                [
                    (x * ((both[n][p, rows:] - delta) * inverse[n])).astype(jnp.bfloat16)
                    for p, x in zip(pieces, expo[n])
                ],
                axis=0,
            )
        for n, i in enumerate(members):
            dk[windows[n], :] += dot(dscore[n], query[n], NN)
            query_grad = dot(keys_t[:, windows[n]], dscore[n], NN) * SCALE
            for h in range(q_heads):
                dq_slabs[i, :, h * HEAD : (h + 1) * HEAD] = query_grad[
                    :, h * BLOCK : (h + 1) * BLOCK
                ].T.astype(dq_ref.dtype)
            dq_copy(i).start()

    def one_step(step, carry):
        members = [order[step * TOGETHER + n] for n in range(TOGETHER)]
        sizes = [counts[step * TOGETHER + n] for n in range(TOGETHER)]
        for count in range(1, WB + 2):
            pl.when(sizes[-1] == count)(functools.partial(work, count, members, sizes))
        return carry

    lax.fori_loop(0, blocks // TOGETHER, one_step, 0)
    for j in range(blocks):
        early = slice(j * BLOCK, (j + 1) * BLOCK)
        halo_slabs[j, :, :HEAD] = (dk[early, :] * SCALE).astype(halo_slabs.dtype)
        halo_slabs[j, :, HEAD:] = dv[early, :].astype(halo_slabs.dtype)
        halo_copy(j).start()
    for j in range(blocks):
        late = slice(WINDOW + j * BLOCK, WINDOW + (j + 1) * BLOCK)
        dkv_own_ref[j, :, :HEAD] = dk[late, :] * SCALE
        dkv_own_ref[j, :, HEAD:] = dv[late, :]
    for i in range(blocks):
        dq_copy(i).wait()
    for j in range(blocks):
        halo_copy(j).wait()


def attend(chunk_index, doc_ids, band, queries_grads, own, halo):
    blocks = own.shape[0]
    total = WINDOW + blocks * BLOCK
    smem = pl.BlockSpec(memory_space=pltpu.SMEM)
    vmem = pl.BlockSpec(memory_space=pltpu.VMEM)
    hbm = pl.BlockSpec(memory_space=pl.ANY)
    order, counts, keys_t = prepare(chunk_index, doc_ids, band, own)
    dq = jax.ShapeDtypeStruct((blocks, BLOCK, queries_grads.shape[2] // 2), jnp.bfloat16)
    return pl.pallas_call(
        attend_kernel,
        in_specs=[smem] * 2 + [vmem] * 4,
        out_specs=[hbm, vmem, hbm],
        out_shape=[
            dq,
            jax.ShapeDtypeStruct(own.shape, jnp.float32),
            jax.ShapeDtypeStruct(own.shape, jnp.bfloat16),
        ],
        scratch_shapes=[
            pltpu.VMEM((total, 2 * HEAD), jnp.bfloat16),
            pltpu.VMEM((HEAD, total), jnp.bfloat16),
            pltpu.VMEM((total, HEAD), jnp.float32),
            pltpu.VMEM((total, HEAD), jnp.float32),
            pltpu.VMEM(dq.shape, dq.dtype),
            pltpu.VMEM(own.shape, jnp.bfloat16),
            pltpu.SemaphoreType.DMA((blocks,)),
            pltpu.SemaphoreType.DMA((blocks,)),
        ],
        compiler_params=pltpu.CompilerParams(vmem_limit_bytes=40 * 1024 * 1024),
    )(order, counts, queries_grads, own, keys_t, halo)


def add_kernel(own_ref, spill_ref, out_ref, slabs, sems):
    copies = []
    for j in range(out_ref.shape[0]):
        slabs[j] = (own_ref[j] + spill_ref[j].astype(jnp.float32)).astype(slabs.dtype)
        copies.append(pltpu.make_async_copy(slabs.at[j], out_ref.at[j], sems.at[j]))
        copies[j].start()
    for copy in copies:
        copy.wait()


def add_spill(own, spill):
    return pl.pallas_call(
        add_kernel,
        in_specs=[pl.BlockSpec(memory_space=pltpu.VMEM)] * 2,
        out_specs=pl.BlockSpec(memory_space=pl.ANY),
        out_shape=jax.ShapeDtypeStruct(spill.shape, spill.dtype),
        scratch_shapes=[
            pltpu.VMEM(spill.shape, spill.dtype),
            pltpu.SemaphoreType.DMA((spill.shape[0],)),
        ],
        compiler_params=pltpu.CompilerParams(vmem_limit_bytes=SMALL),
    )(own, spill)


def per_device(queries, keys, values, upstream, doc_ids, band):
    tokens = queries.shape[0]
    parts = WINDOW // tokens
    cores = lax.axis_size("heads")
    spans = lax.axis_size("blk")
    step = parts // cores
    axes = ("blk", "heads")
    groups = [
        [first * parts + member for member in range(parts)] for first in range(spans // step)
    ]

    def exchange(value):
        return lax.all_to_all(
            value, axes, split_axis=0, concat_axis=0, axis_index_groups=groups, tiled=True
        )

    kv = exchange(pack(keys, values, parts))
    halo = lax.ppermute(kv, "blk", [(s, s + step) for s in range(spans - step)])
    qd = exchange(pack(queries, upstream, parts))
    chunk_index = (lax.axis_index("blk") // step).astype(jnp.int32).reshape(1)
    dq, dkv_own, dkv_halo = attend(chunk_index, doc_ids, band, qd, kv, halo)
    spill = lax.ppermute(dkv_halo, "blk", [(s + step, s) for s in range(spans - step)])
    query_out = exchange(dq)
    dkv = exchange(add_spill(dkv_own, spill))

    return (*unpack(query_out, 1), *unpack(dkv, 2))


def solution(mesh):
    sharded = P(("groups", "blk", "heads"), None)
    return jax.shard_map(
        per_device,
        mesh=mesh,
        in_specs=(sharded,) * 4 + (P("groups"),) * 2,
        out_specs=(sharded,) * 3,
        check_vma=False,
    )
```

```python
import functools
import math

import jax
import jax.numpy as jnp
from jax import lax
from jax.experimental import pallas as pl
from jax.experimental.pallas import tpu as pltpu
from jax.sharding import PartitionSpec as P

HEAD = 128
SCALAR = 168
WINDOW = 1024
BLOCK = 128
WB = WINDOW // BLOCK
SCALE = SCALAR ** (-0.5)
LOG2E = math.log2(math.e)
SMALL = 8 * 1024 * 1024
LARGE = 40 * 1024 * 1024
TOGETHER = 2

NT = (((1,), (1,)), ((), ()))
NN = (((1,), (0,)), ((), ()))


def dot(a, b, dims):
    return lax.dot_general(a, b, dims, preferred_element_type=jnp.float32)


def run_copies(pairs, sems):
    copies = [pltpu.make_async_copy(x, y, sems.at[n]) for n, (x, y) in enumerate(pairs)]
    for copy in copies:
        copy.start()
    for copy in copies:
        copy.wait()


def pack_kernel(a_ref, b_ref, out_ref, slabs, in_sems, out_sems):
    heads = out_ref.shape[0]
    width = out_ref.shape[2] // 2
    reads = [
        [
            pltpu.make_async_copy(
                ref.at[:, pl.ds(h * width, width)],
                slabs.at[h, :, pl.ds(n * width, width)],
                in_sems.at[2 * h + n],
            )
            for n, ref in enumerate((a_ref, b_ref))
        ]
        for h in range(heads)
    ]
    writes = [
        pltpu.make_async_copy(slabs.at[h], out_ref.at[h], out_sems.at[h]) for h in range(heads)
    ]
    for pair in reads:
        for copy in pair:
            copy.start()
    for pair, write in zip(reads, writes):
        for copy in pair:
            copy.wait()
        write.start()
    for write in writes:
        write.wait()


def pack(a, b, heads):
    tokens, cols = a.shape
    hbm = pl.BlockSpec(memory_space=pl.ANY)
    shape = (heads, tokens, 2 * cols // heads)
    return pl.pallas_call(
        pack_kernel,
        in_specs=[hbm] * 2,
        out_specs=hbm,
        out_shape=jax.ShapeDtypeStruct(shape, a.dtype),
        scratch_shapes=[
            pltpu.VMEM(shape, a.dtype),
            pltpu.SemaphoreType.DMA((2 * heads,)),
            pltpu.SemaphoreType.DMA((heads,)),
        ],
    )(a, b)


def unpack_kernel(in_ref, *refs):
    out_refs, sems = refs[:-1], refs[-1]
    width = in_ref.shape[2] // len(out_refs)
    run_copies(
        [
            (in_ref.at[h, :, pl.ds(n * width, width)], ref.at[:, pl.ds(h * width, width)])
            for h in range(in_ref.shape[0])
            for n, ref in enumerate(out_refs)
        ],
        sems,
    )


def unpack(value, outputs):
    heads, tokens, width = value.shape
    shape = jax.ShapeDtypeStruct((tokens, heads * width // outputs), value.dtype)
    return pl.pallas_call(
        unpack_kernel,
        in_specs=[pl.BlockSpec(memory_space=pltpu.VMEM)],
        out_specs=[pl.BlockSpec(memory_space=pl.ANY)] * outputs,
        out_shape=[shape] * outputs,
        scratch_shapes=[pltpu.SemaphoreType.DMA((outputs * heads,))],
        compiler_params=pltpu.CompilerParams(vmem_limit_bytes=SMALL),
    )(value)


def prepare_kernel(chunk_ref, doc_ref, band_ref, own_ref, order, counts, own_t_ref):
    blocks = own_ref.shape[0]
    for j in range(blocks):
        own_t_ref[:, j * BLOCK : (j + 1) * BLOCK] = own_ref[j, :, :HEAD].T
    first = chunk_ref[0] * blocks
    length = jnp.int32(0)
    for back in range(1, WB + 1):
        same = (first >= back) & (doc_ref[jnp.maximum(first - back, 0)] == doc_ref[first])
        length = length + same.astype(jnp.int32)
    seen = []
    for i in range(blocks):
        if i > 0:
            same = doc_ref[first + i] == doc_ref[first + i - 1]
            length = jnp.where(same, length + 1, 0)
        seen.append(jnp.minimum(band_ref[first + i], length) + 1)
    far = [(seen[i] > i + 1).astype(jnp.int32) for i in range(blocks)]
    place = [seen[i] + 2 * WB * far[i] for i in range(blocks)]
    for i in range(blocks):
        rank = jnp.int32(0)
        for j in range(blocks):
            if j != i:
                below = place[j] <= place[i] if j < i else place[j] < place[i]
                rank = rank + below.astype(jnp.int32)
        order[rank] = i
        counts[rank] = seen[i]
    near = blocks - functools.reduce(jnp.add, far)
    counts[blocks] = near // TOGETHER
    counts[blocks + 1] = functools.reduce(
        jnp.minimum, [jnp.minimum(i + WB + 1 - seen[i], WB) for i in range(blocks)]
    )


def prepare(chunk_index, doc_ids, band, own):
    blocks = own.shape[0]
    smem = pl.BlockSpec(memory_space=pltpu.SMEM)
    vmem = pl.BlockSpec(memory_space=pltpu.VMEM)
    return pl.pallas_call(
        prepare_kernel,
        in_specs=[smem] * 3 + [vmem],
        out_specs=[smem] * 2 + [vmem],
        out_shape=[
            jax.ShapeDtypeStruct((blocks,), jnp.int32),
            jax.ShapeDtypeStruct((blocks + 2,), jnp.int32),
            jax.ShapeDtypeStruct((HEAD, blocks * BLOCK), own.dtype),
        ],
        compiler_params=pltpu.CompilerParams(vmem_limit_bytes=SMALL),
    )(chunk_index, doc_ids, band, own)


def place_own(own_ref, own_t_ref, kv, keys_t):
    for j in range(own_ref.shape[0]):
        late = slice(WINDOW + j * BLOCK, WINDOW + (j + 1) * BLOCK)
        kv[late, :] = own_ref[j]
        keys_t[:, late] = own_t_ref[:, j * BLOCK : (j + 1) * BLOCK]


def near_kernel(order, counts, qd_ref, own_ref, own_t_ref, dq_ref, sums_ref, kv, keys_t, sums):
    kv[:WINDOW, :] = jnp.zeros((WINDOW, 2 * HEAD), kv.dtype)
    keys_t[:, :WINDOW] = jnp.zeros((HEAD, WINDOW), keys_t.dtype)
    place_own(own_ref, own_t_ref, kv, keys_t)
    sums[...] = jnp.zeros_like(sums)
    last = counts[order.shape[0]]
    attend(0, last, order, counts, qd_ref, kv, keys_t, dq_ref, sums, lambda i: None)
    sums_ref[...] = sums[WINDOW:, :]


def far_kernel(
    order, counts, qd_ref, own_ref, own_t_ref, halo_ref, dq_near_ref, sums_near_ref, room_ref,
    dq_ref, sums_ref, spill_ref, kv, keys_t, sums, dq_slabs, spill_slabs, dq_sems, spill_sems,
):
    del room_ref
    sums[:WINDOW, :] = jnp.zeros((WINDOW, 2 * HEAD), sums.dtype)
    sums[WINDOW:, :] = sums_near_ref[...]
    blocks = order.shape[0]
    steps = counts[blocks]

    def dq_copy(slabs, i):
        return pltpu.make_async_copy(slabs.at[i], dq_ref.at[i], dq_sems.at[i])

    def pass_on(m, carry):
        dq_copy(dq_near_ref, order[m]).start()
        return carry

    def fill(j, carry):
        rows = pl.ds(pl.multiple_of(j * BLOCK, BLOCK), BLOCK)
        kv[rows, :] = halo_ref[j]
        keys_t[:, rows] = halo_ref[j, :, :HEAD].T
        return carry

    def blank(j, carry):
        rows = pl.ds(pl.multiple_of(j * BLOCK, BLOCK), BLOCK)
        kv[rows, :] = jnp.zeros((BLOCK, 2 * HEAD), kv.dtype)
        keys_t[:, rows] = jnp.zeros((HEAD, BLOCK), keys_t.dtype)
        return carry

    lax.fori_loop(0, steps * TOGETHER, pass_on, 0)
    lax.fori_loop(0, counts[blocks + 1], blank, 0)
    lax.fori_loop(counts[blocks + 1], WB, fill, 0)
    place_own(own_ref, own_t_ref, kv, keys_t)
    attend(
        steps, blocks // TOGETHER, order, counts, qd_ref, kv, keys_t, dq_slabs, sums,
        lambda i: dq_copy(dq_slabs, i).start(),
    )
    copies = []
    for j in range(WB):
        rows = slice(j * BLOCK, (j + 1) * BLOCK)
        spill_slabs[j, :, :HEAD] = (sums[rows, :HEAD] * SCALE).astype(spill_slabs.dtype)
        spill_slabs[j, :, HEAD:] = sums[rows, HEAD:].astype(spill_slabs.dtype)
        copies.append(
            pltpu.make_async_copy(spill_slabs.at[j], spill_ref.at[j], spill_sems.at[j])
        )
        copies[j].start()
    sums_ref[...] = sums[WINDOW:, :]
    for i in range(blocks):
        dq_copy(dq_slabs, i).wait()
    for copy in copies:
        copy.wait()


def attend(first_step, last_step, order, counts, qd_ref, kv, keys_t, dq_slabs, sums, ready):
    q_heads = qd_ref.shape[2] // (2 * HEAD)
    rows = q_heads * BLOCK

    def stacked(i, offset):
        return jnp.concatenate(
            [qd_ref[i, :, (offset + h) * HEAD : (offset + h + 1) * HEAD] for h in range(q_heads)],
            axis=0,
        )

    def fold(x, reduce):
        return reduce(x.reshape(BLOCK // 8, 8, rows), axis=0)

    def work(count, members, sizes):
        span = count * BLOCK
        windows = [
            pl.ds(pl.multiple_of((i + WB + 1 - count) * BLOCK, BLOCK), span) for i in members
        ]
        lanes = range(len(members))

        def split(x):
            return [x[b * BLOCK : (b + 1) * BLOCK] for b in range(count)]

        query = [stacked(i, 0) for i in members]
        grad = [stacked(i, q_heads) for i in members]
        scores = [split(dot(kv[windows[n], :HEAD], query[n], NT)) for n in lanes]
        key_pos = lax.broadcasted_iota(jnp.int32, (BLOCK, rows), 0)
        query_pos = lax.broadcasted_iota(jnp.int32, (BLOCK, rows), 1) % BLOCK
        causal = key_pos <= query_pos
        probs, probs_b, dprob = {}, {}, {}
        for n in lanes:
            scores[n][-1] = jnp.where(causal, scores[n][-1], -jnp.inf)
            seen = [count - b <= sizes[n] for b in range(count)]
            tops = [
                jnp.where(seen[b], fold(x, jnp.max), -jnp.inf) for b, x in enumerate(scores[n])
            ]
            top = jnp.max(functools.reduce(jnp.maximum, tops), axis=0, keepdims=True)
            shift = [jnp.where(seen[b], top, jnp.inf) for b in range(count)]
            dprob[n] = split(dot(kv[windows[n], HEAD:], grad[n], NT))
            expo = [jnp.exp2((x - y) * (SCALE * LOG2E)) for x, y in zip(scores[n], shift)]
            total = functools.reduce(jnp.add, [fold(x, jnp.sum) for x in expo])
            inverse = 1.0 / jnp.sum(total, axis=0, keepdims=True)
            probs[n] = [x * inverse for x in expo]
            probs_b[n] = [x.astype(jnp.bfloat16) for x in probs[n]]
        dscore = {}
        for n in lanes:
            sums[windows[n], HEAD:] += dot(jnp.concatenate(probs_b[n], axis=0), grad[n], NN)
            delta = functools.reduce(
                jnp.add,
                [
                    fold(x.astype(jnp.float32) * y, jnp.sum)
                    for x, y in zip(probs_b[n], dprob[n])
                ],
            )
            delta = jnp.sum(delta, axis=0, keepdims=True)
            dscore[n] = jnp.concatenate(
                [
                    (x * (y - delta)).astype(jnp.bfloat16)
                    for x, y in zip(probs[n], dprob[n])
                ],
                axis=0,
            )
        for n, i in enumerate(members):
            sums[windows[n], :HEAD] += dot(dscore[n], query[n], NN)
            query_grad = dot(keys_t[:, windows[n]], dscore[n], NN) * SCALE
            for h in range(q_heads):
                dq_slabs[i, :, h * HEAD : (h + 1) * HEAD] = query_grad[
                    :, h * BLOCK : (h + 1) * BLOCK
                ].T.astype(dq_slabs.dtype)
            ready(i)

    def one_step(step, carry):
        members = [order[step * TOGETHER + n] for n in range(TOGETHER)]
        sizes = [counts[step * TOGETHER + n] for n in range(TOGETHER)]
        widest = functools.reduce(jnp.maximum, sizes)
        for count in range(1, WB + 2):
            pl.when(widest == count)(functools.partial(work, count, members, sizes))
        return carry

    lax.fori_loop(first_step, last_step, one_step, 0)


def attend_near(order, counts, qd, own, own_t):
    total = WINDOW + own_t.shape[1]
    smem = pl.BlockSpec(memory_space=pltpu.SMEM)
    vmem = pl.BlockSpec(memory_space=pltpu.VMEM)
    return pl.pallas_call(
        near_kernel,
        in_specs=[smem] * 2 + [vmem] * 3,
        out_specs=[vmem] * 2,
        out_shape=[
            jax.ShapeDtypeStruct((*qd.shape[:2], qd.shape[2] // 2), qd.dtype),
            jax.ShapeDtypeStruct((own_t.shape[1], 2 * HEAD), jnp.float32),
        ],
        scratch_shapes=[
            pltpu.VMEM((total, 2 * HEAD), own.dtype),
            pltpu.VMEM((HEAD, total), own.dtype),
            pltpu.VMEM((total, 2 * HEAD), jnp.float32),
        ],
        compiler_params=pltpu.CompilerParams(vmem_limit_bytes=LARGE),
    )(order, counts, qd, own, own_t)


def attend_far(order, counts, qd, own, own_t, halo, dq, sums, room):
    total = WINDOW + own_t.shape[1]
    smem = pl.BlockSpec(memory_space=pltpu.SMEM)
    vmem = pl.BlockSpec(memory_space=pltpu.VMEM)
    hbm = pl.BlockSpec(memory_space=pl.ANY)
    return pl.pallas_call(
        far_kernel,
        in_specs=[smem] * 2 + [vmem] * 6 + [hbm],
        out_specs=[hbm, vmem, hbm],
        out_shape=[jax.ShapeDtypeStruct(x.shape, x.dtype) for x in (dq, sums, halo)],
        input_output_aliases={8: 0},
        scratch_shapes=[
            pltpu.VMEM((total, 2 * HEAD), own.dtype),
            pltpu.VMEM((HEAD, total), own.dtype),
            pltpu.VMEM((total, 2 * HEAD), jnp.float32),
            pltpu.VMEM(dq.shape, dq.dtype),
            pltpu.VMEM(halo.shape, halo.dtype),
            pltpu.SemaphoreType.DMA(dq.shape[:1]),
            pltpu.SemaphoreType.DMA(halo.shape[:1]),
        ],
        compiler_params=pltpu.CompilerParams(vmem_limit_bytes=LARGE),
    )(order, counts, qd, own, own_t, halo, dq, sums, room)


def add_kernel(sums_ref, spill_ref, out_ref, slabs, sems):
    copies = []
    for j in range(out_ref.shape[0]):
        late = slice(j * BLOCK, (j + 1) * BLOCK)
        for half, scale in ((slice(0, HEAD), SCALE), (slice(HEAD, 2 * HEAD), 1.0)):
            own = sums_ref[late, half] * scale
            slabs[j, :, half] = (own + spill_ref[j, :, half].astype(jnp.float32)).astype(
                slabs.dtype
            )
        copies.append(pltpu.make_async_copy(slabs.at[j], out_ref.at[j], sems.at[j]))
        copies[j].start()
    for copy in copies:
        copy.wait()


def add_spill(sums, spill):
    return pl.pallas_call(
        add_kernel,
        in_specs=[pl.BlockSpec(memory_space=pltpu.VMEM)] * 2,
        out_specs=pl.BlockSpec(memory_space=pl.ANY),
        out_shape=jax.ShapeDtypeStruct(spill.shape, spill.dtype),
        scratch_shapes=[
            pltpu.VMEM(spill.shape, spill.dtype),
            pltpu.SemaphoreType.DMA((spill.shape[0],)),
        ],
        compiler_params=pltpu.CompilerParams(vmem_limit_bytes=SMALL),
    )(sums, spill)


def per_device(queries, keys, values, upstream, doc_ids, band):
    tokens = queries.shape[0]
    parts = WINDOW // tokens
    cores = lax.axis_size("heads")
    spans = lax.axis_size("blk")
    step = parts // cores
    axes = ("blk", "heads")
    groups = [
        [first * parts + member for member in range(parts)] for first in range(spans // step)
    ]

    def exchange(value):
        return lax.all_to_all(
            value, axes, split_axis=0, concat_axis=0, axis_index_groups=groups, tiled=True
        )

    kv_packed = pack(keys, values, parts)
    kv = exchange(kv_packed)
    halo = lax.ppermute(kv, "blk", [(s, s + step) for s in range(spans - step)])
    qd = exchange(pack(queries, upstream, parts))
    chunk_index = (lax.axis_index("blk") // step).astype(jnp.int32).reshape(1)
    order, counts, own_t = prepare(chunk_index, doc_ids, band, kv)
    dq, sums = attend_near(order, counts, qd, kv, own_t)
    dq, sums, spill = attend_far(order, counts, qd, kv, own_t, halo, dq, sums, kv_packed)
    spill = lax.ppermute(spill, "blk", [(s + step, s) for s in range(spans - step)])
    query_out = exchange(dq)
    dkv = exchange(add_spill(sums, spill))

    return (*unpack(query_out, 1), *unpack(dkv, 2))


def solution(mesh):
    sharded = P(("groups", "blk", "heads"), None)
    return jax.shard_map(
        per_device,
        mesh=mesh,
        in_specs=(sharded,) * 4 + (P("groups"),) * 2,
        out_specs=(sharded,) * 3,
        check_vma=False,
    )
```

```python
import functools
import math

import jax
import jax.numpy as jnp
from jax import lax
from jax.experimental import pallas as pl
from jax.experimental.pallas import tpu as pltpu
from jax.sharding import PartitionSpec as P

HEAD = 128
SCALAR = 168
WINDOW = 1024
BLOCK = 128
WB = WINDOW // BLOCK
SCALE = SCALAR ** (-0.5)
LOG2E = math.log2(math.e)
SMALL = 8 * 1024 * 1024
LARGE = 40 * 1024 * 1024
TOGETHER = 2

NT = (((1,), (1,)), ((), ()))
NN = (((1,), (0,)), ((), ()))


def dot(a, b, dims):
    return lax.dot_general(a, b, dims, preferred_element_type=jnp.float32)


def run_copies(pairs, sems):
    copies = [pltpu.make_async_copy(x, y, sems.at[n]) for n, (x, y) in enumerate(pairs)]
    for copy in copies:
        copy.start()
    for copy in copies:
        copy.wait()


def pack_kernel(a_ref, b_ref, out_ref, slabs, in_sems, out_sems):
    heads = out_ref.shape[0]
    width = out_ref.shape[2] // 2
    reads = [
        [
            pltpu.make_async_copy(
                ref.at[:, pl.ds(h * width, width)],
                slabs.at[h, :, pl.ds(n * width, width)],
                in_sems.at[2 * h + n],
            )
            for n, ref in enumerate((a_ref, b_ref))
        ]
        for h in range(heads)
    ]
    writes = [
        pltpu.make_async_copy(slabs.at[h], out_ref.at[h], out_sems.at[h]) for h in range(heads)
    ]
    for pair in reads:
        for copy in pair:
            copy.start()
    for pair, write in zip(reads, writes):
        for copy in pair:
            copy.wait()
        write.start()
    for write in writes:
        write.wait()


def pack(a, b, heads):
    tokens, cols = a.shape
    hbm = pl.BlockSpec(memory_space=pl.ANY)
    shape = (heads, tokens, 2 * cols // heads)
    return pl.pallas_call(
        pack_kernel,
        in_specs=[hbm] * 2,
        out_specs=hbm,
        out_shape=jax.ShapeDtypeStruct(shape, a.dtype),
        scratch_shapes=[
            pltpu.VMEM(shape, a.dtype),
            pltpu.SemaphoreType.DMA((2 * heads,)),
            pltpu.SemaphoreType.DMA((heads,)),
        ],
    )(a, b)


def unpack_kernel(in_ref, *refs):
    out_refs, sems = refs[:-1], refs[-1]
    width = in_ref.shape[2] // len(out_refs)
    run_copies(
        [
            (in_ref.at[h, :, pl.ds(n * width, width)], ref.at[:, pl.ds(h * width, width)])
            for h in range(in_ref.shape[0])
            for n, ref in enumerate(out_refs)
        ],
        sems,
    )


def unpack(value, outputs):
    heads, tokens, width = value.shape
    shape = jax.ShapeDtypeStruct((tokens, heads * width // outputs), value.dtype)
    return pl.pallas_call(
        unpack_kernel,
        in_specs=[pl.BlockSpec(memory_space=pltpu.VMEM)],
        out_specs=[pl.BlockSpec(memory_space=pl.ANY)] * outputs,
        out_shape=[shape] * outputs,
        scratch_shapes=[pltpu.SemaphoreType.DMA((outputs * heads,))],
        compiler_params=pltpu.CompilerParams(vmem_limit_bytes=SMALL),
    )(value)


def prepare_kernel(chunk_ref, doc_ref, band_ref, own_ref, order, counts, own_t_ref):
    blocks = own_ref.shape[0]
    for j in range(blocks):
        own_t_ref[:, j * BLOCK : (j + 1) * BLOCK] = own_ref[j, :, :HEAD].T
    first = chunk_ref[0] * blocks
    length = jnp.int32(0)
    for back in range(1, WB + 1):
        same = (first >= back) & (doc_ref[jnp.maximum(first - back, 0)] == doc_ref[first])
        length = length + same.astype(jnp.int32)
    seen = []
    for i in range(blocks):
        if i > 0:
            same = doc_ref[first + i] == doc_ref[first + i - 1]
            length = jnp.where(same, length + 1, 0)
        seen.append(jnp.minimum(band_ref[first + i], length) + 1)
    far = [(seen[i] > i + 1).astype(jnp.int32) for i in range(blocks)]
    place = [seen[i] + 2 * WB * far[i] for i in range(blocks)]
    for i in range(blocks):
        rank = jnp.int32(0)
        for j in range(blocks):
            if j != i:
                below = place[j] <= place[i] if j < i else place[j] < place[i]
                rank = rank + below.astype(jnp.int32)
        order[rank] = i
        counts[rank] = seen[i]
    near = blocks - functools.reduce(jnp.add, far)
    counts[blocks] = near // TOGETHER
    counts[blocks + 1] = functools.reduce(
        jnp.minimum, [jnp.minimum(i + WB + 1 - seen[i], WB) for i in range(blocks)]
    )


def prepare(chunk_index, doc_ids, band, own):
    blocks = own.shape[0]
    smem = pl.BlockSpec(memory_space=pltpu.SMEM)
    vmem = pl.BlockSpec(memory_space=pltpu.VMEM)
    return pl.pallas_call(
        prepare_kernel,
        in_specs=[smem] * 3 + [vmem],
        out_specs=[smem] * 2 + [vmem],
        out_shape=[
            jax.ShapeDtypeStruct((blocks,), jnp.int32),
            jax.ShapeDtypeStruct((blocks + 2,), jnp.int32),
            jax.ShapeDtypeStruct((HEAD, blocks * BLOCK), own.dtype),
        ],
        compiler_params=pltpu.CompilerParams(vmem_limit_bytes=SMALL),
    )(chunk_index, doc_ids, band, own)


def place_own(own_ref, own_t_ref, kv, keys_t):
    for j in range(own_ref.shape[0]):
        late = slice(WINDOW + j * BLOCK, WINDOW + (j + 1) * BLOCK)
        kv[late, :] = own_ref[j]
        keys_t[:, late] = own_t_ref[:, j * BLOCK : (j + 1) * BLOCK]


def near_kernel(order, counts, qd_ref, own_ref, own_t_ref, dq_ref, sums, kv, keys_t):
    kv[:WINDOW, :] = jnp.zeros((WINDOW, 2 * HEAD), kv.dtype)
    keys_t[:, :WINDOW] = jnp.zeros((HEAD, WINDOW), keys_t.dtype)
    place_own(own_ref, own_t_ref, kv, keys_t)
    sums[...] = jnp.zeros_like(sums)
    last = counts[order.shape[0]]
    attend(0, last, order, counts, qd_ref, kv, keys_t, dq_ref, sums, lambda i: None)


def far_kernel(
    order, counts, qd_ref, own_ref, own_t_ref, halo_ref, dq_near_ref, sums_near_ref, room_ref,
    dq_ref, sums_ref, spill_ref, kv, keys_t, sums, dq_slabs, dq_sems,
):
    del room_ref
    sums[:WINDOW, :] = jnp.zeros((WINDOW, 2 * HEAD), sums.dtype)
    sums[WINDOW:, :] = sums_near_ref[WINDOW:, :]
    blocks = order.shape[0]
    steps = counts[blocks]

    def dq_copy(slabs, i):
        return pltpu.make_async_copy(slabs.at[i], dq_ref.at[i], dq_sems.at[i])

    def pass_on(m, carry):
        dq_copy(dq_near_ref, order[m]).start()
        return carry

    def fill(j, carry):
        rows = pl.ds(pl.multiple_of(j * BLOCK, BLOCK), BLOCK)
        kv[rows, :] = halo_ref[j]
        keys_t[:, rows] = halo_ref[j, :, :HEAD].T
        return carry

    def blank(j, carry):
        rows = pl.ds(pl.multiple_of(j * BLOCK, BLOCK), BLOCK)
        kv[rows, :] = jnp.zeros((BLOCK, 2 * HEAD), kv.dtype)
        keys_t[:, rows] = jnp.zeros((HEAD, BLOCK), keys_t.dtype)
        return carry

    lax.fori_loop(0, steps * TOGETHER, pass_on, 0)
    lax.fori_loop(0, counts[blocks + 1], blank, 0)
    lax.fori_loop(counts[blocks + 1], WB, fill, 0)
    place_own(own_ref, own_t_ref, kv, keys_t)
    attend(
        steps, blocks // TOGETHER, order, counts, qd_ref, kv, keys_t, dq_slabs, sums,
        lambda i: dq_copy(dq_slabs, i).start(),
    )
    for j in range(WB):
        rows = slice(j * BLOCK, (j + 1) * BLOCK)
        spill_ref[j, :, :HEAD] = (sums[rows, :HEAD] * SCALE).astype(spill_ref.dtype)
        spill_ref[j, :, HEAD:] = sums[rows, HEAD:].astype(spill_ref.dtype)
    sums_ref[...] = sums[WINDOW:, :]
    for i in range(blocks):
        dq_copy(dq_slabs, i).wait()


def attend(first_step, last_step, order, counts, qd_ref, kv, keys_t, dq_slabs, sums, ready):
    q_heads = qd_ref.shape[2] // (2 * HEAD)
    rows = q_heads * BLOCK

    def stacked(i, offset):
        return jnp.concatenate(
            [qd_ref[i, :, (offset + h) * HEAD : (offset + h + 1) * HEAD] for h in range(q_heads)],
            axis=0,
        )

    def fold(x, reduce):
        return reduce(x.reshape(BLOCK // 8, 8, rows), axis=0)

    def work(count, members, sizes):
        span = count * BLOCK
        windows = [
            pl.ds(pl.multiple_of((i + WB + 1 - count) * BLOCK, BLOCK), span) for i in members
        ]
        lanes = range(len(members))

        def split(x):
            return [x[b * BLOCK : (b + 1) * BLOCK] for b in range(count)]

        query = [stacked(i, 0) for i in members]
        grad = [stacked(i, q_heads) for i in members]
        scores = [split(dot(kv[windows[n], :HEAD], query[n], NT)) for n in lanes]
        key_pos = lax.broadcasted_iota(jnp.int32, (BLOCK, rows), 0)
        query_pos = lax.broadcasted_iota(jnp.int32, (BLOCK, rows), 1) % BLOCK
        causal = key_pos <= query_pos
        probs, probs_b, dprob = {}, {}, {}
        for n in lanes:
            scores[n][-1] = jnp.where(causal, scores[n][-1], -jnp.inf)
            seen = [count - b <= sizes[n] for b in range(count)]
            tops = [
                jnp.where(seen[b], fold(x, jnp.max), -jnp.inf) for b, x in enumerate(scores[n])
            ]
            top = jnp.max(functools.reduce(jnp.maximum, tops), axis=0, keepdims=True)
            shift = [jnp.where(seen[b], top, jnp.inf) for b in range(count)]
            dprob[n] = split(dot(kv[windows[n], HEAD:], grad[n], NT))
            expo = [jnp.exp2((x - y) * (SCALE * LOG2E)) for x, y in zip(scores[n], shift)]
            total = functools.reduce(jnp.add, [fold(x, jnp.sum) for x in expo])
            inverse = 1.0 / jnp.sum(total, axis=0, keepdims=True)
            probs[n] = [x * inverse for x in expo]
            probs_b[n] = [x.astype(jnp.bfloat16) for x in probs[n]]
        dscore = {}
        for n in lanes:
            sums[windows[n], HEAD:] += dot(jnp.concatenate(probs_b[n], axis=0), grad[n], NN)
            delta = functools.reduce(
                jnp.add,
                [
                    fold(x.astype(jnp.float32) * y, jnp.sum)
                    for x, y in zip(probs_b[n], dprob[n])
                ],
            )
            delta = jnp.sum(delta, axis=0, keepdims=True)
            dscore[n] = jnp.concatenate(
                [
                    (x * (y - delta)).astype(jnp.bfloat16)
                    for x, y in zip(probs[n], dprob[n])
                ],
                axis=0,
            )
        for n, i in enumerate(members):
            sums[windows[n], :HEAD] += dot(dscore[n], query[n], NN)
            query_grad = dot(keys_t[:, windows[n]], dscore[n], NN) * SCALE
            for h in range(q_heads):
                dq_slabs[i, :, h * HEAD : (h + 1) * HEAD] = query_grad[
                    :, h * BLOCK : (h + 1) * BLOCK
                ].T.astype(dq_slabs.dtype)
            ready(i)

    def one_step(step, carry):
        members = [order[step * TOGETHER + n] for n in range(TOGETHER)]
        sizes = [counts[step * TOGETHER + n] for n in range(TOGETHER)]
        widest = functools.reduce(jnp.maximum, sizes)
        for count in range(1, WB + 2):
            pl.when(widest == count)(functools.partial(work, count, members, sizes))
        return carry

    lax.fori_loop(first_step, last_step, one_step, 0)


def attend_near(order, counts, qd, own, own_t):
    total = WINDOW + own_t.shape[1]
    smem = pl.BlockSpec(memory_space=pltpu.SMEM)
    vmem = pl.BlockSpec(memory_space=pltpu.VMEM)
    return pl.pallas_call(
        near_kernel,
        in_specs=[smem] * 2 + [vmem] * 3,
        out_specs=[vmem] * 2,
        out_shape=[
            jax.ShapeDtypeStruct((*qd.shape[:2], qd.shape[2] // 2), qd.dtype),
            jax.ShapeDtypeStruct((total, 2 * HEAD), jnp.float32),
        ],
        scratch_shapes=[
            pltpu.VMEM((total, 2 * HEAD), own.dtype),
            pltpu.VMEM((HEAD, total), own.dtype),
        ],
        compiler_params=pltpu.CompilerParams(vmem_limit_bytes=LARGE),
    )(order, counts, qd, own, own_t)


def attend_far(order, counts, qd, own, own_t, halo, dq, sums, room):
    total = WINDOW + own_t.shape[1]
    smem = pl.BlockSpec(memory_space=pltpu.SMEM)
    vmem = pl.BlockSpec(memory_space=pltpu.VMEM)
    hbm = pl.BlockSpec(memory_space=pl.ANY)
    return pl.pallas_call(
        far_kernel,
        in_specs=[smem] * 2 + [vmem] * 6 + [hbm],
        out_specs=[hbm, vmem, vmem],
        out_shape=[
            jax.ShapeDtypeStruct(dq.shape, dq.dtype),
            jax.ShapeDtypeStruct((own_t.shape[1], 2 * HEAD), sums.dtype),
            jax.ShapeDtypeStruct(halo.shape, halo.dtype),
        ],
        input_output_aliases={8: 0, 5: 2},
        scratch_shapes=[
            pltpu.VMEM((total, 2 * HEAD), own.dtype),
            pltpu.VMEM((HEAD, total), own.dtype),
            pltpu.VMEM(sums.shape, sums.dtype),
            pltpu.VMEM(dq.shape, dq.dtype),
            pltpu.SemaphoreType.DMA(dq.shape[:1]),
        ],
        compiler_params=pltpu.CompilerParams(vmem_limit_bytes=LARGE),
    )(order, counts, qd, own, own_t, halo, dq, sums, room)


def add_kernel(sums_ref, spill_ref, out_ref, slabs, sems):
    copies = []
    for j in range(out_ref.shape[0]):
        late = slice(j * BLOCK, (j + 1) * BLOCK)
        for half, scale in ((slice(0, HEAD), SCALE), (slice(HEAD, 2 * HEAD), 1.0)):
            own = sums_ref[late, half] * scale
            slabs[j, :, half] = (own + spill_ref[j, :, half].astype(jnp.float32)).astype(
                slabs.dtype
            )
        copies.append(pltpu.make_async_copy(slabs.at[j], out_ref.at[j], sems.at[j]))
        copies[j].start()
    for copy in copies:
        copy.wait()


def add_spill(sums, spill):
    return pl.pallas_call(
        add_kernel,
        in_specs=[pl.BlockSpec(memory_space=pltpu.VMEM)] * 2,
        out_specs=pl.BlockSpec(memory_space=pl.ANY),
        out_shape=jax.ShapeDtypeStruct(spill.shape, spill.dtype),
        scratch_shapes=[
            pltpu.VMEM(spill.shape, spill.dtype),
            pltpu.SemaphoreType.DMA((spill.shape[0],)),
        ],
        compiler_params=pltpu.CompilerParams(vmem_limit_bytes=SMALL),
    )(sums, spill)


def per_device(queries, keys, values, upstream, doc_ids, band):
    tokens = queries.shape[0]
    parts = WINDOW // tokens
    cores = lax.axis_size("heads")
    spans = lax.axis_size("blk")
    step = parts // cores
    axes = ("blk", "heads")
    groups = [
        [first * parts + member for member in range(parts)] for first in range(spans // step)
    ]

    def exchange(value):
        return lax.all_to_all(
            value, axes, split_axis=0, concat_axis=0, axis_index_groups=groups, tiled=True
        )

    kv_packed = pack(keys, values, parts)
    kv = exchange(kv_packed)
    halo = lax.ppermute(kv, "blk", [(s, s + step) for s in range(spans - step)])
    qd = exchange(pack(queries, upstream, parts))
    chunk_index = (lax.axis_index("blk") // step).astype(jnp.int32).reshape(1)
    order, counts, own_t = prepare(chunk_index, doc_ids, band, kv)
    dq, sums = attend_near(order, counts, qd, kv, own_t)
    dq, sums, spill = attend_far(order, counts, qd, kv, own_t, halo, dq, sums, kv_packed)
    spill = lax.ppermute(spill, "blk", [(s + step, s) for s in range(spans - step)])
    query_out = exchange(dq)
    dkv = exchange(add_spill(sums, spill))

    return (*unpack(query_out, 1), *unpack(dkv, 2))


def solution(mesh):
    sharded = P(("groups", "blk", "heads"), None)
    return jax.shard_map(
        per_device,
        mesh=mesh,
        in_specs=(sharded,) * 4 + (P("groups"),) * 2,
        out_specs=(sharded,) * 3,
        check_vma=False,
    )
```

```python
import functools
import math

import jax
import jax.numpy as jnp
from jax import lax
from jax.experimental import pallas as pl
from jax.experimental.pallas import tpu as pltpu
from jax.sharding import PartitionSpec as P

HEAD = 128
SCALAR = 168
WINDOW = 1024
BLOCK = 128
WB = WINDOW // BLOCK
SCALE = SCALAR ** (-0.5)
LOG2E = math.log2(math.e)
SMALL = 8 * 1024 * 1024
LARGE = 40 * 1024 * 1024
TOGETHER = 2

NT = (((1,), (1,)), ((), ()))
NN = (((1,), (0,)), ((), ()))


def dot(a, b, dims):
    return lax.dot_general(a, b, dims, preferred_element_type=jnp.float32)


def run_copies(pairs, sems):
    copies = [pltpu.make_async_copy(x, y, sems.at[n]) for n, (x, y) in enumerate(pairs)]
    for copy in copies:
        copy.start()
    for copy in copies:
        copy.wait()


def pack_kernel(a_ref, b_ref, out_ref, slabs, in_sems, out_sems):
    heads = out_ref.shape[0]
    width = out_ref.shape[2] // 2
    reads = [
        [
            pltpu.make_async_copy(
                ref.at[:, pl.ds(h * width, width)],
                slabs.at[h, :, pl.ds(n * width, width)],
                in_sems.at[2 * h + n],
            )
            for n, ref in enumerate((a_ref, b_ref))
        ]
        for h in range(heads)
    ]
    writes = [
        pltpu.make_async_copy(slabs.at[h], out_ref.at[h], out_sems.at[h]) for h in range(heads)
    ]
    for pair in reads:
        for copy in pair:
            copy.start()
    for pair, write in zip(reads, writes):
        for copy in pair:
            copy.wait()
        write.start()
    for write in writes:
        write.wait()


def pack(a, b, heads):
    tokens, cols = a.shape
    hbm = pl.BlockSpec(memory_space=pl.ANY)
    shape = (heads, tokens, 2 * cols // heads)
    return pl.pallas_call(
        pack_kernel,
        in_specs=[hbm] * 2,
        out_specs=hbm,
        out_shape=jax.ShapeDtypeStruct(shape, a.dtype),
        scratch_shapes=[
            pltpu.VMEM(shape, a.dtype),
            pltpu.SemaphoreType.DMA((2 * heads,)),
            pltpu.SemaphoreType.DMA((heads,)),
        ],
    )(a, b)


def unpack_kernel(in_ref, *refs):
    out_refs, sems = refs[:-1], refs[-1]
    width = in_ref.shape[2] // len(out_refs)
    run_copies(
        [
            (in_ref.at[h, :, pl.ds(n * width, width)], ref.at[:, pl.ds(h * width, width)])
            for h in range(in_ref.shape[0])
            for n, ref in enumerate(out_refs)
        ],
        sems,
    )


def unpack(value, outputs):
    heads, tokens, width = value.shape
    shape = jax.ShapeDtypeStruct((tokens, heads * width // outputs), value.dtype)
    return pl.pallas_call(
        unpack_kernel,
        in_specs=[pl.BlockSpec(memory_space=pltpu.VMEM)],
        out_specs=[pl.BlockSpec(memory_space=pl.ANY)] * outputs,
        out_shape=[shape] * outputs,
        scratch_shapes=[pltpu.SemaphoreType.DMA((outputs * heads,))],
        compiler_params=pltpu.CompilerParams(vmem_limit_bytes=SMALL),
    )(value)


def prepare_kernel(chunk_ref, doc_ref, band_ref, own_ref, order, counts, own_t_ref):
    blocks = own_ref.shape[0]
    for j in range(blocks):
        own_t_ref[:, j * BLOCK : (j + 1) * BLOCK] = own_ref[j, :, :HEAD].T
    first = chunk_ref[0] * blocks
    length = jnp.int32(0)
    for back in range(1, WB + 1):
        same = (first >= back) & (doc_ref[jnp.maximum(first - back, 0)] == doc_ref[first])
        length = length + same.astype(jnp.int32)
    seen = []
    for i in range(blocks):
        if i > 0:
            same = doc_ref[first + i] == doc_ref[first + i - 1]
            length = jnp.where(same, length + 1, 0)
        seen.append(jnp.minimum(band_ref[first + i], length) + 1)
    far = [(seen[i] > i + 1).astype(jnp.int32) for i in range(blocks)]
    place = [seen[i] + 2 * WB * far[i] for i in range(blocks)]
    for i in range(blocks):
        rank = jnp.int32(0)
        for j in range(blocks):
            if j != i:
                below = place[j] <= place[i] if j < i else place[j] < place[i]
                rank = rank + below.astype(jnp.int32)
        order[rank] = i
        counts[rank] = seen[i]
    near = blocks - functools.reduce(jnp.add, far)
    counts[blocks] = near // TOGETHER
    counts[blocks + 1] = functools.reduce(
        jnp.minimum, [jnp.minimum(i + WB + 1 - seen[i], WB) for i in range(blocks)]
    )


def prepare(chunk_index, doc_ids, band, own):
    blocks = own.shape[0]
    smem = pl.BlockSpec(memory_space=pltpu.SMEM)
    vmem = pl.BlockSpec(memory_space=pltpu.VMEM)
    return pl.pallas_call(
        prepare_kernel,
        in_specs=[smem] * 3 + [vmem],
        out_specs=[smem] * 2 + [vmem],
        out_shape=[
            jax.ShapeDtypeStruct((blocks,), jnp.int32),
            jax.ShapeDtypeStruct((blocks + 2,), jnp.int32),
            jax.ShapeDtypeStruct((HEAD, blocks * BLOCK), own.dtype),
        ],
        compiler_params=pltpu.CompilerParams(vmem_limit_bytes=SMALL),
    )(chunk_index, doc_ids, band, own)


def place_own(own_ref, own_t_ref, kv, keys_t):
    for j in range(own_ref.shape[0]):
        late = slice(WINDOW + j * BLOCK, WINDOW + (j + 1) * BLOCK)
        kv[late, :] = own_ref[j]
        keys_t[:, late] = own_t_ref[:, j * BLOCK : (j + 1) * BLOCK]


def near_kernel(order, counts, qd_ref, own_ref, own_t_ref, dq_ref, sums, kv, keys_t):
    kv[:WINDOW, :] = jnp.zeros((WINDOW, 2 * HEAD), kv.dtype)
    keys_t[:, :WINDOW] = jnp.zeros((HEAD, WINDOW), keys_t.dtype)
    place_own(own_ref, own_t_ref, kv, keys_t)
    sums[...] = jnp.zeros_like(sums)
    last = counts[order.shape[0]]
    attend(0, last, order, counts, qd_ref, kv, keys_t, dq_ref, sums, lambda i: None)


def far_kernel(
    order, counts, qd_ref, halo_ref, dq_near_ref, room_ref, kv_in, keys_t_in, sums_in,
    dq_ref, sums_ref, spill_ref, kv, keys_t, sums, dq_slabs, dq_sems,
):
    del room_ref, kv_in, keys_t_in, sums_in
    blocks = order.shape[0]
    steps = counts[blocks]

    def dq_copy(slabs, i):
        return pltpu.make_async_copy(slabs.at[i], dq_ref.at[i], dq_sems.at[i])

    def pass_on(m, carry):
        dq_copy(dq_near_ref, order[m]).start()
        return carry

    def fill(j, carry):
        rows = pl.ds(pl.multiple_of(j * BLOCK, BLOCK), BLOCK)
        kv[rows, :] = halo_ref[j]
        keys_t[:, rows] = halo_ref[j, :, :HEAD].T
        return carry

    lax.fori_loop(0, steps * TOGETHER, pass_on, 0)
    lax.fori_loop(counts[blocks + 1], WB, fill, 0)
    attend(
        steps, blocks // TOGETHER, order, counts, qd_ref, kv, keys_t, dq_slabs, sums,
        lambda i: dq_copy(dq_slabs, i).start(),
    )
    for j in range(WB):
        rows = slice(j * BLOCK, (j + 1) * BLOCK)
        spill_ref[j, :, :HEAD] = (sums[rows, :HEAD] * SCALE).astype(spill_ref.dtype)
        spill_ref[j, :, HEAD:] = sums[rows, HEAD:].astype(spill_ref.dtype)
    sums_ref[...] = sums[WINDOW:, :]
    for i in range(blocks):
        dq_copy(dq_slabs, i).wait()


def attend(first_step, last_step, order, counts, qd_ref, kv, keys_t, dq_slabs, sums, ready):
    q_heads = qd_ref.shape[2] // (2 * HEAD)
    rows = q_heads * BLOCK

    def stacked(i, offset):
        return jnp.concatenate(
            [qd_ref[i, :, (offset + h) * HEAD : (offset + h + 1) * HEAD] for h in range(q_heads)],
            axis=0,
        )

    def fold(x, reduce):
        return reduce(x.reshape(BLOCK // 8, 8, rows), axis=0)

    def work(count, members, sizes):
        span = count * BLOCK
        windows = [
            pl.ds(pl.multiple_of((i + WB + 1 - count) * BLOCK, BLOCK), span) for i in members
        ]
        lanes = range(len(members))

        def split(x):
            return [x[b * BLOCK : (b + 1) * BLOCK] for b in range(count)]

        query = [stacked(i, 0) for i in members]
        grad = [stacked(i, q_heads) for i in members]
        scores = [split(dot(kv[windows[n], :HEAD], query[n], NT)) for n in lanes]
        key_pos = lax.broadcasted_iota(jnp.int32, (BLOCK, rows), 0)
        query_pos = lax.broadcasted_iota(jnp.int32, (BLOCK, rows), 1) % BLOCK
        causal = key_pos <= query_pos
        probs, probs_b, dprob = {}, {}, {}
        for n in lanes:
            scores[n][-1] = jnp.where(causal, scores[n][-1], -jnp.inf)
            seen = [count - b <= sizes[n] for b in range(count)]
            tops = [
                jnp.where(seen[b], fold(x, jnp.max), -jnp.inf) for b, x in enumerate(scores[n])
            ]
            top = jnp.max(functools.reduce(jnp.maximum, tops), axis=0, keepdims=True)
            shift = [jnp.where(seen[b], top, jnp.inf) for b in range(count)]
            dprob[n] = split(dot(kv[windows[n], HEAD:], grad[n], NT))
            expo = [jnp.exp2((x - y) * (SCALE * LOG2E)) for x, y in zip(scores[n], shift)]
            total = functools.reduce(jnp.add, [fold(x, jnp.sum) for x in expo])
            inverse = 1.0 / jnp.sum(total, axis=0, keepdims=True)
            probs[n] = [x * inverse for x in expo]
            probs_b[n] = [x.astype(jnp.bfloat16) for x in probs[n]]
        dscore = {}
        for n in lanes:
            sums[windows[n], HEAD:] += dot(jnp.concatenate(probs_b[n], axis=0), grad[n], NN)
            delta = functools.reduce(
                jnp.add,
                [
                    fold(x.astype(jnp.float32) * y, jnp.sum)
                    for x, y in zip(probs_b[n], dprob[n])
                ],
            )
            delta = jnp.sum(delta, axis=0, keepdims=True)
            dscore[n] = jnp.concatenate(
                [
                    (x * (y - delta)).astype(jnp.bfloat16)
                    for x, y in zip(probs[n], dprob[n])
                ],
                axis=0,
            )
        for n, i in enumerate(members):
            sums[windows[n], :HEAD] += dot(dscore[n], query[n], NN)
            query_grad = dot(keys_t[:, windows[n]], dscore[n], NN) * SCALE
            for h in range(q_heads):
                dq_slabs[i, :, h * HEAD : (h + 1) * HEAD] = query_grad[
                    :, h * BLOCK : (h + 1) * BLOCK
                ].T.astype(dq_slabs.dtype)
            ready(i)

    def one_step(step, carry):
        members = [order[step * TOGETHER + n] for n in range(TOGETHER)]
        sizes = [counts[step * TOGETHER + n] for n in range(TOGETHER)]
        widest = functools.reduce(jnp.maximum, sizes)
        for count in range(1, WB + 2):
            pl.when(widest == count)(functools.partial(work, count, members, sizes))
        return carry

    lax.fori_loop(first_step, last_step, one_step, 0)


def attend_near(order, counts, qd, own, own_t):
    total = WINDOW + own_t.shape[1]
    smem = pl.BlockSpec(memory_space=pltpu.SMEM)
    vmem = pl.BlockSpec(memory_space=pltpu.VMEM)
    return pl.pallas_call(
        near_kernel,
        in_specs=[smem] * 2 + [vmem] * 3,
        out_specs=[vmem] * 4,
        out_shape=[
            jax.ShapeDtypeStruct((*qd.shape[:2], qd.shape[2] // 2), qd.dtype),
            jax.ShapeDtypeStruct((total, 2 * HEAD), jnp.float32),
            jax.ShapeDtypeStruct((total, 2 * HEAD), own.dtype),
            jax.ShapeDtypeStruct((HEAD, total), own.dtype),
        ],
        compiler_params=pltpu.CompilerParams(vmem_limit_bytes=LARGE),
    )(order, counts, qd, own, own_t)


def attend_far(order, counts, qd, halo, dq, room, kv, keys_t, sums):
    smem = pl.BlockSpec(memory_space=pltpu.SMEM)
    vmem = pl.BlockSpec(memory_space=pltpu.VMEM)
    hbm = pl.BlockSpec(memory_space=pl.ANY)
    own_sums = jax.ShapeDtypeStruct((sums.shape[0] - WINDOW, sums.shape[1]), sums.dtype)
    shapes = [jax.ShapeDtypeStruct(x.shape, x.dtype) for x in (dq, halo, kv, keys_t, sums)]
    return pl.pallas_call(
        far_kernel,
        in_specs=[smem] * 2 + [vmem] * 3 + [hbm] + [vmem] * 3,
        out_specs=[hbm] + [vmem] * 5,
        out_shape=[shapes[0], own_sums, *shapes[1:]],
        input_output_aliases={5: 0, 3: 2, 6: 3, 7: 4, 8: 5},
        scratch_shapes=[
            pltpu.VMEM(dq.shape, dq.dtype),
            pltpu.SemaphoreType.DMA(dq.shape[:1]),
        ],
        compiler_params=pltpu.CompilerParams(vmem_limit_bytes=LARGE),
    )(order, counts, qd, halo, dq, room, kv, keys_t, sums)[:3]


def add_kernel(sums_ref, spill_ref, out_ref, slabs, sems):
    copies = []
    for j in range(out_ref.shape[0]):
        late = slice(j * BLOCK, (j + 1) * BLOCK)
        for half, scale in ((slice(0, HEAD), SCALE), (slice(HEAD, 2 * HEAD), 1.0)):
            own = sums_ref[late, half] * scale
            slabs[j, :, half] = (own + spill_ref[j, :, half].astype(jnp.float32)).astype(
                slabs.dtype
            )
        copies.append(pltpu.make_async_copy(slabs.at[j], out_ref.at[j], sems.at[j]))
        copies[j].start()
    for copy in copies:
        copy.wait()


def add_spill(sums, spill):
    return pl.pallas_call(
        add_kernel,
        in_specs=[pl.BlockSpec(memory_space=pltpu.VMEM)] * 2,
        out_specs=pl.BlockSpec(memory_space=pl.ANY),
        out_shape=jax.ShapeDtypeStruct(spill.shape, spill.dtype),
        scratch_shapes=[
            pltpu.VMEM(spill.shape, spill.dtype),
            pltpu.SemaphoreType.DMA((spill.shape[0],)),
        ],
        compiler_params=pltpu.CompilerParams(vmem_limit_bytes=SMALL),
    )(sums, spill)


def per_device(queries, keys, values, upstream, doc_ids, band):
    tokens = queries.shape[0]
    parts = WINDOW // tokens
    cores = lax.axis_size("heads")
    spans = lax.axis_size("blk")
    step = parts // cores
    axes = ("blk", "heads")
    groups = [
        [first * parts + member for member in range(parts)] for first in range(spans // step)
    ]

    def exchange(value):
        return lax.all_to_all(
            value, axes, split_axis=0, concat_axis=0, axis_index_groups=groups, tiled=True
        )

    kv_packed = pack(keys, values, parts)
    kv = exchange(kv_packed)
    halo = lax.ppermute(kv, "blk", [(s, s + step) for s in range(spans - step)])
    qd = exchange(pack(queries, upstream, parts))
    chunk_index = (lax.axis_index("blk") // step).astype(jnp.int32).reshape(1)
    order, counts, own_t = prepare(chunk_index, doc_ids, band, kv)
    dq, sums, rows, rows_t = attend_near(order, counts, qd, kv, own_t)
    dq, sums, spill = attend_far(order, counts, qd, halo, dq, kv_packed, rows, rows_t, sums)
    spill = lax.ppermute(spill, "blk", [(s + step, s) for s in range(spans - step)])
    query_out = exchange(dq)
    dkv = exchange(add_spill(sums, spill))

    return (*unpack(query_out, 1), *unpack(dkv, 2))


def solution(mesh):
    sharded = P(("groups", "blk", "heads"), None)
    return jax.shard_map(
        per_device,
        mesh=mesh,
        in_specs=(sharded,) * 4 + (P("groups"),) * 2,
        out_specs=(sharded,) * 3,
        check_vma=False,
    )
```

```python
import functools
import math

import jax
import jax.numpy as jnp
from jax import lax
from jax.experimental import pallas as pl
from jax.experimental.pallas import tpu as pltpu
from jax.sharding import PartitionSpec as P

HEAD = 128
SCALAR = 168
WINDOW = 1024
BLOCK = 128
WB = WINDOW // BLOCK
SCALE = SCALAR ** (-0.5)
LOG2E = math.log2(math.e)
SMALL = 8 * 1024 * 1024
LARGE = 40 * 1024 * 1024
TOGETHER = 2

NT = (((1,), (1,)), ((), ()))
NN = (((1,), (0,)), ((), ()))


def dot(a, b, dims):
    return lax.dot_general(a, b, dims, preferred_element_type=jnp.float32)


def run_copies(pairs, sems):
    copies = [pltpu.make_async_copy(x, y, sems.at[n]) for n, (x, y) in enumerate(pairs)]
    for copy in copies:
        copy.start()
    for copy in copies:
        copy.wait()


def pack_kernel(a_ref, b_ref, out_ref, slabs, in_sems, out_sems):
    heads = out_ref.shape[0]
    width = out_ref.shape[2] // 2
    reads = [
        [
            pltpu.make_async_copy(
                ref.at[:, pl.ds(h * width, width)],
                slabs.at[h, :, pl.ds(n * width, width)],
                in_sems.at[2 * h + n],
            )
            for n, ref in enumerate((a_ref, b_ref))
        ]
        for h in range(heads)
    ]
    writes = [
        pltpu.make_async_copy(slabs.at[h], out_ref.at[h], out_sems.at[h]) for h in range(heads)
    ]
    for pair in reads:
        for copy in pair:
            copy.start()
    for pair, write in zip(reads, writes):
        for copy in pair:
            copy.wait()
        write.start()
    for write in writes:
        write.wait()


def pack(a, b, heads):
    tokens, cols = a.shape
    hbm = pl.BlockSpec(memory_space=pl.ANY)
    shape = (heads, tokens, 2 * cols // heads)
    return pl.pallas_call(
        pack_kernel,
        in_specs=[hbm] * 2,
        out_specs=hbm,
        out_shape=jax.ShapeDtypeStruct(shape, a.dtype),
        scratch_shapes=[
            pltpu.VMEM(shape, a.dtype),
            pltpu.SemaphoreType.DMA((2 * heads,)),
            pltpu.SemaphoreType.DMA((heads,)),
        ],
    )(a, b)


def unpack_kernel(in_ref, *refs):
    out_refs, sems = refs[:-1], refs[-1]
    width = in_ref.shape[2] // len(out_refs)
    run_copies(
        [
            (in_ref.at[h, :, pl.ds(n * width, width)], ref.at[:, pl.ds(h * width, width)])
            for h in range(in_ref.shape[0])
            for n, ref in enumerate(out_refs)
        ],
        sems,
    )


def unpack(value, outputs):
    heads, tokens, width = value.shape
    shape = jax.ShapeDtypeStruct((tokens, heads * width // outputs), value.dtype)
    return pl.pallas_call(
        unpack_kernel,
        in_specs=[pl.BlockSpec(memory_space=pltpu.VMEM)],
        out_specs=[pl.BlockSpec(memory_space=pl.ANY)] * outputs,
        out_shape=[shape] * outputs,
        scratch_shapes=[pltpu.SemaphoreType.DMA((outputs * heads,))],
        compiler_params=pltpu.CompilerParams(vmem_limit_bytes=SMALL),
    )(value)


def prepare_kernel(chunk_ref, doc_ref, band_ref, own_ref, order, counts, own_t_ref):
    blocks = own_ref.shape[0]
    for j in range(blocks):
        own_t_ref[:, j * BLOCK : (j + 1) * BLOCK] = own_ref[j, :, :HEAD].T
    first = chunk_ref[0] * blocks
    length = jnp.int32(0)
    for back in range(1, WB + 1):
        same = (first >= back) & (doc_ref[jnp.maximum(first - back, 0)] == doc_ref[first])
        length = length + same.astype(jnp.int32)
    seen = []
    for i in range(blocks):
        if i > 0:
            same = doc_ref[first + i] == doc_ref[first + i - 1]
            length = jnp.where(same, length + 1, 0)
        seen.append(jnp.minimum(band_ref[first + i], length) + 1)
    far = [(seen[i] > i + 1).astype(jnp.int32) for i in range(blocks)]
    place = [seen[i] + 2 * WB * far[i] for i in range(blocks)]
    for i in range(blocks):
        rank = jnp.int32(0)
        for j in range(blocks):
            if j != i:
                below = place[j] <= place[i] if j < i else place[j] < place[i]
                rank = rank + below.astype(jnp.int32)
        order[rank] = i
        counts[rank] = seen[i]
    near = blocks - functools.reduce(jnp.add, far)
    counts[blocks] = near // TOGETHER
    counts[blocks + 1] = functools.reduce(
        jnp.minimum, [jnp.minimum(i + WB + 1 - seen[i], WB) for i in range(blocks)]
    )


def prepare(chunk_index, doc_ids, band, own):
    blocks = own.shape[0]
    smem = pl.BlockSpec(memory_space=pltpu.SMEM)
    vmem = pl.BlockSpec(memory_space=pltpu.VMEM)
    return pl.pallas_call(
        prepare_kernel,
        in_specs=[smem] * 3 + [vmem],
        out_specs=[smem] * 2 + [vmem],
        out_shape=[
            jax.ShapeDtypeStruct((blocks,), jnp.int32),
            jax.ShapeDtypeStruct((blocks + 2,), jnp.int32),
            jax.ShapeDtypeStruct((HEAD, blocks * BLOCK), own.dtype),
        ],
        compiler_params=pltpu.CompilerParams(vmem_limit_bytes=SMALL),
    )(chunk_index, doc_ids, band, own)


def place_own(own_ref, own_t_ref, kv, keys_t):
    for j in range(own_ref.shape[0]):
        late = slice(WINDOW + j * BLOCK, WINDOW + (j + 1) * BLOCK)
        kv[late, :] = own_ref[j]
        keys_t[:, late] = own_t_ref[:, j * BLOCK : (j + 1) * BLOCK]


def near_kernel(order, counts, qd_ref, own_ref, own_t_ref, dq_ref, sums, kv, keys_t):
    kv[:WINDOW, :] = jnp.zeros((WINDOW, 2 * HEAD), kv.dtype)
    keys_t[:, :WINDOW] = jnp.zeros((HEAD, WINDOW), keys_t.dtype)
    place_own(own_ref, own_t_ref, kv, keys_t)
    sums[...] = jnp.zeros_like(sums)
    last = counts[order.shape[0]]
    attend(0, last, order, counts, qd_ref, kv, keys_t, dq_ref, sums, lambda i: None)


def far_kernel(
    order, counts, qd_ref, halo_ref, dq_near_ref, room_ref, kv_in, keys_t_in, sums_in,
    dq_ref, sums_ref, spill_ref, kv, keys_t, sums, dq_slabs, dq_sems,
):
    del room_ref, kv_in, keys_t_in, sums_in
    blocks = order.shape[0]
    steps = counts[blocks]

    def dq_copy(slabs, i):
        return pltpu.make_async_copy(slabs.at[i], dq_ref.at[i], dq_sems.at[i])

    def pass_on(m, carry):
        dq_copy(dq_near_ref, order[m]).start()
        return carry

    lax.fori_loop(0, steps * TOGETHER, pass_on, 0)

    @pl.when(counts[blocks + 1] < WB)
    def fill():
        for j in range(WB):
            rows = slice(j * BLOCK, (j + 1) * BLOCK)
            kv[rows, :] = halo_ref[j]
            keys_t[:, rows] = halo_ref[j, :, :HEAD].T

    attend(
        steps, blocks // TOGETHER, order, counts, qd_ref, kv, keys_t, dq_slabs, sums,
        lambda i: dq_copy(dq_slabs, i).start(),
    )
    for j in range(WB):
        rows = slice(j * BLOCK, (j + 1) * BLOCK)
        spill_ref[j, :, :HEAD] = (sums[rows, :HEAD] * SCALE).astype(spill_ref.dtype)
        spill_ref[j, :, HEAD:] = sums[rows, HEAD:].astype(spill_ref.dtype)
    sums_ref[...] = sums[WINDOW:, :]
    for i in range(blocks):
        dq_copy(dq_slabs, i).wait()


def attend(first_step, last_step, order, counts, qd_ref, kv, keys_t, dq_slabs, sums, ready):
    q_heads = qd_ref.shape[2] // (2 * HEAD)
    rows = q_heads * BLOCK

    def stacked(i, offset):
        return jnp.concatenate(
            [qd_ref[i, :, (offset + h) * HEAD : (offset + h + 1) * HEAD] for h in range(q_heads)],
            axis=0,
        )

    def fold(x, reduce):
        return reduce(x.reshape(BLOCK // 8, 8, rows), axis=0)

    def work(count, members, sizes):
        span = count * BLOCK
        windows = [
            pl.ds(pl.multiple_of((i + WB + 1 - count) * BLOCK, BLOCK), span) for i in members
        ]
        lanes = range(len(members))

        def split(x):
            return [x[b * BLOCK : (b + 1) * BLOCK] for b in range(count)]

        query = [stacked(i, 0) for i in members]
        grad = [stacked(i, q_heads) for i in members]
        scores = [split(dot(kv[windows[n], :HEAD], query[n], NT)) for n in lanes]
        key_pos = lax.broadcasted_iota(jnp.int32, (BLOCK, rows), 0)
        query_pos = lax.broadcasted_iota(jnp.int32, (BLOCK, rows), 1) % BLOCK
        causal = key_pos <= query_pos
        probs, probs_b, dprob = {}, {}, {}
        for n in lanes:
            scores[n][-1] = jnp.where(causal, scores[n][-1], -jnp.inf)
            seen = [count - b <= sizes[n] for b in range(count)]
            tops = [
                jnp.where(seen[b], fold(x, jnp.max), -jnp.inf) for b, x in enumerate(scores[n])
            ]
            top = jnp.max(functools.reduce(jnp.maximum, tops), axis=0, keepdims=True)
            shift = [jnp.where(seen[b], top, jnp.inf) for b in range(count)]
            dprob[n] = split(dot(kv[windows[n], HEAD:], grad[n], NT))
            expo = [jnp.exp2((x - y) * (SCALE * LOG2E)) for x, y in zip(scores[n], shift)]
            total = functools.reduce(jnp.add, [fold(x, jnp.sum) for x in expo])
            inverse = 1.0 / jnp.sum(total, axis=0, keepdims=True)
            probs[n] = [x * inverse for x in expo]
            probs_b[n] = [x.astype(jnp.bfloat16) for x in probs[n]]
        dscore = {}
        for n in lanes:
            sums[windows[n], HEAD:] += dot(jnp.concatenate(probs_b[n], axis=0), grad[n], NN)
            delta = functools.reduce(
                jnp.add,
                [
                    fold(x.astype(jnp.float32) * y, jnp.sum)
                    for x, y in zip(probs_b[n], dprob[n])
                ],
            )
            delta = jnp.sum(delta, axis=0, keepdims=True)
            dscore[n] = jnp.concatenate(
                [
                    (x * (y - delta)).astype(jnp.bfloat16)
                    for x, y in zip(probs[n], dprob[n])
                ],
                axis=0,
            )
        for n, i in enumerate(members):
            sums[windows[n], :HEAD] += dot(dscore[n], query[n], NN)
            query_grad = dot(keys_t[:, windows[n]], dscore[n], NN) * SCALE
            for h in range(q_heads):
                dq_slabs[i, :, h * HEAD : (h + 1) * HEAD] = query_grad[
                    :, h * BLOCK : (h + 1) * BLOCK
                ].T.astype(dq_slabs.dtype)
            ready(i)

    def one_step(step, carry):
        members = [order[step * TOGETHER + n] for n in range(TOGETHER)]
        sizes = [counts[step * TOGETHER + n] for n in range(TOGETHER)]
        widest = functools.reduce(jnp.maximum, sizes)
        for count in range(1, WB + 2):
            pl.when(widest == count)(functools.partial(work, count, members, sizes))
        return carry

    lax.fori_loop(first_step, last_step, one_step, 0)


def attend_near(order, counts, qd, own, own_t):
    total = WINDOW + own_t.shape[1]
    smem = pl.BlockSpec(memory_space=pltpu.SMEM)
    vmem = pl.BlockSpec(memory_space=pltpu.VMEM)
    return pl.pallas_call(
        near_kernel,
        in_specs=[smem] * 2 + [vmem] * 3,
        out_specs=[vmem] * 4,
        out_shape=[
            jax.ShapeDtypeStruct((*qd.shape[:2], qd.shape[2] // 2), qd.dtype),
            jax.ShapeDtypeStruct((total, 2 * HEAD), jnp.float32),
            jax.ShapeDtypeStruct((total, 2 * HEAD), own.dtype),
            jax.ShapeDtypeStruct((HEAD, total), own.dtype),
        ],
        compiler_params=pltpu.CompilerParams(vmem_limit_bytes=LARGE),
    )(order, counts, qd, own, own_t)


def attend_far(order, counts, qd, halo, dq, room, kv, keys_t, sums):
    smem = pl.BlockSpec(memory_space=pltpu.SMEM)
    vmem = pl.BlockSpec(memory_space=pltpu.VMEM)
    hbm = pl.BlockSpec(memory_space=pl.ANY)
    own_sums = jax.ShapeDtypeStruct((sums.shape[0] - WINDOW, sums.shape[1]), sums.dtype)
    shapes = [jax.ShapeDtypeStruct(x.shape, x.dtype) for x in (dq, halo, kv, keys_t, sums)]
    return pl.pallas_call(
        far_kernel,
        in_specs=[smem] * 2 + [vmem] * 3 + [hbm] + [vmem] * 3,
        out_specs=[hbm] + [vmem] * 5,
        out_shape=[shapes[0], own_sums, *shapes[1:]],
        input_output_aliases={5: 0, 3: 2, 6: 3, 7: 4, 8: 5},
        scratch_shapes=[
            pltpu.VMEM(dq.shape, dq.dtype),
            pltpu.SemaphoreType.DMA(dq.shape[:1]),
        ],
        compiler_params=pltpu.CompilerParams(vmem_limit_bytes=LARGE),
    )(order, counts, qd, halo, dq, room, kv, keys_t, sums)[:3]


def add_kernel(sums_ref, spill_ref, out_ref, slabs, sems):
    copies = []
    for j in range(out_ref.shape[0]):
        late = slice(j * BLOCK, (j + 1) * BLOCK)
        for half, scale in ((slice(0, HEAD), SCALE), (slice(HEAD, 2 * HEAD), 1.0)):
            own = sums_ref[late, half] * scale
            slabs[j, :, half] = (own + spill_ref[j, :, half].astype(jnp.float32)).astype(
                slabs.dtype
            )
        copies.append(pltpu.make_async_copy(slabs.at[j], out_ref.at[j], sems.at[j]))
        copies[j].start()
    for copy in copies:
        copy.wait()


def add_spill(sums, spill):
    return pl.pallas_call(
        add_kernel,
        in_specs=[pl.BlockSpec(memory_space=pltpu.VMEM)] * 2,
        out_specs=pl.BlockSpec(memory_space=pl.ANY),
        out_shape=jax.ShapeDtypeStruct(spill.shape, spill.dtype),
        scratch_shapes=[
            pltpu.VMEM(spill.shape, spill.dtype),
            pltpu.SemaphoreType.DMA((spill.shape[0],)),
        ],
        compiler_params=pltpu.CompilerParams(vmem_limit_bytes=SMALL),
    )(sums, spill)


def per_device(queries, keys, values, upstream, doc_ids, band):
    tokens = queries.shape[0]
    parts = WINDOW // tokens
    cores = lax.axis_size("heads")
    spans = lax.axis_size("blk")
    step = parts // cores
    axes = ("blk", "heads")
    groups = [
        [first * parts + member for member in range(parts)] for first in range(spans // step)
    ]

    def exchange(value):
        return lax.all_to_all(
            value, axes, split_axis=0, concat_axis=0, axis_index_groups=groups, tiled=True
        )

    kv_packed = pack(keys, values, parts)
    kv = exchange(kv_packed)
    halo = lax.ppermute(kv, "blk", [(s, s + step) for s in range(spans - step)])
    qd = exchange(pack(queries, upstream, parts))
    chunk_index = (lax.axis_index("blk") // step).astype(jnp.int32).reshape(1)
    order, counts, own_t = prepare(chunk_index, doc_ids, band, kv)
    dq, sums, rows, rows_t = attend_near(order, counts, qd, kv, own_t)
    dq, sums, spill = attend_far(order, counts, qd, halo, dq, kv_packed, rows, rows_t, sums)
    spill = lax.ppermute(spill, "blk", [(s + step, s) for s in range(spans - step)])
    query_out = exchange(dq)
    dkv = exchange(add_spill(sums, spill))

    return (*unpack(query_out, 1), *unpack(dkv, 2))


def solution(mesh):
    sharded = P(("groups", "blk", "heads"), None)
    return jax.shard_map(
        per_device,
        mesh=mesh,
        in_specs=(sharded,) * 4 + (P("groups"),) * 2,
        out_specs=(sharded,) * 3,
        check_vma=False,
    )
```

```python
import functools
import math

import jax
import jax.numpy as jnp
from jax import lax
from jax.experimental import pallas as pl
from jax.experimental.pallas import tpu as pltpu
from jax.sharding import PartitionSpec as P

HEAD = 128
SCALAR = 168
WINDOW = 1024
BLOCK = 128
WB = WINDOW // BLOCK
SCALE = SCALAR ** (-0.5)
LOG2E = math.log2(math.e)
SMALL = 8 * 1024 * 1024
LARGE = 40 * 1024 * 1024
TOGETHER = 2

NT = (((1,), (1,)), ((), ()))
NN = (((1,), (0,)), ((), ()))


def dot(a, b, dims):
    return lax.dot_general(a, b, dims, preferred_element_type=jnp.float32)


def run_copies(pairs, sems):
    copies = [pltpu.make_async_copy(x, y, sems.at[n]) for n, (x, y) in enumerate(pairs)]
    for copy in copies:
        copy.start()
    for copy in copies:
        copy.wait()


def pack_kernel(a_ref, b_ref, out_ref, slabs, in_sems, out_sems):
    heads = out_ref.shape[0]
    width = out_ref.shape[2] // 2
    reads = [
        [
            pltpu.make_async_copy(
                ref.at[:, pl.ds(h * width, width)],
                slabs.at[h, :, pl.ds(n * width, width)],
                in_sems.at[2 * h + n],
            )
            for n, ref in enumerate((a_ref, b_ref))
        ]
        for h in range(heads)
    ]
    writes = [
        pltpu.make_async_copy(slabs.at[h], out_ref.at[h], out_sems.at[h]) for h in range(heads)
    ]
    for pair in reads:
        for copy in pair:
            copy.start()
    for pair, write in zip(reads, writes):
        for copy in pair:
            copy.wait()
        write.start()
    for write in writes:
        write.wait()


def pack(a, b, heads):
    tokens, cols = a.shape
    hbm = pl.BlockSpec(memory_space=pl.ANY)
    shape = (heads, tokens, 2 * cols // heads)
    return pl.pallas_call(
        pack_kernel,
        in_specs=[hbm] * 2,
        out_specs=hbm,
        out_shape=jax.ShapeDtypeStruct(shape, a.dtype),
        scratch_shapes=[
            pltpu.VMEM(shape, a.dtype),
            pltpu.SemaphoreType.DMA((2 * heads,)),
            pltpu.SemaphoreType.DMA((heads,)),
        ],
    )(a, b)


def unpack_kernel(in_ref, *refs):
    out_refs, sems = refs[:-1], refs[-1]
    width = in_ref.shape[2] // len(out_refs)
    run_copies(
        [
            (in_ref.at[h, :, pl.ds(n * width, width)], ref.at[:, pl.ds(h * width, width)])
            for h in range(in_ref.shape[0])
            for n, ref in enumerate(out_refs)
        ],
        sems,
    )


def unpack(value, outputs):
    heads, tokens, width = value.shape
    shape = jax.ShapeDtypeStruct((tokens, heads * width // outputs), value.dtype)
    return pl.pallas_call(
        unpack_kernel,
        in_specs=[pl.BlockSpec(memory_space=pltpu.VMEM)],
        out_specs=[pl.BlockSpec(memory_space=pl.ANY)] * outputs,
        out_shape=[shape] * outputs,
        scratch_shapes=[pltpu.SemaphoreType.DMA((outputs * heads,))],
        compiler_params=pltpu.CompilerParams(vmem_limit_bytes=SMALL),
    )(value)


def prepare_kernel(chunk_ref, doc_ref, band_ref, own_ref, order, counts, own_t_ref):
    blocks = own_ref.shape[0]
    for j in range(blocks):
        own_t_ref[:, j * BLOCK : (j + 1) * BLOCK] = own_ref[j, :, :HEAD].T
    first = chunk_ref[0] * blocks
    length = jnp.int32(0)
    for back in range(1, WB + 1):
        same = (first >= back) & (doc_ref[jnp.maximum(first - back, 0)] == doc_ref[first])
        length = length + same.astype(jnp.int32)
    seen = []
    for i in range(blocks):
        if i > 0:
            same = doc_ref[first + i] == doc_ref[first + i - 1]
            length = jnp.where(same, length + 1, 0)
        seen.append(jnp.minimum(band_ref[first + i], length) + 1)
    far = [(seen[i] > i + 1).astype(jnp.int32) for i in range(blocks)]
    place = [seen[i] + 2 * WB * far[i] for i in range(blocks)]
    for i in range(blocks):
        rank = jnp.int32(0)
        for j in range(blocks):
            if j != i:
                below = place[j] <= place[i] if j < i else place[j] < place[i]
                rank = rank + below.astype(jnp.int32)
        order[rank] = i
        counts[rank] = seen[i]
    near = blocks - functools.reduce(jnp.add, far)
    counts[blocks] = near // TOGETHER
    counts[blocks + 1] = functools.reduce(
        jnp.minimum, [jnp.minimum(i + WB + 1 - seen[i], WB) for i in range(blocks)]
    )


def prepare(chunk_index, doc_ids, band, own):
    blocks = own.shape[0]
    smem = pl.BlockSpec(memory_space=pltpu.SMEM)
    vmem = pl.BlockSpec(memory_space=pltpu.VMEM)
    return pl.pallas_call(
        prepare_kernel,
        in_specs=[smem] * 3 + [vmem],
        out_specs=[smem] * 2 + [vmem],
        out_shape=[
            jax.ShapeDtypeStruct((blocks,), jnp.int32),
            jax.ShapeDtypeStruct((blocks + 2,), jnp.int32),
            jax.ShapeDtypeStruct((HEAD, blocks * BLOCK), own.dtype),
        ],
        compiler_params=pltpu.CompilerParams(vmem_limit_bytes=SMALL),
    )(chunk_index, doc_ids, band, own)


def place_own(own_ref, own_t_ref, kv, keys_t):
    for j in range(own_ref.shape[0]):
        late = slice(WINDOW + j * BLOCK, WINDOW + (j + 1) * BLOCK)
        kv[late, :] = own_ref[j]
        keys_t[:, late] = own_t_ref[:, j * BLOCK : (j + 1) * BLOCK]


def near_kernel(order, counts, qd_ref, own_ref, own_t_ref, dq_ref, sums, kv, keys_t):
    kv[:WINDOW, :] = jnp.zeros((WINDOW, 2 * HEAD), kv.dtype)
    keys_t[:, :WINDOW] = jnp.zeros((HEAD, WINDOW), keys_t.dtype)
    place_own(own_ref, own_t_ref, kv, keys_t)
    sums[...] = jnp.zeros_like(sums)
    last = counts[order.shape[0]]
    attend(0, last, order, counts, qd_ref, kv, keys_t, dq_ref, sums, lambda i: None)


def far_kernel(
    order, counts, qd_ref, halo_ref, dq_near_ref, room_ref, kv_in, keys_t_in, sums_in,
    dq_ref, sums_ref, spill_ref, kv, keys_t, sums, dq_slabs, dq_sems,
):
    del room_ref, kv_in, keys_t_in, sums_in
    blocks = order.shape[0]
    steps = counts[blocks]

    def dq_copy(slabs, i):
        return pltpu.make_async_copy(slabs.at[i], dq_ref.at[i], dq_sems.at[i])

    def pass_on(m, carry):
        dq_copy(dq_near_ref, order[m]).start()
        return carry

    lax.fori_loop(0, steps * TOGETHER, pass_on, 0)

    @pl.when(counts[blocks + 1] < WB)
    def fill():
        for j in range(WB):
            rows = slice(j * BLOCK, (j + 1) * BLOCK)
            kv[rows, :] = halo_ref[j]
            keys_t[:, rows] = halo_ref[j, :, :HEAD].T

    attend(
        steps, blocks // TOGETHER, order, counts, qd_ref, kv, keys_t, dq_slabs, sums,
        lambda i: dq_copy(dq_slabs, i).start(),
    )
    for j in range(WB):
        rows = slice(j * BLOCK, (j + 1) * BLOCK)
        spill_ref[j, :, :HEAD] = (sums[rows, :HEAD] * SCALE).astype(spill_ref.dtype)
        spill_ref[j, :, HEAD:] = sums[rows, HEAD:].astype(spill_ref.dtype)
    sums_ref[...] = sums[WINDOW:, :]
    for i in range(blocks):
        dq_copy(dq_slabs, i).wait()


def attend(first_step, last_step, order, counts, qd_ref, kv, keys_t, dq_slabs, sums, ready):
    q_heads = qd_ref.shape[2] // (2 * HEAD)
    rows = q_heads * BLOCK

    def stacked(i, offset):
        return jnp.concatenate(
            [qd_ref[i, :, (offset + h) * HEAD : (offset + h + 1) * HEAD] for h in range(q_heads)],
            axis=0,
        )

    def fold(x, reduce):
        return reduce(x.reshape(BLOCK // 8, 8, rows), axis=0)

    def work(count, members, sizes):
        span = count * BLOCK
        windows = [
            pl.ds(pl.multiple_of((i + WB + 1 - count) * BLOCK, BLOCK), span) for i in members
        ]
        lanes = range(len(members))

        def split(x):
            return [x[b * BLOCK : (b + 1) * BLOCK] for b in range(count)]

        query = [stacked(i, 0) for i in members]
        grad = [stacked(i, q_heads) for i in members]
        scores = [split(dot(kv[windows[n], :HEAD], query[n], NT)) for n in lanes]
        key_pos = lax.broadcasted_iota(jnp.int32, (BLOCK, rows), 0)
        query_pos = lax.broadcasted_iota(jnp.int32, (BLOCK, rows), 1) % BLOCK
        causal = key_pos <= query_pos
        probs, probs_b, dprob = {}, {}, {}
        for n in lanes:
            scores[n][-1] = jnp.where(causal, scores[n][-1], -jnp.inf)
            seen = [count - b <= sizes[n] for b in range(count)]
            dprob[n] = split(dot(kv[windows[n], HEAD:], grad[n], NT))
            tops, expo, totals = [], [], []
            for x in scores[n]:
                top = jnp.max(fold(x, jnp.max), axis=0, keepdims=True)
                x = jnp.exp2((x - top) * (SCALE * LOG2E))
                tops.append(top)
                expo.append(x)
                totals.append(jnp.sum(fold(x, jnp.sum), axis=0, keepdims=True))
            shown = [jnp.where(y, x, -jnp.inf) for x, y in zip(tops, seen)]
            top = functools.reduce(jnp.maximum, shown)
            parts = [jnp.exp2((x - top) * (SCALE * LOG2E)) for x in shown]
            total = functools.reduce(jnp.add, [x * y for x, y in zip(totals, parts)])
            inverse = 1.0 / total
            probs[n] = [x * (y * inverse) for x, y in zip(expo, parts)]
            probs_b[n] = [x.astype(jnp.bfloat16) for x in probs[n]]
        dscore = {}
        for n in lanes:
            sums[windows[n], HEAD:] += dot(jnp.concatenate(probs_b[n], axis=0), grad[n], NN)
            delta = functools.reduce(
                jnp.add,
                [
                    fold(x.astype(jnp.float32) * y, jnp.sum)
                    for x, y in zip(probs_b[n], dprob[n])
                ],
            )
            delta = jnp.sum(delta, axis=0, keepdims=True)
            dscore[n] = jnp.concatenate(
                [
                    (x * (y - delta)).astype(jnp.bfloat16)
                    for x, y in zip(probs[n], dprob[n])
                ],
                axis=0,
            )
        for n, i in enumerate(members):
            sums[windows[n], :HEAD] += dot(dscore[n], query[n], NN)
            query_grad = dot(keys_t[:, windows[n]], dscore[n], NN) * SCALE
            for h in range(q_heads):
                dq_slabs[i, :, h * HEAD : (h + 1) * HEAD] = query_grad[
                    :, h * BLOCK : (h + 1) * BLOCK
                ].T.astype(dq_slabs.dtype)
            ready(i)

    def one_step(step, carry):
        members = [order[step * TOGETHER + n] for n in range(TOGETHER)]
        sizes = [counts[step * TOGETHER + n] for n in range(TOGETHER)]
        widest = functools.reduce(jnp.maximum, sizes)
        for count in range(1, WB + 2):
            pl.when(widest == count)(functools.partial(work, count, members, sizes))
        return carry

    lax.fori_loop(first_step, last_step, one_step, 0)


def attend_near(order, counts, qd, own, own_t):
    total = WINDOW + own_t.shape[1]
    smem = pl.BlockSpec(memory_space=pltpu.SMEM)
    vmem = pl.BlockSpec(memory_space=pltpu.VMEM)
    return pl.pallas_call(
        near_kernel,
        in_specs=[smem] * 2 + [vmem] * 3,
        out_specs=[vmem] * 4,
        out_shape=[
            jax.ShapeDtypeStruct((*qd.shape[:2], qd.shape[2] // 2), qd.dtype),
            jax.ShapeDtypeStruct((total, 2 * HEAD), jnp.float32),
            jax.ShapeDtypeStruct((total, 2 * HEAD), own.dtype),
            jax.ShapeDtypeStruct((HEAD, total), own.dtype),
        ],
        compiler_params=pltpu.CompilerParams(vmem_limit_bytes=LARGE),
    )(order, counts, qd, own, own_t)


def attend_far(order, counts, qd, halo, dq, room, kv, keys_t, sums):
    smem = pl.BlockSpec(memory_space=pltpu.SMEM)
    vmem = pl.BlockSpec(memory_space=pltpu.VMEM)
    hbm = pl.BlockSpec(memory_space=pl.ANY)
    own_sums = jax.ShapeDtypeStruct((sums.shape[0] - WINDOW, sums.shape[1]), sums.dtype)
    shapes = [jax.ShapeDtypeStruct(x.shape, x.dtype) for x in (dq, halo, kv, keys_t, sums)]
    return pl.pallas_call(
        far_kernel,
        in_specs=[smem] * 2 + [vmem] * 3 + [hbm] + [vmem] * 3,
        out_specs=[hbm] + [vmem] * 5,
        out_shape=[shapes[0], own_sums, *shapes[1:]],
        input_output_aliases={5: 0, 3: 2, 6: 3, 7: 4, 8: 5},
        scratch_shapes=[
            pltpu.VMEM(dq.shape, dq.dtype),
            pltpu.SemaphoreType.DMA(dq.shape[:1]),
        ],
        compiler_params=pltpu.CompilerParams(vmem_limit_bytes=LARGE),
    )(order, counts, qd, halo, dq, room, kv, keys_t, sums)[:3]


def add_kernel(sums_ref, spill_ref, out_ref, slabs, sems):
    copies = []
    for j in range(out_ref.shape[0]):
        late = slice(j * BLOCK, (j + 1) * BLOCK)
        for half, scale in ((slice(0, HEAD), SCALE), (slice(HEAD, 2 * HEAD), 1.0)):
            own = sums_ref[late, half] * scale
            slabs[j, :, half] = (own + spill_ref[j, :, half].astype(jnp.float32)).astype(
                slabs.dtype
            )
        copies.append(pltpu.make_async_copy(slabs.at[j], out_ref.at[j], sems.at[j]))
        copies[j].start()
    for copy in copies:
        copy.wait()


def add_spill(sums, spill):
    return pl.pallas_call(
        add_kernel,
        in_specs=[pl.BlockSpec(memory_space=pltpu.VMEM)] * 2,
        out_specs=pl.BlockSpec(memory_space=pl.ANY),
        out_shape=jax.ShapeDtypeStruct(spill.shape, spill.dtype),
        scratch_shapes=[
            pltpu.VMEM(spill.shape, spill.dtype),
            pltpu.SemaphoreType.DMA((spill.shape[0],)),
        ],
        compiler_params=pltpu.CompilerParams(vmem_limit_bytes=SMALL),
    )(sums, spill)


def per_device(queries, keys, values, upstream, doc_ids, band):
    tokens = queries.shape[0]
    parts = WINDOW // tokens
    cores = lax.axis_size("heads")
    spans = lax.axis_size("blk")
    step = parts // cores
    axes = ("blk", "heads")
    groups = [
        [first * parts + member for member in range(parts)] for first in range(spans // step)
    ]

    def exchange(value):
        return lax.all_to_all(
            value, axes, split_axis=0, concat_axis=0, axis_index_groups=groups, tiled=True
        )

    kv_packed = pack(keys, values, parts)
    kv = exchange(kv_packed)
    halo = lax.ppermute(kv, "blk", [(s, s + step) for s in range(spans - step)])
    qd = exchange(pack(queries, upstream, parts))
    chunk_index = (lax.axis_index("blk") // step).astype(jnp.int32).reshape(1)
    order, counts, own_t = prepare(chunk_index, doc_ids, band, kv)
    dq, sums, rows, rows_t = attend_near(order, counts, qd, kv, own_t)
    dq, sums, spill = attend_far(order, counts, qd, halo, dq, kv_packed, rows, rows_t, sums)
    spill = lax.ppermute(spill, "blk", [(s + step, s) for s in range(spans - step)])
    query_out = exchange(dq)
    dkv = exchange(add_spill(sums, spill))

    return (*unpack(query_out, 1), *unpack(dkv, 2))


def solution(mesh):
    sharded = P(("groups", "blk", "heads"), None)
    return jax.shard_map(
        per_device,
        mesh=mesh,
        in_specs=(sharded,) * 4 + (P("groups"),) * 2,
        out_specs=(sharded,) * 3,
        check_vma=False,
    )
```

```python
import functools
import math

import jax
import jax.numpy as jnp
from jax import lax
from jax.experimental import pallas as pl
from jax.experimental.pallas import tpu as pltpu
from jax.sharding import PartitionSpec as P

HEAD = 128
SCALAR = 168
WINDOW = 1024
BLOCK = 128
WB = WINDOW // BLOCK
SCALE = SCALAR ** (-0.5)
LOG2E = math.log2(math.e)
SMALL = 8 * 1024 * 1024
LARGE = 40 * 1024 * 1024
TOGETHER = 2

NT = (((1,), (1,)), ((), ()))
NN = (((1,), (0,)), ((), ()))


def dot(a, b, dims):
    return lax.dot_general(a, b, dims, preferred_element_type=jnp.float32)


def run_copies(pairs, sems):
    copies = [pltpu.make_async_copy(x, y, sems.at[n]) for n, (x, y) in enumerate(pairs)]
    for copy in copies:
        copy.start()
    for copy in copies:
        copy.wait()


def pack_kernel(a_ref, b_ref, out_ref, slabs, in_sems, out_sems):
    heads = out_ref.shape[0]
    width = out_ref.shape[2] // 2
    reads = [
        [
            pltpu.make_async_copy(
                ref.at[:, pl.ds(h * width, width)],
                slabs.at[h, :, pl.ds(n * width, width)],
                in_sems.at[2 * h + n],
            )
            for n, ref in enumerate((a_ref, b_ref))
        ]
        for h in range(heads)
    ]
    writes = [
        pltpu.make_async_copy(slabs.at[h], out_ref.at[h], out_sems.at[h]) for h in range(heads)
    ]
    for pair in reads:
        for copy in pair:
            copy.start()
    for pair, write in zip(reads, writes):
        for copy in pair:
            copy.wait()
        write.start()
    for write in writes:
        write.wait()


def pack(a, b, heads):
    tokens, cols = a.shape
    hbm = pl.BlockSpec(memory_space=pl.ANY)
    shape = (heads, tokens, 2 * cols // heads)
    return pl.pallas_call(
        pack_kernel,
        in_specs=[hbm] * 2,
        out_specs=hbm,
        out_shape=jax.ShapeDtypeStruct(shape, a.dtype),
        scratch_shapes=[
            pltpu.VMEM(shape, a.dtype),
            pltpu.SemaphoreType.DMA((2 * heads,)),
            pltpu.SemaphoreType.DMA((heads,)),
        ],
    )(a, b)


def unpack_kernel(in_ref, *refs):
    out_refs, sems = refs[:-1], refs[-1]
    width = in_ref.shape[2] // len(out_refs)
    run_copies(
        [
            (in_ref.at[h, :, pl.ds(n * width, width)], ref.at[:, pl.ds(h * width, width)])
            for h in range(in_ref.shape[0])
            for n, ref in enumerate(out_refs)
        ],
        sems,
    )


def unpack(value, outputs):
    heads, tokens, width = value.shape
    shape = jax.ShapeDtypeStruct((tokens, heads * width // outputs), value.dtype)
    return pl.pallas_call(
        unpack_kernel,
        in_specs=[pl.BlockSpec(memory_space=pltpu.VMEM)],
        out_specs=[pl.BlockSpec(memory_space=pl.ANY)] * outputs,
        out_shape=[shape] * outputs,
        scratch_shapes=[pltpu.SemaphoreType.DMA((outputs * heads,))],
        compiler_params=pltpu.CompilerParams(vmem_limit_bytes=SMALL),
    )(value)


def prepare_kernel(chunk_ref, doc_ref, band_ref, own_ref, order, counts, own_t_ref):
    blocks = own_ref.shape[0]
    for j in range(blocks):
        own_t_ref[:, j * BLOCK : (j + 1) * BLOCK] = own_ref[j, :, :HEAD].T
    first = chunk_ref[0] * blocks
    length = jnp.int32(0)
    for back in range(1, WB + 1):
        same = (first >= back) & (doc_ref[jnp.maximum(first - back, 0)] == doc_ref[first])
        length = length + same.astype(jnp.int32)
    seen = []
    for i in range(blocks):
        if i > 0:
            same = doc_ref[first + i] == doc_ref[first + i - 1]
            length = jnp.where(same, length + 1, 0)
        seen.append(jnp.minimum(band_ref[first + i], length) + 1)
    far = [(seen[i] > i + 1).astype(jnp.int32) for i in range(blocks)]
    place = [seen[i] + 2 * WB * far[i] for i in range(blocks)]
    for i in range(blocks):
        rank = jnp.int32(0)
        for j in range(blocks):
            if j != i:
                below = place[j] <= place[i] if j < i else place[j] < place[i]
                rank = rank + below.astype(jnp.int32)
        order[rank] = i
        counts[rank] = seen[i]
    near = blocks - functools.reduce(jnp.add, far)
    counts[blocks] = near // TOGETHER
    counts[blocks + 1] = functools.reduce(
        jnp.minimum, [jnp.minimum(i + WB + 1 - seen[i], WB) for i in range(blocks)]
    )


def prepare(chunk_index, doc_ids, band, own):
    blocks = own.shape[0]
    smem = pl.BlockSpec(memory_space=pltpu.SMEM)
    vmem = pl.BlockSpec(memory_space=pltpu.VMEM)
    return pl.pallas_call(
        prepare_kernel,
        in_specs=[smem] * 3 + [vmem],
        out_specs=[smem] * 2 + [vmem],
        out_shape=[
            jax.ShapeDtypeStruct((blocks,), jnp.int32),
            jax.ShapeDtypeStruct((blocks + 2,), jnp.int32),
            jax.ShapeDtypeStruct((HEAD, blocks * BLOCK), own.dtype),
        ],
        compiler_params=pltpu.CompilerParams(vmem_limit_bytes=SMALL),
    )(chunk_index, doc_ids, band, own)


def place_own(own_ref, own_t_ref, kv, keys_t):
    for j in range(own_ref.shape[0]):
        late = slice(WINDOW + j * BLOCK, WINDOW + (j + 1) * BLOCK)
        kv[late, :] = own_ref[j]
        keys_t[:, late] = own_t_ref[:, j * BLOCK : (j + 1) * BLOCK]


def near_kernel(order, counts, qd_ref, own_ref, own_t_ref, dq_ref, sums, kv, keys_t):
    kv[:WINDOW, :] = jnp.zeros((WINDOW, 2 * HEAD), kv.dtype)
    keys_t[:, :WINDOW] = jnp.zeros((HEAD, WINDOW), keys_t.dtype)
    place_own(own_ref, own_t_ref, kv, keys_t)
    sums[...] = jnp.zeros_like(sums)
    last = counts[order.shape[0]]
    attend(0, last, order, counts, qd_ref, kv, keys_t, dq_ref, sums, lambda i: None)


def far_kernel(
    order, counts, qd_ref, halo_ref, dq_near_ref, room_ref, kv_in, keys_t_in, sums_in,
    dq_ref, sums_ref, spill_ref, kv, keys_t, sums, dq_slabs, dq_sems,
):
    del room_ref, kv_in, keys_t_in, sums_in
    blocks = order.shape[0]
    steps = counts[blocks]

    def dq_copy(slabs, i):
        return pltpu.make_async_copy(slabs.at[i], dq_ref.at[i], dq_sems.at[i])

    def pass_on(m, carry):
        dq_copy(dq_near_ref, order[m]).start()
        return carry

    lax.fori_loop(0, steps * TOGETHER, pass_on, 0)

    @pl.when(counts[blocks + 1] < WB)
    def fill():
        for j in range(WB):
            rows = slice(j * BLOCK, (j + 1) * BLOCK)
            kv[rows, :] = halo_ref[j]
            keys_t[:, rows] = halo_ref[j, :, :HEAD].T

    attend(
        steps, blocks // TOGETHER, order, counts, qd_ref, kv, keys_t, dq_slabs, sums,
        lambda i: dq_copy(dq_slabs, i).start(),
    )
    for j in range(WB):
        rows = slice(j * BLOCK, (j + 1) * BLOCK)
        spill_ref[j, :, :HEAD] = (sums[rows, :HEAD] * SCALE).astype(spill_ref.dtype)
        spill_ref[j, :, HEAD:] = sums[rows, HEAD:].astype(spill_ref.dtype)
    sums_ref[...] = sums[WINDOW:, :]
    for i in range(blocks):
        dq_copy(dq_slabs, i).wait()


def attend(first_step, last_step, order, counts, qd_ref, kv, keys_t, dq_slabs, sums, ready):
    q_heads = qd_ref.shape[2] // (2 * HEAD)
    rows = q_heads * BLOCK

    def stacked(i, offset):
        return jnp.concatenate(
            [qd_ref[i, :, (offset + h) * HEAD : (offset + h + 1) * HEAD] for h in range(q_heads)],
            axis=0,
        )

    def fold(x, reduce):
        return reduce(x.reshape(BLOCK // 8, 8, rows), axis=0)

    def work(count, members, sizes):
        span = count * BLOCK
        windows = [
            pl.ds(pl.multiple_of((i + WB + 1 - count) * BLOCK, BLOCK), span) for i in members
        ]
        lanes = range(len(members))

        def split(x):
            return [x[b * BLOCK : (b + 1) * BLOCK] for b in range(count)]

        query = [stacked(i, 0) for i in members]
        grad = [stacked(i, q_heads) for i in members]
        scores = [split(dot(kv[windows[n], :HEAD], query[n], NT)) for n in lanes]
        key_pos = lax.broadcasted_iota(jnp.int32, (BLOCK, rows), 0)
        query_pos = lax.broadcasted_iota(jnp.int32, (BLOCK, rows), 1) % BLOCK
        causal = key_pos <= query_pos
        probs, probs_b, dprob = {}, {}, {}
        for n in lanes:
            scores[n][-1] = jnp.where(causal, scores[n][-1], -jnp.inf)
            seen = [count - b <= sizes[n] for b in range(count)]
            dprob[n] = split(dot(kv[windows[n], HEAD:], grad[n], NT))
            tops, expo, totals = [], [], []
            for x in scores[n]:
                top = jnp.max(fold(x, jnp.max), axis=0, keepdims=True)
                x = jnp.exp2((x - top) * (SCALE * LOG2E))
                tops.append(top)
                expo.append(x)
                totals.append(jnp.sum(fold(x, jnp.sum), axis=0, keepdims=True))
            shown = [jnp.where(y, x, -jnp.inf) for x, y in zip(tops, seen)]
            top = functools.reduce(jnp.maximum, shown)
            parts = [jnp.exp2((x - top) * (SCALE * LOG2E)) for x in shown]
            total = functools.reduce(jnp.add, [x * y for x, y in zip(totals, parts)])
            inverse = 1.0 / total
            probs[n] = [x * (y * inverse) for x, y in zip(expo, parts)]
            probs_b[n] = [x.astype(jnp.bfloat16) for x in probs[n]]
        dscore = {}
        for n in lanes:
            sums[windows[n], HEAD:] += dot(jnp.concatenate(probs_b[n], axis=0), grad[n], NN)
            delta = functools.reduce(
                jnp.add,
                [
                    fold(x.astype(jnp.float32) * y, jnp.sum)
                    for x, y in zip(probs_b[n], dprob[n])
                ],
            )
            delta = jnp.sum(delta, axis=0, keepdims=True)
            dscore[n] = jnp.concatenate(
                [
                    (x * (y - delta)).astype(jnp.bfloat16)
                    for x, y in zip(probs[n], dprob[n])
                ],
                axis=0,
            )
        for n, i in enumerate(members):
            sums[windows[n], :HEAD] += dot(dscore[n], query[n], NN)
            query_grad = dot(keys_t[:, windows[n]], dscore[n], NN) * SCALE
            query_grad = query_grad.astype(dq_slabs.dtype)
            for h in range(q_heads):
                dq_slabs[i, :, h * HEAD : (h + 1) * HEAD] = query_grad[
                    :, h * BLOCK : (h + 1) * BLOCK
                ].T
        for i in members:
            ready(i)

    def one_step(step, carry):
        members = [order[step * TOGETHER + n] for n in range(TOGETHER)]
        sizes = [counts[step * TOGETHER + n] for n in range(TOGETHER)]
        widest = functools.reduce(jnp.maximum, sizes)
        for count in range(1, WB + 2):
            pl.when(widest == count)(functools.partial(work, count, members, sizes))
        return carry

    lax.fori_loop(first_step, last_step, one_step, 0)


def attend_near(order, counts, qd, own, own_t):
    total = WINDOW + own_t.shape[1]
    smem = pl.BlockSpec(memory_space=pltpu.SMEM)
    vmem = pl.BlockSpec(memory_space=pltpu.VMEM)
    return pl.pallas_call(
        near_kernel,
        in_specs=[smem] * 2 + [vmem] * 3,
        out_specs=[vmem] * 4,
        out_shape=[
            jax.ShapeDtypeStruct((*qd.shape[:2], qd.shape[2] // 2), qd.dtype),
            jax.ShapeDtypeStruct((total, 2 * HEAD), jnp.float32),
            jax.ShapeDtypeStruct((total, 2 * HEAD), own.dtype),
            jax.ShapeDtypeStruct((HEAD, total), own.dtype),
        ],
        compiler_params=pltpu.CompilerParams(vmem_limit_bytes=LARGE),
    )(order, counts, qd, own, own_t)


def attend_far(order, counts, qd, halo, dq, room, kv, keys_t, sums):
    smem = pl.BlockSpec(memory_space=pltpu.SMEM)
    vmem = pl.BlockSpec(memory_space=pltpu.VMEM)
    hbm = pl.BlockSpec(memory_space=pl.ANY)
    own_sums = jax.ShapeDtypeStruct((sums.shape[0] - WINDOW, sums.shape[1]), sums.dtype)
    shapes = [jax.ShapeDtypeStruct(x.shape, x.dtype) for x in (dq, halo, kv, keys_t, sums)]
    return pl.pallas_call(
        far_kernel,
        in_specs=[smem] * 2 + [vmem] * 3 + [hbm] + [vmem] * 3,
        out_specs=[hbm] + [vmem] * 5,
        out_shape=[shapes[0], own_sums, *shapes[1:]],
        input_output_aliases={5: 0, 3: 2, 6: 3, 7: 4, 8: 5},
        scratch_shapes=[
            pltpu.VMEM(dq.shape, dq.dtype),
            pltpu.SemaphoreType.DMA(dq.shape[:1]),
        ],
        compiler_params=pltpu.CompilerParams(vmem_limit_bytes=LARGE),
    )(order, counts, qd, halo, dq, room, kv, keys_t, sums)[:3]


def add_kernel(sums_ref, spill_ref, out_ref, slabs, sems):
    copies = []
    for j in range(out_ref.shape[0]):
        late = slice(j * BLOCK, (j + 1) * BLOCK)
        for half, scale in ((slice(0, HEAD), SCALE), (slice(HEAD, 2 * HEAD), 1.0)):
            own = sums_ref[late, half] * scale
            slabs[j, :, half] = (own + spill_ref[j, :, half].astype(jnp.float32)).astype(
                slabs.dtype
            )
        copies.append(pltpu.make_async_copy(slabs.at[j], out_ref.at[j], sems.at[j]))
        copies[j].start()
    for copy in copies:
        copy.wait()


def add_spill(sums, spill):
    return pl.pallas_call(
        add_kernel,
        in_specs=[pl.BlockSpec(memory_space=pltpu.VMEM)] * 2,
        out_specs=pl.BlockSpec(memory_space=pl.ANY),
        out_shape=jax.ShapeDtypeStruct(spill.shape, spill.dtype),
        scratch_shapes=[
            pltpu.VMEM(spill.shape, spill.dtype),
            pltpu.SemaphoreType.DMA((spill.shape[0],)),
        ],
        compiler_params=pltpu.CompilerParams(vmem_limit_bytes=SMALL),
    )(sums, spill)


def per_device(queries, keys, values, upstream, doc_ids, band):
    tokens = queries.shape[0]
    parts = WINDOW // tokens
    cores = lax.axis_size("heads")
    spans = lax.axis_size("blk")
    step = parts // cores
    axes = ("blk", "heads")
    groups = [
        [first * parts + member for member in range(parts)] for first in range(spans // step)
    ]

    def exchange(value):
        return lax.all_to_all(
            value, axes, split_axis=0, concat_axis=0, axis_index_groups=groups, tiled=True
        )

    kv_packed = pack(keys, values, parts)
    kv = exchange(kv_packed)
    halo = lax.ppermute(kv, "blk", [(s, s + step) for s in range(spans - step)])
    qd = exchange(pack(queries, upstream, parts))
    chunk_index = (lax.axis_index("blk") // step).astype(jnp.int32).reshape(1)
    order, counts, own_t = prepare(chunk_index, doc_ids, band, kv)
    dq, sums, rows, rows_t = attend_near(order, counts, qd, kv, own_t)
    dq, sums, spill = attend_far(order, counts, qd, halo, dq, kv_packed, rows, rows_t, sums)
    spill = lax.ppermute(spill, "blk", [(s + step, s) for s in range(spans - step)])
    query_out = exchange(dq)
    dkv = exchange(add_spill(sums, spill))

    return (*unpack(query_out, 1), *unpack(dkv, 2))


def solution(mesh):
    sharded = P(("groups", "blk", "heads"), None)
    return jax.shard_map(
        per_device,
        mesh=mesh,
        in_specs=(sharded,) * 4 + (P("groups"),) * 2,
        out_specs=(sharded,) * 3,
        check_vma=False,
    )
```

```python
import functools
import math

import jax
import jax.numpy as jnp
from jax import lax
from jax.experimental import pallas as pl
from jax.experimental.pallas import tpu as pltpu
from jax.sharding import PartitionSpec as P

HEAD = 128
SCALAR = 168
WINDOW = 1024
BLOCK = 128
WB = WINDOW // BLOCK
SCALE = SCALAR ** (-0.5)
LOG2E = math.log2(math.e)
SMALL = 8 * 1024 * 1024
LARGE = 40 * 1024 * 1024
TOGETHER = 2

NT = (((1,), (1,)), ((), ()))
NN = (((1,), (0,)), ((), ()))


def dot(a, b, dims):
    return lax.dot_general(a, b, dims, preferred_element_type=jnp.float32)


def run_copies(pairs, sems):
    copies = [pltpu.make_async_copy(x, y, sems.at[n]) for n, (x, y) in enumerate(pairs)]
    for copy in copies:
        copy.start()
    for copy in copies:
        copy.wait()


def pack_kernel(a_ref, b_ref, out_ref, slabs, in_sems, out_sems):
    heads = out_ref.shape[0]
    width = out_ref.shape[2] // 2
    reads = [
        [
            pltpu.make_async_copy(
                ref.at[:, pl.ds(h * width, width)],
                slabs.at[h, :, pl.ds(n * width, width)],
                in_sems.at[2 * h + n],
            )
            for n, ref in enumerate((a_ref, b_ref))
        ]
        for h in range(heads)
    ]
    writes = [
        pltpu.make_async_copy(slabs.at[h], out_ref.at[h], out_sems.at[h]) for h in range(heads)
    ]
    for pair in reads:
        for copy in pair:
            copy.start()
    for pair, write in zip(reads, writes):
        for copy in pair:
            copy.wait()
        write.start()
    for write in writes:
        write.wait()


def pack(a, b, heads):
    tokens, cols = a.shape
    hbm = pl.BlockSpec(memory_space=pl.ANY)
    shape = (heads, tokens, 2 * cols // heads)
    return pl.pallas_call(
        pack_kernel,
        in_specs=[hbm] * 2,
        out_specs=hbm,
        out_shape=jax.ShapeDtypeStruct(shape, a.dtype),
        scratch_shapes=[
            pltpu.VMEM(shape, a.dtype),
            pltpu.SemaphoreType.DMA((2 * heads,)),
            pltpu.SemaphoreType.DMA((heads,)),
        ],
    )(a, b)


def unpack_kernel(in_ref, *refs):
    out_refs, sems = refs[:-1], refs[-1]
    width = in_ref.shape[2] // len(out_refs)
    run_copies(
        [
            (in_ref.at[h, :, pl.ds(n * width, width)], ref.at[:, pl.ds(h * width, width)])
            for h in range(in_ref.shape[0])
            for n, ref in enumerate(out_refs)
        ],
        sems,
    )


def unpack(value, outputs):
    heads, tokens, width = value.shape
    shape = jax.ShapeDtypeStruct((tokens, heads * width // outputs), value.dtype)
    return pl.pallas_call(
        unpack_kernel,
        in_specs=[pl.BlockSpec(memory_space=pltpu.VMEM)],
        out_specs=[pl.BlockSpec(memory_space=pl.ANY)] * outputs,
        out_shape=[shape] * outputs,
        scratch_shapes=[pltpu.SemaphoreType.DMA((outputs * heads,))],
        compiler_params=pltpu.CompilerParams(vmem_limit_bytes=SMALL),
    )(value)


def prepare_kernel(chunk_ref, doc_ref, band_ref, own_ref, order, counts, own_t_ref):
    blocks = own_ref.shape[0]
    for j in range(blocks):
        own_t_ref[:, j * BLOCK : (j + 1) * BLOCK] = own_ref[j, :, :HEAD].T
    first = chunk_ref[0] * blocks
    length = jnp.int32(0)
    for back in range(1, WB + 1):
        same = (first >= back) & (doc_ref[jnp.maximum(first - back, 0)] == doc_ref[first])
        length = length + same.astype(jnp.int32)
    seen = []
    for i in range(blocks):
        if i > 0:
            same = doc_ref[first + i] == doc_ref[first + i - 1]
            length = jnp.where(same, length + 1, 0)
        seen.append(jnp.minimum(band_ref[first + i], length) + 1)
    far = [(seen[i] > i + 1).astype(jnp.int32) for i in range(blocks)]
    place = [seen[i] + 2 * WB * far[i] for i in range(blocks)]
    for i in range(blocks):
        rank = jnp.int32(0)
        for j in range(blocks):
            if j != i:
                below = place[j] <= place[i] if j < i else place[j] < place[i]
                rank = rank + below.astype(jnp.int32)
        order[rank] = i
        counts[rank] = seen[i]
    near = blocks - functools.reduce(jnp.add, far)
    counts[blocks] = near // TOGETHER
    counts[blocks + 1] = functools.reduce(
        jnp.minimum, [jnp.minimum(i + WB + 1 - seen[i], WB) for i in range(blocks)]
    )


def prepare(chunk_index, doc_ids, band, own):
    blocks = own.shape[0]
    smem = pl.BlockSpec(memory_space=pltpu.SMEM)
    vmem = pl.BlockSpec(memory_space=pltpu.VMEM)
    return pl.pallas_call(
        prepare_kernel,
        in_specs=[smem] * 3 + [vmem],
        out_specs=[smem] * 2 + [vmem],
        out_shape=[
            jax.ShapeDtypeStruct((blocks,), jnp.int32),
            jax.ShapeDtypeStruct((blocks + 2,), jnp.int32),
            jax.ShapeDtypeStruct((HEAD, blocks * BLOCK), own.dtype),
        ],
        compiler_params=pltpu.CompilerParams(vmem_limit_bytes=SMALL),
    )(chunk_index, doc_ids, band, own)


def place_own(own_ref, own_t_ref, kv, keys_t):
    for j in range(own_ref.shape[0]):
        late = slice(WINDOW + j * BLOCK, WINDOW + (j + 1) * BLOCK)
        kv[late, :] = own_ref[j]
        keys_t[:, late] = own_t_ref[:, j * BLOCK : (j + 1) * BLOCK]


def near_kernel(order, counts, qd_ref, own_ref, own_t_ref, dq_ref, sums, kv, keys_t):
    kv[:WINDOW, :] = jnp.zeros((WINDOW, 2 * HEAD), kv.dtype)
    keys_t[:, :WINDOW] = jnp.zeros((HEAD, WINDOW), keys_t.dtype)
    place_own(own_ref, own_t_ref, kv, keys_t)
    sums[...] = jnp.zeros_like(sums)
    last = counts[order.shape[0]]
    attend(0, last, order, counts, qd_ref, kv, keys_t, dq_ref, sums, lambda i: None)


def far_kernel(
    order, counts, qd_ref, halo_ref, dq_near_ref, room_ref, kv_in, keys_t_in, sums_in,
    dq_ref, sums_ref, spill_ref, kv, keys_t, sums, dq_slabs, dq_sems,
):
    del room_ref, kv_in, keys_t_in, sums_in
    blocks = order.shape[0]
    steps = counts[blocks]

    def dq_copy(slabs, i):
        return pltpu.make_async_copy(slabs.at[i], dq_ref.at[i], dq_sems.at[i])

    def pass_on(m, carry):
        dq_copy(dq_near_ref, order[m]).start()
        return carry

    lax.fori_loop(0, steps * TOGETHER, pass_on, 0)

    @pl.when(counts[blocks + 1] < WB)
    def fill():
        for j in range(WB):
            rows = slice(j * BLOCK, (j + 1) * BLOCK)
            kv[rows, :] = halo_ref[j]
            keys_t[:, rows] = halo_ref[j, :, :HEAD].T

    attend(
        steps, blocks // TOGETHER, order, counts, qd_ref, kv, keys_t, dq_slabs, sums,
        lambda i: dq_copy(dq_slabs, i).start(),
    )
    for j in range(WB):
        rows = slice(j * BLOCK, (j + 1) * BLOCK)
        spill_ref[j, :, :HEAD] = (sums[rows, :HEAD] * SCALE).astype(spill_ref.dtype)
        spill_ref[j, :, HEAD:] = sums[rows, HEAD:].astype(spill_ref.dtype)
    sums_ref[...] = sums[WINDOW:, :]
    for i in range(blocks):
        dq_copy(dq_slabs, i).wait()


def attend(first_step, last_step, order, counts, qd_ref, kv, keys_t, dq_slabs, sums, ready):
    q_heads = qd_ref.shape[2] // (2 * HEAD)
    rows = q_heads * BLOCK

    def stacked(i, offset):
        return jnp.concatenate(
            [qd_ref[i, :, (offset + h) * HEAD : (offset + h + 1) * HEAD] for h in range(q_heads)],
            axis=0,
        )

    def fold(x, reduce):
        return reduce(x.reshape(BLOCK // 8, 8, rows), axis=0)

    def work(count, members, sizes):
        span = count * BLOCK
        windows = [
            pl.ds(pl.multiple_of((i + WB + 1 - count) * BLOCK, BLOCK), span) for i in members
        ]
        lanes = range(len(members))

        def split(x):
            return [x[b * BLOCK : (b + 1) * BLOCK] for b in range(count)]

        query = [stacked(i, 0) for i in members]
        grad = [stacked(i, q_heads) for i in members]
        scores = [split(dot(kv[windows[n], :HEAD], query[n], NT)) for n in lanes]
        key_pos = lax.broadcasted_iota(jnp.int32, (BLOCK, rows), 0)
        query_pos = lax.broadcasted_iota(jnp.int32, (BLOCK, rows), 1) % BLOCK
        causal = key_pos <= query_pos
        probs, probs_b, dprob = {}, {}, {}
        for n in lanes:
            scores[n][-1] = jnp.where(causal, scores[n][-1], -jnp.inf)
            seen = [count - b <= sizes[n] for b in range(count)]
            tops, expo, totals = [], [], []
            for x in scores[n]:
                top = jnp.max(fold(x, jnp.max), axis=0, keepdims=True)
                x = jnp.exp2((x - top) * (SCALE * LOG2E))
                tops.append(top)
                expo.append(x)
                totals.append(jnp.sum(fold(x, jnp.sum), axis=0, keepdims=True))
            shown = [jnp.where(y, x, -jnp.inf) for x, y in zip(tops, seen)]
            top = functools.reduce(jnp.maximum, shown)
            parts = [jnp.exp2((x - top) * (SCALE * LOG2E)) for x in shown]
            total = functools.reduce(jnp.add, [x * y for x, y in zip(totals, parts)])
            inverse = 1.0 / total
            probs[n] = [x * (y * inverse) for x, y in zip(expo, parts)]
            probs_b[n] = [x.astype(jnp.bfloat16) for x in probs[n]]
        dscore = {}
        for n in lanes:
            dprob[n] = split(dot(kv[windows[n], HEAD:], grad[n], NT))
            sums[windows[n], HEAD:] += dot(jnp.concatenate(probs_b[n], axis=0), grad[n], NN)
            delta = functools.reduce(
                jnp.add,
                [
                    fold(x.astype(jnp.float32) * y, jnp.sum)
                    for x, y in zip(probs_b[n], dprob[n])
                ],
            )
            delta = jnp.sum(delta, axis=0, keepdims=True)
            dscore[n] = jnp.concatenate(
                [
                    (x * (y - delta)).astype(jnp.bfloat16)
                    for x, y in zip(probs[n], dprob[n])
                ],
                axis=0,
            )
        for n, i in enumerate(members):
            sums[windows[n], :HEAD] += dot(dscore[n], query[n], NN)
            query_grad = dot(keys_t[:, windows[n]], dscore[n], NN) * SCALE
            query_grad = query_grad.astype(dq_slabs.dtype)
            for h in range(q_heads):
                dq_slabs[i, :, h * HEAD : (h + 1) * HEAD] = query_grad[
                    :, h * BLOCK : (h + 1) * BLOCK
                ].T
        for i in members:
            ready(i)

    def one_step(step, carry):
        members = [order[step * TOGETHER + n] for n in range(TOGETHER)]
        sizes = [counts[step * TOGETHER + n] for n in range(TOGETHER)]
        widest = functools.reduce(jnp.maximum, sizes)
        for count in range(1, WB + 2):
            pl.when(widest == count)(functools.partial(work, count, members, sizes))
        return carry

    lax.fori_loop(first_step, last_step, one_step, 0)


def attend_near(order, counts, qd, own, own_t):
    total = WINDOW + own_t.shape[1]
    smem = pl.BlockSpec(memory_space=pltpu.SMEM)
    vmem = pl.BlockSpec(memory_space=pltpu.VMEM)
    return pl.pallas_call(
        near_kernel,
        in_specs=[smem] * 2 + [vmem] * 3,
        out_specs=[vmem] * 4,
        out_shape=[
            jax.ShapeDtypeStruct((*qd.shape[:2], qd.shape[2] // 2), qd.dtype),
            jax.ShapeDtypeStruct((total, 2 * HEAD), jnp.float32),
            jax.ShapeDtypeStruct((total, 2 * HEAD), own.dtype),
            jax.ShapeDtypeStruct((HEAD, total), own.dtype),
        ],
        compiler_params=pltpu.CompilerParams(vmem_limit_bytes=LARGE),
    )(order, counts, qd, own, own_t)


def attend_far(order, counts, qd, halo, dq, room, kv, keys_t, sums):
    smem = pl.BlockSpec(memory_space=pltpu.SMEM)
    vmem = pl.BlockSpec(memory_space=pltpu.VMEM)
    hbm = pl.BlockSpec(memory_space=pl.ANY)
    own_sums = jax.ShapeDtypeStruct((sums.shape[0] - WINDOW, sums.shape[1]), sums.dtype)
    shapes = [jax.ShapeDtypeStruct(x.shape, x.dtype) for x in (dq, halo, kv, keys_t, sums)]
    return pl.pallas_call(
        far_kernel,
        in_specs=[smem] * 2 + [vmem] * 3 + [hbm] + [vmem] * 3,
        out_specs=[hbm] + [vmem] * 5,
        out_shape=[shapes[0], own_sums, *shapes[1:]],
        input_output_aliases={5: 0, 3: 2, 6: 3, 7: 4, 8: 5},
        scratch_shapes=[
            pltpu.VMEM(dq.shape, dq.dtype),
            pltpu.SemaphoreType.DMA(dq.shape[:1]),
        ],
        compiler_params=pltpu.CompilerParams(vmem_limit_bytes=LARGE),
    )(order, counts, qd, halo, dq, room, kv, keys_t, sums)[:3]


def add_kernel(sums_ref, spill_ref, out_ref, slabs, sems):
    copies = []
    for j in range(out_ref.shape[0]):
        late = slice(j * BLOCK, (j + 1) * BLOCK)
        for half, scale in ((slice(0, HEAD), SCALE), (slice(HEAD, 2 * HEAD), 1.0)):
            own = sums_ref[late, half] * scale
            slabs[j, :, half] = (own + spill_ref[j, :, half].astype(jnp.float32)).astype(
                slabs.dtype
            )
        copies.append(pltpu.make_async_copy(slabs.at[j], out_ref.at[j], sems.at[j]))
        copies[j].start()
    for copy in copies:
        copy.wait()


def add_spill(sums, spill):
    return pl.pallas_call(
        add_kernel,
        in_specs=[pl.BlockSpec(memory_space=pltpu.VMEM)] * 2,
        out_specs=pl.BlockSpec(memory_space=pl.ANY),
        out_shape=jax.ShapeDtypeStruct(spill.shape, spill.dtype),
        scratch_shapes=[
            pltpu.VMEM(spill.shape, spill.dtype),
            pltpu.SemaphoreType.DMA((spill.shape[0],)),
        ],
        compiler_params=pltpu.CompilerParams(vmem_limit_bytes=SMALL),
    )(sums, spill)


def per_device(queries, keys, values, upstream, doc_ids, band):
    tokens = queries.shape[0]
    parts = WINDOW // tokens
    cores = lax.axis_size("heads")
    spans = lax.axis_size("blk")
    step = parts // cores
    axes = ("blk", "heads")
    groups = [
        [first * parts + member for member in range(parts)] for first in range(spans // step)
    ]

    def exchange(value):
        return lax.all_to_all(
            value, axes, split_axis=0, concat_axis=0, axis_index_groups=groups, tiled=True
        )

    kv_packed = pack(keys, values, parts)
    kv = exchange(kv_packed)
    halo = lax.ppermute(kv, "blk", [(s, s + step) for s in range(spans - step)])
    qd = exchange(pack(queries, upstream, parts))
    chunk_index = (lax.axis_index("blk") // step).astype(jnp.int32).reshape(1)
    order, counts, own_t = prepare(chunk_index, doc_ids, band, kv)
    dq, sums, rows, rows_t = attend_near(order, counts, qd, kv, own_t)
    dq, sums, spill = attend_far(order, counts, qd, halo, dq, kv_packed, rows, rows_t, sums)
    spill = lax.ppermute(spill, "blk", [(s + step, s) for s in range(spans - step)])
    query_out = exchange(dq)
    dkv = exchange(add_spill(sums, spill))

    return (*unpack(query_out, 1), *unpack(dkv, 2))


def solution(mesh):
    sharded = P(("groups", "blk", "heads"), None)
    return jax.shard_map(
        per_device,
        mesh=mesh,
        in_specs=(sharded,) * 4 + (P("groups"),) * 2,
        out_specs=(sharded,) * 3,
        check_vma=False,
    )
```

```python
import functools
import math

import jax
import jax.numpy as jnp
from jax import lax
from jax.experimental import pallas as pl
from jax.experimental.pallas import tpu as pltpu
from jax.sharding import PartitionSpec as P

HEAD = 128
SCALAR = 168
WINDOW = 1024
BLOCK = 128
WB = WINDOW // BLOCK
SCALE = SCALAR ** (-0.5)
LOG2E = math.log2(math.e)
SMALL = 8 * 1024 * 1024
LARGE = 40 * 1024 * 1024
TOGETHER = 2
CHUNKS = 4

NT = (((1,), (1,)), ((), ()))
NN = (((1,), (0,)), ((), ()))


def dot(a, b, dims):
    return lax.dot_general(a, b, dims, preferred_element_type=jnp.float32)


def run_copies(pairs, sems):
    copies = [pltpu.make_async_copy(x, y, sems.at[n]) for n, (x, y) in enumerate(pairs)]
    for copy in copies:
        copy.start()
    for copy in copies:
        copy.wait()


def pack_kernel(a_ref, b_ref, out_ref, a_rows, b_rows, slabs, in_sems, out_sems):
    heads, tokens = out_ref.shape[:2]
    width = out_ref.shape[2] // 2
    size = tokens // CHUNKS
    chunks = [pl.ds(c * size, size) for c in range(CHUNKS)]
    sides = ((a_ref, a_rows), (b_ref, b_rows))
    reads = [
        [
            pltpu.make_async_copy(ref.at[rows], held.at[rows], in_sems.at[2 * c + n])
            for n, (ref, held) in enumerate(sides)
        ]
        for c, rows in enumerate(chunks)
    ]
    writes = [
        pltpu.make_async_copy(slabs.at[:, rows], out_ref.at[:, rows], out_sems.at[c])
        for c, rows in enumerate(chunks)
    ]
    for pair in reads:
        for copy in pair:
            copy.start()
    for rows, pair, write in zip(chunks, reads, writes):
        for copy in pair:
            copy.wait()
        for h in range(heads):
            for n, (_, held) in enumerate(sides):
                slabs[h, rows, n * width : (n + 1) * width] = held[
                    rows, h * width : (h + 1) * width
                ]
        write.start()
    for write in writes:
        write.wait()


def pack(a, b, heads):
    tokens, cols = a.shape
    hbm = pl.BlockSpec(memory_space=pl.ANY)
    shape = (heads, tokens, 2 * cols // heads)
    return pl.pallas_call(
        pack_kernel,
        in_specs=[hbm] * 2,
        out_specs=hbm,
        out_shape=jax.ShapeDtypeStruct(shape, a.dtype),
        scratch_shapes=[
            pltpu.VMEM(a.shape, a.dtype),
            pltpu.VMEM(b.shape, b.dtype),
            pltpu.VMEM(shape, a.dtype),
            pltpu.SemaphoreType.DMA((2 * CHUNKS,)),
            pltpu.SemaphoreType.DMA((CHUNKS,)),
        ],
    )(a, b)


def unpack_kernel(in_ref, *refs):
    out_refs, sems = refs[:-1], refs[-1]
    width = in_ref.shape[2] // len(out_refs)
    run_copies(
        [
            (in_ref.at[h, :, pl.ds(n * width, width)], ref.at[:, pl.ds(h * width, width)])
            for h in range(in_ref.shape[0])
            for n, ref in enumerate(out_refs)
        ],
        sems,
    )


def unpack(value, outputs):
    heads, tokens, width = value.shape
    shape = jax.ShapeDtypeStruct((tokens, heads * width // outputs), value.dtype)
    return pl.pallas_call(
        unpack_kernel,
        in_specs=[pl.BlockSpec(memory_space=pltpu.VMEM)],
        out_specs=[pl.BlockSpec(memory_space=pl.ANY)] * outputs,
        out_shape=[shape] * outputs,
        scratch_shapes=[pltpu.SemaphoreType.DMA((outputs * heads,))],
        compiler_params=pltpu.CompilerParams(vmem_limit_bytes=SMALL),
    )(value)


def prepare_kernel(chunk_ref, doc_ref, band_ref, own_ref, order, counts, own_t_ref):
    blocks = own_ref.shape[0]
    for j in range(blocks):
        own_t_ref[:, j * BLOCK : (j + 1) * BLOCK] = own_ref[j, :, :HEAD].T
    first = chunk_ref[0] * blocks
    length = jnp.int32(0)
    for back in range(1, WB + 1):
        same = (first >= back) & (doc_ref[jnp.maximum(first - back, 0)] == doc_ref[first])
        length = length + same.astype(jnp.int32)
    seen = []
    for i in range(blocks):
        if i > 0:
            same = doc_ref[first + i] == doc_ref[first + i - 1]
            length = jnp.where(same, length + 1, 0)
        seen.append(jnp.minimum(band_ref[first + i], length) + 1)
    far = [(seen[i] > i + 1).astype(jnp.int32) for i in range(blocks)]
    place = [seen[i] + 2 * WB * far[i] for i in range(blocks)]
    for i in range(blocks):
        rank = jnp.int32(0)
        for j in range(blocks):
            if j != i:
                below = place[j] <= place[i] if j < i else place[j] < place[i]
                rank = rank + below.astype(jnp.int32)
        order[rank] = i
        counts[rank] = seen[i]
    near = blocks - functools.reduce(jnp.add, far)
    counts[blocks] = near // TOGETHER
    counts[blocks + 1] = functools.reduce(
        jnp.minimum, [jnp.minimum(i + WB + 1 - seen[i], WB) for i in range(blocks)]
    )


def prepare(chunk_index, doc_ids, band, own):
    blocks = own.shape[0]
    smem = pl.BlockSpec(memory_space=pltpu.SMEM)
    vmem = pl.BlockSpec(memory_space=pltpu.VMEM)
    return pl.pallas_call(
        prepare_kernel,
        in_specs=[smem] * 3 + [vmem],
        out_specs=[smem] * 2 + [vmem],
        out_shape=[
            jax.ShapeDtypeStruct((blocks,), jnp.int32),
            jax.ShapeDtypeStruct((blocks + 2,), jnp.int32),
            jax.ShapeDtypeStruct((HEAD, blocks * BLOCK), own.dtype),
        ],
        compiler_params=pltpu.CompilerParams(vmem_limit_bytes=SMALL),
    )(chunk_index, doc_ids, band, own)


def place_own(own_ref, own_t_ref, kv, keys_t):
    for j in range(own_ref.shape[0]):
        late = slice(WINDOW + j * BLOCK, WINDOW + (j + 1) * BLOCK)
        kv[late, :] = own_ref[j]
        keys_t[:, late] = own_t_ref[:, j * BLOCK : (j + 1) * BLOCK]


def near_kernel(order, counts, qd_ref, own_ref, own_t_ref, dq_ref, sums, kv, keys_t):
    kv[:WINDOW, :] = jnp.zeros((WINDOW, 2 * HEAD), kv.dtype)
    keys_t[:, :WINDOW] = jnp.zeros((HEAD, WINDOW), keys_t.dtype)
    place_own(own_ref, own_t_ref, kv, keys_t)
    sums[...] = jnp.zeros_like(sums)
    last = counts[order.shape[0]]
    attend(0, last, order, counts, qd_ref, kv, keys_t, dq_ref, sums, lambda i: None)


def far_kernel(
    order, counts, qd_ref, halo_ref, dq_near_ref, room_ref, kv_in, keys_t_in, sums_in,
    dq_ref, sums_ref, spill_ref, kv, keys_t, sums, dq_slabs, dq_sems,
):
    del room_ref, kv_in, keys_t_in, sums_in
    blocks = order.shape[0]
    steps = counts[blocks]

    def dq_copy(slabs, i):
        return pltpu.make_async_copy(slabs.at[i], dq_ref.at[i], dq_sems.at[i])

    def pass_on(m, carry):
        dq_copy(dq_near_ref, order[m]).start()
        return carry

    lax.fori_loop(0, steps * TOGETHER, pass_on, 0)

    @pl.when(counts[blocks + 1] < WB)
    def fill():
        for j in range(WB):
            rows = slice(j * BLOCK, (j + 1) * BLOCK)
            kv[rows, :] = halo_ref[j]
            keys_t[:, rows] = halo_ref[j, :, :HEAD].T

    attend(
        steps, blocks // TOGETHER, order, counts, qd_ref, kv, keys_t, dq_slabs, sums,
        lambda i: dq_copy(dq_slabs, i).start(),
    )
    for j in range(WB):
        rows = slice(j * BLOCK, (j + 1) * BLOCK)
        spill_ref[j, :, :HEAD] = (sums[rows, :HEAD] * SCALE).astype(spill_ref.dtype)
        spill_ref[j, :, HEAD:] = sums[rows, HEAD:].astype(spill_ref.dtype)
    sums_ref[...] = sums[WINDOW:, :]
    for i in range(blocks):
        dq_copy(dq_slabs, i).wait()


def attend(first_step, last_step, order, counts, qd_ref, kv, keys_t, dq_slabs, sums, ready):
    q_heads = qd_ref.shape[2] // (2 * HEAD)
    rows = q_heads * BLOCK

    def stacked(i, offset):
        return jnp.concatenate(
            [qd_ref[i, :, (offset + h) * HEAD : (offset + h + 1) * HEAD] for h in range(q_heads)],
            axis=0,
        )

    def fold(x, reduce):
        return reduce(x.reshape(BLOCK // 8, 8, rows), axis=0)

    def work(count, members, sizes):
        span = count * BLOCK
        windows = [
            pl.ds(pl.multiple_of((i + WB + 1 - count) * BLOCK, BLOCK), span) for i in members
        ]
        lanes = range(len(members))

        def split(x):
            return [x[b * BLOCK : (b + 1) * BLOCK] for b in range(count)]

        query = [stacked(i, 0) for i in members]
        grad = [stacked(i, q_heads) for i in members]
        scores = [split(dot(kv[windows[n], :HEAD], query[n], NT)) for n in lanes]
        key_pos = lax.broadcasted_iota(jnp.int32, (BLOCK, rows), 0)
        query_pos = lax.broadcasted_iota(jnp.int32, (BLOCK, rows), 1) % BLOCK
        causal = key_pos <= query_pos
        probs, probs_b, dprob = {}, {}, {}
        for n in lanes:
            scores[n][-1] = jnp.where(causal, scores[n][-1], -jnp.inf)
            seen = [count - b <= sizes[n] for b in range(count)]
            dprob[n] = split(dot(kv[windows[n], HEAD:], grad[n], NT))
            tops, expo, totals = [], [], []
            for x in scores[n]:
                top = jnp.max(fold(x, jnp.max), axis=0, keepdims=True)
                x = jnp.exp2((x - top) * (SCALE * LOG2E))
                tops.append(top)
                expo.append(x)
                totals.append(jnp.sum(fold(x, jnp.sum), axis=0, keepdims=True))
            shown = [jnp.where(y, x, -jnp.inf) for x, y in zip(tops, seen)]
            top = functools.reduce(jnp.maximum, shown)
            parts = [jnp.exp2((x - top) * (SCALE * LOG2E)) for x in shown]
            total = functools.reduce(jnp.add, [x * y for x, y in zip(totals, parts)])
            inverse = 1.0 / total
            probs[n] = [x * (y * inverse) for x, y in zip(expo, parts)]
            probs_b[n] = [x.astype(jnp.bfloat16) for x in probs[n]]
        dscore = {}
        for n in lanes:
            sums[windows[n], HEAD:] += dot(jnp.concatenate(probs_b[n], axis=0), grad[n], NN)
            delta = functools.reduce(
                jnp.add,
                [
                    fold(x.astype(jnp.float32) * y, jnp.sum)
                    for x, y in zip(probs_b[n], dprob[n])
                ],
            )
            delta = jnp.sum(delta, axis=0, keepdims=True)
            dscore[n] = jnp.concatenate(
                [
                    (x * (y - delta)).astype(jnp.bfloat16)
                    for x, y in zip(probs[n], dprob[n])
                ],
                axis=0,
            )
        for n, i in enumerate(members):
            sums[windows[n], :HEAD] += dot(dscore[n], query[n], NN)
            query_grad = dot(keys_t[:, windows[n]], dscore[n], NN) * SCALE
            for h in range(q_heads):
                dq_slabs[i, :, h * HEAD : (h + 1) * HEAD] = query_grad[
                    :, h * BLOCK : (h + 1) * BLOCK
                ].T.astype(dq_slabs.dtype)
            ready(i)

    def one_step(step, carry):
        members = [order[step * TOGETHER + n] for n in range(TOGETHER)]
        sizes = [counts[step * TOGETHER + n] for n in range(TOGETHER)]
        widest = functools.reduce(jnp.maximum, sizes)
        for count in range(1, WB + 2):
            pl.when(widest == count)(functools.partial(work, count, members, sizes))
        return carry

    lax.fori_loop(first_step, last_step, one_step, 0)


def attend_near(order, counts, qd, own, own_t):
    total = WINDOW + own_t.shape[1]
    smem = pl.BlockSpec(memory_space=pltpu.SMEM)
    vmem = pl.BlockSpec(memory_space=pltpu.VMEM)
    return pl.pallas_call(
        near_kernel,
        in_specs=[smem] * 2 + [vmem] * 3,
        out_specs=[vmem] * 4,
        out_shape=[
            jax.ShapeDtypeStruct((*qd.shape[:2], qd.shape[2] // 2), qd.dtype),
            jax.ShapeDtypeStruct((total, 2 * HEAD), jnp.float32),
            jax.ShapeDtypeStruct((total, 2 * HEAD), own.dtype),
            jax.ShapeDtypeStruct((HEAD, total), own.dtype),
        ],
        compiler_params=pltpu.CompilerParams(vmem_limit_bytes=LARGE),
    )(order, counts, qd, own, own_t)


def attend_far(order, counts, qd, halo, dq, room, kv, keys_t, sums):
    smem = pl.BlockSpec(memory_space=pltpu.SMEM)
    vmem = pl.BlockSpec(memory_space=pltpu.VMEM)
    hbm = pl.BlockSpec(memory_space=pl.ANY)
    own_sums = jax.ShapeDtypeStruct((sums.shape[0] - WINDOW, sums.shape[1]), sums.dtype)
    shapes = [jax.ShapeDtypeStruct(x.shape, x.dtype) for x in (dq, halo, kv, keys_t, sums)]
    return pl.pallas_call(
        far_kernel,
        in_specs=[smem] * 2 + [vmem] * 3 + [hbm] + [vmem] * 3,
        out_specs=[hbm] + [vmem] * 5,
        out_shape=[shapes[0], own_sums, *shapes[1:]],
        input_output_aliases={5: 0, 3: 2, 6: 3, 7: 4, 8: 5},
        scratch_shapes=[
            pltpu.VMEM(dq.shape, dq.dtype),
            pltpu.SemaphoreType.DMA(dq.shape[:1]),
        ],
        compiler_params=pltpu.CompilerParams(vmem_limit_bytes=LARGE),
    )(order, counts, qd, halo, dq, room, kv, keys_t, sums)[:3]


def add_kernel(sums_ref, spill_ref, out_ref, slabs, sems):
    copies = []
    for j in range(out_ref.shape[0]):
        late = slice(j * BLOCK, (j + 1) * BLOCK)
        for half, scale in ((slice(0, HEAD), SCALE), (slice(HEAD, 2 * HEAD), 1.0)):
            own = sums_ref[late, half] * scale
            slabs[j, :, half] = (own + spill_ref[j, :, half].astype(jnp.float32)).astype(
                slabs.dtype
            )
        copies.append(pltpu.make_async_copy(slabs.at[j], out_ref.at[j], sems.at[j]))
        copies[j].start()
    for copy in copies:
        copy.wait()


def add_spill(sums, spill):
    return pl.pallas_call(
        add_kernel,
        in_specs=[pl.BlockSpec(memory_space=pltpu.VMEM)] * 2,
        out_specs=pl.BlockSpec(memory_space=pl.ANY),
        out_shape=jax.ShapeDtypeStruct(spill.shape, spill.dtype),
        scratch_shapes=[
            pltpu.VMEM(spill.shape, spill.dtype),
            pltpu.SemaphoreType.DMA((spill.shape[0],)),
        ],
        compiler_params=pltpu.CompilerParams(vmem_limit_bytes=SMALL),
    )(sums, spill)


def per_device(queries, keys, values, upstream, doc_ids, band):
    tokens = queries.shape[0]
    parts = WINDOW // tokens
    cores = lax.axis_size("heads")
    spans = lax.axis_size("blk")
    step = parts // cores
    axes = ("blk", "heads")
    groups = [
        [first * parts + member for member in range(parts)] for first in range(spans // step)
    ]

    def exchange(value):
        return lax.all_to_all(
            value, axes, split_axis=0, concat_axis=0, axis_index_groups=groups, tiled=True
        )

    kv_packed = pack(keys, values, parts)
    kv = exchange(kv_packed)
    halo = lax.ppermute(kv, "blk", [(s, s + step) for s in range(spans - step)])
    qd = exchange(pack(queries, upstream, parts))
    chunk_index = (lax.axis_index("blk") // step).astype(jnp.int32).reshape(1)
    order, counts, own_t = prepare(chunk_index, doc_ids, band, kv)
    dq, sums, rows, rows_t = attend_near(order, counts, qd, kv, own_t)
    dq, sums, spill = attend_far(order, counts, qd, halo, dq, kv_packed, rows, rows_t, sums)
    spill = lax.ppermute(spill, "blk", [(s + step, s) for s in range(spans - step)])
    query_out = exchange(dq)
    dkv = exchange(add_spill(sums, spill))

    return (*unpack(query_out, 1), *unpack(dkv, 2))


def solution(mesh):
    sharded = P(("groups", "blk", "heads"), None)
    return jax.shard_map(
        per_device,
        mesh=mesh,
        in_specs=(sharded,) * 4 + (P("groups"),) * 2,
        out_specs=(sharded,) * 3,
        check_vma=False,
    )
```
